256 devices in a mesh: dp: 16 (over z, y_lo), head: 4 (over y_hi, core), mp: 4 (over x).
Axes of the slice: x: 4, y: 4 (y_hi: 2, y_lo: 2; y = y_hi * 2 + y_lo), z: 8, core: 2. Of those that a mesh axis runs over, the one named last changes fastest.
Arguments:
- teacher_states: bfloat16 [6144, 8192], P('dp', ('head', 'mp')), may hold values from -8 to 8
- teacher_wq: bfloat16 [8192, 8192], P('dp', ('head', 'mp')), may hold values from -0.0625 to 0.0625
- teacher_wk: bfloat16 [8192, 1024], P('dp', ('head', 'mp')), may hold values from -0.0625 to 0.0625
- teacher_wv: bfloat16 [8192, 1024], P('dp', ('head', 'mp')), may hold values from -0.0625 to 0.0625
- student_states: bfloat16 [6144, 3584], P('dp'), may hold values from -9 to 9
- student_wq: bfloat16 [3584, 3584], P(None, ('head', 'mp')), may hold values from -0.09375 to 0.09375
- student_wk: bfloat16 [3584, 512], P(None, ('head', 'mp')), may hold values from -0.09375 to 0.09375
- student_wv: bfloat16 [3584, 512], P(None, ('head', 'mp')), may hold values from -0.09375 to 0.09375
- lengths: int32 [16], P('dp'), may hold values from 192 to 384, as said below
Outputs:
- grad_wq: float32 [3584, 3584], P('dp', ('head', 'mp'))
- grad_wk: float32 [3584, 512], P('dp', ('head', 'mp'))
- grad_wv: float32 [3584, 512], P('dp', ('head', 'mp'))
- grad_states: float32 [6144, 3584], P(('dp', 'head', 'mp'))
- loss: float32 [16], P('dp')
The draws below stay inside these ranges and needn't reach their ends.
Inputs may be any that keep to these rules, and one draw needn't show every extreme that they name: `lengths`: each sequence has between 192 and 384 valid positions; some sequence has exactly 384.
All inputs are finite; a program needn't handle non-finite values.
Results may differ from the reference program's by a relative error of at most 0.022.
Values may be sent and summed in bfloat16 or wider, within the bound.
No kernel may reach another device: no remote copies, remote signals or barrier semaphores. Data moves between devices by JAX's collectives and lax.ppermute only.
A program may use at most 128 MiB of HBM per device.

```python
import math
import jax
import jax.numpy as jnp
from jax import lax

DT = 8192
KVT = 1024
DS = 3584
KVS = 512
R = 64
L = 384
SEQS = 16
TOKENS = 6144
N_HEAD = 4
N_MP = 4


def draw_teacher_states(key, part):
    key = jax.random.fold_in(key, 11)
    first = jax.random.fold_in(key, 0)
    values = jax.random.truncated_normal(first, -6.0, 6.0, (TOKENS, DT), jnp.float32) * 0.5
    return values.astype(jnp.bfloat16)


def draw_student_states(key, part):
    key = jax.random.fold_in(key, 23)
    first = jax.random.fold_in(key, 0)
    values = jax.random.truncated_normal(first, -6.0, 6.0, (TOKENS, DS), jnp.float32) * 0.6
    return values.astype(jnp.bfloat16)


def draw_lengths(key, part):
    key = jax.random.fold_in(key, 5)
    first, second = jax.random.split(key)
    values = jax.random.randint(first, (SEQS,), L // 2, L + 1)
    chosen = jax.random.randint(second, (), 0, SEQS)
    return jnp.where(jnp.arange(SEQS) == chosen, L, values).astype(jnp.int32)


def block_scale(rng, dims, pieces, low, top_value):
    gain, own = 1.0, jax.random.fold_in(rng, 6)
    for dim, parts in pieces:
        steps = jnp.exp(jax.random.uniform(jax.random.fold_in(own, dim), (parts,), jnp.float32, low / len(pieces), top_value / len(pieces)))
        gain = gain * jnp.repeat(steps, dims[dim] // parts).reshape([-1 if axis == dim else 1 for axis in range(len(dims))])
    return gain


def gaussian(key, shape, scale, reach, pieces=(), held_as=jnp.bfloat16):
    loudness = block_scale(key, shape, pieces, -0.22, 0.18) if pieces else 1.0
    values = jax.random.normal(key, shape, jnp.float32) * scale * loudness
    return jnp.minimum(jnp.maximum(values, -reach), reach).astype(held_as)


def setup_inputs(seed: int = 0) -> dict:
    arg_keys = jax.random.split(jax.random.key(seed), 10)
    return {
        "teacher_states": draw_teacher_states(jax.random.fold_in(arg_keys[9], 71), 0),
        "teacher_wq": gaussian(arg_keys[1], (DT, DT), DT ** -0.5, 0.0625, ((0, 16), (1, 16))),
        "teacher_wk": gaussian(arg_keys[2], (DT, KVT), DT ** -0.5, 0.0625, ((0, 16), (1, 16))),
        "teacher_wv": gaussian(arg_keys[3], (DT, KVT), DT ** -0.5, 0.0625, ((0, 16), (1, 16))),
        "student_states": draw_student_states(jax.random.fold_in(arg_keys[9], 71), 0),
        "student_wq": gaussian(arg_keys[5], (DS, DS), DS ** -0.5, 0.09375, ((1, 16),)),
        "student_wk": gaussian(arg_keys[6], (DS, KVS), DS ** -0.5, 0.09375, ((1, 16),)),
        "student_wv": gaussian(arg_keys[7], (DS, KVS), DS ** -0.5, 0.09375, ((1, 16),)),
        "lengths": draw_lengths(jax.random.fold_in(arg_keys[9], 71), 0),
    }


LOSS_SCALE = 16.0
MASK_VALUE = -1000000000.0

def relation_grad(teacher_cols, student_cols, head_count, valid_rows):
    length_rows = teacher_cols.shape[0]
    teacher_head_width = teacher_cols.shape[1] // head_count
    student_head_width = student_cols.shape[1] // head_count
    teacher_head_count = teacher_cols.reshape(length_rows, head_count, teacher_head_width).astype(jnp.float32)
    student_head_count = student_cols.reshape(length_rows, head_count, student_head_width).astype(jnp.float32)
    teacher_relation_scores = jnp.einsum('fve,qve->vfq', teacher_head_count, teacher_head_count) / math.sqrt(teacher_head_width)
    student_relation_scores = jnp.einsum('fve,qve->vfq', student_head_count, student_head_count) / math.sqrt(student_head_width)
    key_mask = valid_rows[None, None, :]
    teacher_relation_scores = jnp.where(key_mask, teacher_relation_scores, MASK_VALUE)
    student_relation_scores = jnp.where(key_mask, student_relation_scores, MASK_VALUE)
    teacher_log = teacher_relation_scores - jax.nn.logsumexp(teacher_relation_scores, axis=-1, keepdims=True)
    student_log = student_relation_scores - jax.nn.logsumexp(student_relation_scores, axis=-1, keepdims=True)
    teacher_prob = jnp.exp(teacher_log)
    student_prob = jnp.exp(student_log)
    row_kl = lax.optimization_barrier(jnp.sum(teacher_prob * (teacher_log - student_log), axis=-1))
    kl_total = jnp.sum(jnp.where(valid_rows[None, :], row_kl, 0.0))
    score_gradient = jnp.where(valid_rows[None, :, None], LOSS_SCALE * (student_prob - teacher_prob), 0.0)
    score_gradient = score_gradient.astype(jnp.bfloat16).astype(jnp.float32)
    forward_pass = jnp.einsum('zwn,nzt->wzt', score_gradient, student_head_count)
    backward_pass = jnp.einsum('nur,unz->rnz', score_gradient, student_head_count)
    block_grad = (forward_pass + backward_pass) / math.sqrt(student_head_width)
    return (kl_total, block_grad.reshape(length_rows, head_count * student_head_width))

def state_gradient(column_grads, weights):
    owners = N_HEAD * N_MP
    total = jnp.zeros((L, DS), jnp.float32)
    for owner_index in range(owners):
        term = jnp.zeros((L, DS), jnp.float32)
        for column_grad, weight in zip(column_grads, weights):
            width = weight.shape[1] // owners
            first = owner_index * width
            term = term + jnp.dot(column_grad[:, first:first + width], weight[:, first:first + width].T, preferred_element_type=jnp.float32)
        rounded = lax.optimization_barrier(term.astype(jnp.bfloat16))
        total = total + rounded.astype(jnp.float32)
    return total

def reference(teacher_states, teacher_wq, teacher_wk, teacher_wv, student_states, student_wq, student_wk, student_wv, lengths):
    positions = jnp.arange(L, dtype=jnp.int32)
    teacher_seq = teacher_states.reshape(SEQS, L, DT)
    student_seq = student_states.reshape(SEQS, L, DS)

    def one_sequence(running, inputs):
        teacher_rows, student_rows, length = inputs
        valid_rows = positions < length.astype(jnp.int32)
        teacher_q = jnp.dot(teacher_rows, teacher_wq, preferred_element_type=jnp.float32).astype(jnp.bfloat16)
        teacher_k = jnp.dot(teacher_rows, teacher_wk, preferred_element_type=jnp.float32).astype(jnp.bfloat16)
        teacher_v = jnp.dot(teacher_rows, teacher_wv, preferred_element_type=jnp.float32).astype(jnp.bfloat16)
        student_q = jnp.dot(student_rows, student_wq, preferred_element_type=jnp.float32).astype(jnp.bfloat16)
        student_k = jnp.dot(student_rows, student_wk, preferred_element_type=jnp.float32).astype(jnp.bfloat16)
        student_v = jnp.dot(student_rows, student_wv, preferred_element_type=jnp.float32).astype(jnp.bfloat16)
        query_kl, query_grad = relation_grad(teacher_q, student_q, R, valid_rows)
        key_kl, key_grad = relation_grad(teacher_k, student_k, R, valid_rows)
        value_kl, value_grad = relation_grad(teacher_v, student_v, R, valid_rows)
        query_grad = query_grad.astype(jnp.bfloat16)
        key_grad = key_grad.astype(jnp.bfloat16)
        value_grad = value_grad.astype(jnp.bfloat16)
        state_grad = state_gradient((query_grad, key_grad, value_grad), (student_wq, student_wk, student_wv))
        updated = (running[0] + jnp.dot(student_rows.T, query_grad, preferred_element_type=jnp.float32), running[1] + jnp.dot(student_rows.T, key_grad, preferred_element_type=jnp.float32), running[2] + jnp.dot(student_rows.T, value_grad, preferred_element_type=jnp.float32))
        seq_loss = (query_kl + key_kl + value_kl) / (3.0 * R * length.astype(jnp.float32))
        return (updated, (state_grad, seq_loss))
    start_sums = (jnp.zeros((DS, DS), jnp.float32), jnp.zeros((DS, KVS), jnp.float32), jnp.zeros((DS, KVS), jnp.float32))
    weight_sums, outputs = lax.scan(one_sequence, start_sums, (teacher_seq, student_seq, lengths))
    state_grads, losses = outputs
    return (weight_sums[0], weight_sums[1], weight_sums[2], state_grads.reshape(TOKENS, DS), losses)
```

```python
import math

import jax
import jax.numpy as jnp
from jax import lax
from jax.sharding import PartitionSpec as P

R = 64

LOSS_SCALE = 16.0
MASK_VALUE = -1000000000.0

BF = jnp.bfloat16
F32 = jnp.float32


def shift_z(a, step):
    return lax.ppermute(a, "dp", [(d, (d + 2 * step) % 16) for d in range(16)])


def swap_dp(a, bits):
    return lax.ppermute(a, "dp", [(d, d ^ bits) for d in range(16)])


def swap_head(a, bits):
    return lax.ppermute(a, "head", [(h, h ^ bits) for h in range(4)])


def shift_x(a, step):
    return lax.ppermute(a, "mp", [(m, (m + step) % 4) for m in range(4)])


def swap_x(a, bits):
    return lax.ppermute(a, "mp", [(m, m ^ bits) for m in range(4)])


def dot(a, b):
    return jnp.dot(a, b, preferred_element_type=F32)


def relation_grad(teacher_cols, student_cols, head_count, valid_rows):
    length_rows = teacher_cols.shape[0]
    teacher_head_width = teacher_cols.shape[1] // head_count
    student_head_width = student_cols.shape[1] // head_count
    teacher = teacher_cols.reshape(length_rows, head_count, teacher_head_width)
    student = student_cols.reshape(length_rows, head_count, student_head_width)
    teacher_scores = jnp.einsum("fve,qve->vfq", teacher, teacher, preferred_element_type=F32)
    teacher_scores = teacher_scores / math.sqrt(teacher_head_width)
    student_scores = jnp.einsum("fve,qve->vfq", student, student, preferred_element_type=F32)
    student_scores = student_scores / math.sqrt(student_head_width)
    key_mask = valid_rows[None, None, :]
    teacher_scores = jnp.where(key_mask, teacher_scores, MASK_VALUE)
    student_scores = jnp.where(key_mask, student_scores, MASK_VALUE)
    teacher_log = teacher_scores - jax.nn.logsumexp(teacher_scores, axis=-1, keepdims=True)
    student_log = student_scores - jax.nn.logsumexp(student_scores, axis=-1, keepdims=True)
    teacher_prob = jnp.exp(teacher_log)
    student_prob = jnp.exp(student_log)
    row_kl = jnp.sum(teacher_prob * (teacher_log - student_log), axis=-1)
    kl_total = jnp.sum(jnp.where(valid_rows[None, :], row_kl, 0.0))
    score_gradient = jnp.where(
        valid_rows[None, :, None], LOSS_SCALE * (student_prob - teacher_prob), 0.0
    ).astype(BF)
    forward_pass = jnp.einsum("zwn,nzt->wzt", score_gradient, student, preferred_element_type=F32)
    backward_pass = jnp.einsum("nur,unz->rnz", score_gradient, student, preferred_element_type=F32)
    block_grad = (forward_pass + backward_pass) / math.sqrt(student_head_width)
    return (kl_total, block_grad.reshape(length_rows, head_count * student_head_width).astype(BF))


def gather_states(block, head, x):
    width = block.shape[1]
    pair = jnp.concatenate([block, swap_head(block, 2)], axis=1)
    left = shift_x(pair, 1)
    right = shift_x(pair, -1)
    half = block.shape[0] // 2
    far = jnp.concatenate([shift_x(left[:half], 1), shift_x(right[half:], -1)], axis=0)
    mine = jnp.concatenate([pair, left, right, far], axis=1)
    other = swap_head(mine, 1)
    whole = jnp.zeros((block.shape[0], width * 16), BF)
    for core_bit, part in ((0, mine), (1, other)):
        for slot, offset in enumerate((0, -1, 1, 2)):
            for yh_bit in (0, 1):
                owner = (head ^ (2 * yh_bit + core_bit)) * 4 + (x + offset + 4) % 4
                first = (slot * 2 + yh_bit) * width
                whole = lax.dynamic_update_slice(
                    whole, part[:, first : first + width], (0, owner * width)
                )
    return whole


def ring(start):
    half = start.shape[0] // 2
    steps = []
    ahead = back = start
    for distance in (1, 2, 3):
        ahead = shift_z(ahead, 1)
        back = shift_z(back, -1)
        steps.append((distance, ahead, back))
    far = (shift_z(ahead[:half], 1), shift_z(back[half:], -1))
    return steps, far


def per_device(
    teacher_states,
    teacher_wq,
    teacher_wk,
    teacher_wv,
    student_states,
    student_wq,
    student_wk,
    student_wv,
    lengths,
):
    d = lax.axis_index("dp")
    head = lax.axis_index("head")
    x = lax.axis_index("mp")
    z, yl = d // 2, d % 2
    rows = student_states.shape[0]
    depth = teacher_wq.shape[0]
    q_width = teacher_wq.shape[1] // 4

    part_z = jnp.concatenate([teacher_wk, teacher_wv, teacher_wq[:, :q_width]], axis=1)
    part_y = teacher_wq[:, q_width:]
    other_y = swap_dp(part_y, 1)
    pair_y = jnp.where(
        yl == 0,
        jnp.concatenate([part_y, other_y], axis=0),
        jnp.concatenate([other_y, part_y], axis=0),
    )
    steps_z, far_z = ring(part_z)
    across = [swap_dp(part_z, 1)]
    for _, ahead, back in steps_z:
        across.append(swap_dp(jnp.concatenate([ahead, back], axis=0), 1))
    whole_far = jnp.concatenate(far_z, axis=0)
    across_far = swap_dp(whole_far, 1)
    steps_y, far_y = ring(pair_y)

    states = gather_states(teacher_states, head, x)

    def state_cols(offset, first, size):
        block = (z + offset + 8) % 8
        return lax.dynamic_slice(states, (0, block * 2 * depth + first), (rows, size))

    mine, other = yl * depth, (1 - yl) * depth
    acc_z = dot(state_cols(0, mine, depth), part_z) + dot(state_cols(0, other, depth), across[0])
    for (distance, ahead, back), crossed in zip(steps_z, across[1:]):
        acc_z = acc_z + dot(state_cols(-distance, mine, depth), ahead)
        acc_z = acc_z + dot(state_cols(distance, mine, depth), back)
        acc_z = acc_z + dot(state_cols(-distance, other, depth), crossed[:depth])
        acc_z = acc_z + dot(state_cols(distance, other, depth), crossed[depth:])
    acc_z = acc_z + dot(state_cols(4, mine, depth), whole_far)
    acc_z = acc_z + dot(state_cols(4, other, depth), across_far)
    acc_z = acc_z.astype(BF)

    acc_y = dot(state_cols(0, 0, 2 * depth), pair_y)
    for distance, ahead, back in steps_y:
        acc_y = acc_y + dot(state_cols(-distance, 0, 2 * depth), ahead)
        acc_y = acc_y + dot(state_cols(distance, 0, 2 * depth), back)
    acc_y = acc_y + dot(state_cols(4, 0, depth), far_y[0])
    acc_y = acc_y + dot(state_cols(4, depth, depth), far_y[1])
    acc_y = acc_y.astype(BF)

    kv_width = teacher_wk.shape[1]
    student_w = jnp.concatenate([student_wq, student_wk, student_wv], axis=1)
    student = dot(student_states, student_w).astype(BF)
    sq = student_wq.shape[1]
    sk = student_wk.shape[1]
    length = lengths[0]
    valid_rows = jnp.arange(rows, dtype=jnp.int32) < length
    head0 = sq // 4
    key_kl, key_grad = relation_grad(
        acc_z[:, :kv_width], student[:, sq : sq + sk], 4, valid_rows
    )
    value_kl, value_grad = relation_grad(
        acc_z[:, kv_width : 2 * kv_width], student[:, sq + sk :], 4, valid_rows
    )
    first_kl, first_grad = relation_grad(
        acc_z[:, 2 * kv_width :], student[:, :head0], 1, valid_rows
    )
    rest_kl, rest_grad = relation_grad(acc_y, student[:, head0:sq], 3, valid_rows)
    grads = jnp.concatenate([first_grad, rest_grad, key_grad, value_grad], axis=1)

    unit = student_states.shape[1] // 16
    columns = []
    for e in range(4):
        blocks = []
        for r in range(4):
            owner = ((d ^ e) + 4 * r) % 16
            blocks.append(lax.dynamic_slice(student_states, (0, owner * unit), (rows, unit)))
        columns.append(jnp.concatenate(blocks, axis=1))

    def weight_term(e):
        return lax.dot_general(
            grads, columns[e], (((0,), (0,)), ((), ())), preferred_element_type=F32
        )

    received = [swap_dp(weight_term(e).astype(BF), e) for e in (3, 2, 1)]
    square = weight_term(0)
    for part in received:
        square = square + part.astype(F32)
    chunks = [square[:, r * unit : (r + 1) * unit] for r in range(4)]
    weight_grad = chunks[0]
    for r in (1, 2, 3):
        sent = lax.ppermute(
            chunks[r].astype(BF), "dp", [(i, (i + 4 * r) % 16) for i in range(16)]
        )
        weight_grad = weight_grad + sent.astype(F32)
    weight_grad = weight_grad.T

    piece = rows // 16
    order = []
    for core_bit in (0, 1):
        for x_step in range(4):
            for yh_bit in (0, 1):
                owner = (head ^ (2 * yh_bit + core_bit)) * 4 + (x + x_step) % 4
                order.append(
                    lax.dynamic_slice(grads, (owner * piece, 0), (piece, grads.shape[1]))
                )
    half = rows // 2
    ordered = jnp.concatenate(order, axis=0)

    def state_term(part):
        return lax.dot_general(
            part, student_w, (((1,), (1,)), ((), ())), preferred_element_type=F32
        ).astype(BF)

    from_core = swap_head(state_term(ordered[half:]), 1)
    summed = (state_term(ordered[:half]).astype(F32) + from_core.astype(F32)).astype(BF)
    slab = half // 4
    total = summed[:slab].astype(F32)
    for step in (2, 1, 3):
        total = total + shift_x(summed[step * slab : (step + 1) * slab], step).astype(F32)
    grad_states = total[:piece] + swap_head(total[piece:].astype(BF), 2).astype(F32)

    loss = (key_kl + value_kl + first_kl + rest_kl) / (3.0 * R * length.astype(F32))
    loss = jnp.full((8, 128), loss, F32)
    loss = loss + swap_head(loss, 1)
    loss = loss + swap_x(loss, 1)
    loss = loss + swap_x(loss, 2)
    loss = loss + swap_head(loss, 2)
    seq_loss = loss[0, :1]

    return (
        weight_grad[:, :sq],
        weight_grad[:, sq : sq + sk],
        weight_grad[:, sq + sk :],
        grad_states,
        seq_loss,
    )


def solution(mesh):
    in_specs = (
        P("dp", ("head", "mp")),
        P("dp", ("head", "mp")),
        P("dp", ("head", "mp")),
        P("dp", ("head", "mp")),
        P("dp", None),
        P(None, ("head", "mp")),
        P(None, ("head", "mp")),
        P(None, ("head", "mp")),
        P("dp"),
    )
    out_specs = (
        P("dp", ("head", "mp")),
        P("dp", ("head", "mp")),
        P("dp", ("head", "mp")),
        P(("dp", "head", "mp"), None),
        P("dp"),
    )
    return jax.shard_map(
        per_device, mesh=mesh, in_specs=in_specs, out_specs=out_specs, check_vma=False
    )
```

```python
import math

import jax
import jax.numpy as jnp
from jax import lax
from jax.experimental import pallas as pl
from jax.experimental.pallas import tpu as pltpu
from jax.sharding import PartitionSpec as P

R = 64

LOSS_SCALE = 16.0
MASK_VALUE = -1000000000.0

BF = jnp.bfloat16
F32 = jnp.float32


def shift_z(a, step):
    return lax.ppermute(a, "dp", [(d, (d + 2 * step) % 16) for d in range(16)])


def swap_dp(a, bits):
    return lax.ppermute(a, "dp", [(d, d ^ bits) for d in range(16)])


def swap_head(a, bits):
    return lax.ppermute(a, "head", [(h, h ^ bits) for h in range(4)])


def shift_x(a, step):
    return lax.ppermute(a, "mp", [(m, (m + step) % 4) for m in range(4)])


def dot(a, b):
    return jnp.dot(a, b, preferred_element_type=F32)


def relation_grad(teacher_cols, student_cols, head_count, valid_rows):
    length_rows = teacher_cols.shape[0]
    teacher_head_width = teacher_cols.shape[1] // head_count
    student_head_width = student_cols.shape[1] // head_count
    teacher = teacher_cols.reshape(length_rows, head_count, teacher_head_width)
    student = student_cols.reshape(length_rows, head_count, student_head_width)
    teacher_scores = jnp.einsum("fve,qve->vfq", teacher, teacher, preferred_element_type=F32)
    teacher_scores = teacher_scores / math.sqrt(teacher_head_width)
    student_scores = jnp.einsum("fve,qve->vfq", student, student, preferred_element_type=F32)
    student_scores = student_scores / math.sqrt(student_head_width)
    key_mask = valid_rows[None, None, :]
    teacher_scores = jnp.where(key_mask, teacher_scores, MASK_VALUE)
    student_scores = jnp.where(key_mask, student_scores, MASK_VALUE)
    teacher_log = teacher_scores - jax.nn.logsumexp(teacher_scores, axis=-1, keepdims=True)
    student_log = student_scores - jax.nn.logsumexp(student_scores, axis=-1, keepdims=True)
    teacher_prob = jnp.exp(teacher_log)
    student_prob = jnp.exp(student_log)
    row_kl = jnp.sum(teacher_prob * (teacher_log - student_log), axis=-1)
    kl_total = jnp.sum(jnp.where(valid_rows[None, :], row_kl, 0.0))
    score_gradient = jnp.where(
        valid_rows[None, :, None], LOSS_SCALE * (student_prob - teacher_prob), 0.0
    ).astype(BF)
    forward_pass = jnp.einsum("zwn,nzt->wzt", score_gradient, student, preferred_element_type=F32)
    backward_pass = jnp.einsum("nur,unz->rnz", score_gradient, student, preferred_element_type=F32)
    block_grad = (forward_pass + backward_pass) / math.sqrt(student_head_width)
    return (kl_total, block_grad.reshape(length_rows, head_count * student_head_width).astype(BF))


OFFSETS = (0, -1, 1, -2, 2, -3, 3, 4)


def project_kernel(
    coord, pair, left, right, far, near_core, far_core, pair_y, z0, z1a, z1b, m1a, m1b, m2a, m2b,
    m3a, m3b, f0, f1, c1, c2, c3, c4, out, a_v, w_v, acc, sems,
):
    z, yl, head, x = coord[0], coord[1], coord[2], coord[3]
    depth, y_cols, z_cols = w_v.shape[2], pair_y.shape[1], z0.shape[1]
    copies = []

    def copy(src, dst):
        made = pltpu.make_async_copy(src, dst, sems.at[len(copies)])
        made.start()
        copies.append(made)
        return made

    a_copies = []
    for core_bit, groups in (
        (0, ((pair, 0, 0), (left, 0, -1), (right, 0, 1), (far, 0, 2))),
        (1, ((near_core, 0, 0), (near_core, 2, -1), (near_core, 4, 1), (far_core, 0, 2))),
    ):
        for ref, first, offset in groups:
            for yh_bit in (0, 1):
                owner = (head ^ (2 * yh_bit + core_bit)) * 4 + ((x + offset + 4) & 3)
                src = ref.at[:, pl.ds((first + yh_bit) * depth, depth)]
                a_copies.append(copy(src, a_v.at[owner]))

    y_sources = (
        ((pair_y, 0), (pair_y, depth)), ((m1a, 0), (m1a, depth)), ((m1b, 0), (m1b, depth)),
        ((m2a, 0), (m2a, depth)), ((m2b, 0), (m2b, depth)), ((m3a, 0), (m3a, depth)),
        ((m3b, 0), (m3b, depth)), ((f0, 0), (f1, 0)),
    )
    z_sources = (
        ((z0, 0, 0), (c1, 0)), ((z1a, 0, 0), (c1, 1)), ((z1b, 0, 0), (c1, 2)),
        ((m1a, 0, y_cols), (c2, 0)), ((m1b, 0, y_cols), (c2, 1)),
        ((m2a, 0, y_cols), (c3, 0)), ((m2b, 0, y_cols), (c3, 1)), ((m3a, 0, y_cols), (c4, 0)),
    )
    w_copies = []
    for slot in range(8):
        mine = []
        for side, (ref, first) in enumerate(y_sources[slot]):
            src = ref.at[pl.ds(first, depth), pl.ds(0, y_cols)]
            mine.append(copy(src, w_v.at[slot, side, :, pl.ds(0, y_cols)]))
        (own, _, col), (crossed, place) = z_sources[slot]
        for fold in (0, 1):
            cols = pl.ds(y_cols + fold * z_cols, z_cols)
            src = own.at[pl.ds(fold * depth, depth), pl.ds(col, z_cols)]
            mine.append(copy(src, w_v.at[slot, yl, :, cols]))
            src = crossed.at[pl.ds((2 * place + fold) * depth, depth), :]
            mine.append(copy(src, w_v.at[slot, 1 - yl, :, cols]))
        w_copies.append(mine)

    for made in a_copies:
        made.wait()
    for slot, offset in enumerate(OFFSETS):
        for made in w_copies[slot]:
            made.wait()
        owner = (z + offset + 8) & 7
        term = dot(a_v[2 * owner], w_v[slot, 0]) + dot(a_v[2 * owner + 1], w_v[slot, 1])
        if slot == 0:
            acc[...] = term
        elif slot < 7:
            acc[...] += term
        else:
            out[...] = (acc[...] + term).astype(out.dtype)


def project(coord, a_parts, w_parts, rows, depth, cols):
    any_spec = pl.BlockSpec(memory_space=pl.ANY)
    parts = tuple(a_parts) + tuple(w_parts)
    return pl.pallas_call(
        project_kernel,
        out_shape=jax.ShapeDtypeStruct((rows, cols), BF),
        in_specs=[pl.BlockSpec(memory_space=pltpu.SMEM)] + [any_spec] * len(parts),
        out_specs=pl.BlockSpec(memory_space=pltpu.VMEM),
        scratch_shapes=[
            pltpu.VMEM((16, rows, depth), BF),
            pltpu.VMEM((8, 2, depth, cols), BF),
            pltpu.VMEM((rows, cols), F32),
            pltpu.SemaphoreType.DMA((64,)),
        ],
        compiler_params=pltpu.CompilerParams(vmem_limit_bytes=36 * 1024 * 1024),
        cost_estimate=pl.CostEstimate(
            flops=2 * rows * 16 * depth * cols,
            bytes_accessed=2 * 16 * depth * (rows + cols),
            transcendentals=0,
        ),
        name="project",
    )(coord, *parts)


def per_device(
    teacher_states,
    teacher_wq,
    teacher_wk,
    teacher_wv,
    student_states,
    student_wq,
    student_wk,
    student_wv,
    lengths,
):
    d = lax.axis_index("dp")
    head = lax.axis_index("head")
    x = lax.axis_index("mp")
    z, yl = d // 2, d % 2
    rows = student_states.shape[0]
    depth = teacher_wq.shape[0]
    q_width = teacher_wq.shape[1] // 4

    depth = teacher_wq.shape[0]
    part_y = teacher_wq[:, q_width:]
    z0 = jnp.concatenate(
        [jnp.concatenate([teacher_wk, teacher_wv], axis=1), teacher_wq[:, :q_width]], axis=0
    )
    y_cols = part_y.shape[1]
    cat, fence = jnp.concatenate, lax.optimization_barrier

    other_y = swap_dp(part_y, 1)
    z1a, z1b = shift_z(z0, 1), shift_z(z0, -1)
    other_y, z1a, z1b, states = fence((other_y, z1a, z1b, teacher_states))
    pair_y = jnp.where(yl == 0, cat([part_y, other_y], 0), cat([other_y, part_y], 0))
    m1a = shift_z(cat([pair_y, z1a], 1), 1)
    m1b = shift_z(cat([pair_y, z1b], 1), -1)
    c1 = swap_dp(cat([z0, z1a, z1b], 0), 1)
    pair = cat([states, swap_head(states, 2)], 1)
    m1a, m1b, c1, pair = fence((m1a, m1b, c1, pair))
    m2a, m2b = shift_z(m1a, 1), shift_z(m1b, -1)
    c2 = swap_dp(cat([m1a[:, y_cols:], m1b[:, y_cols:]], 0), 1)
    left, right = shift_x(pair, 1), shift_x(pair, -1)
    m2a, m2b, c2, left, right = fence((m2a, m2b, c2, left, right))
    m3a, m3b = shift_z(m2a, 1), shift_z(m2b, -1)
    c3 = swap_dp(cat([m2a[:, y_cols:], m2b[:, y_cols:]], 0), 1)
    half = rows // 2
    far = cat([shift_x(left[:half], 1), shift_x(right[half:], -1)], 0)
    near_core = swap_head(cat([pair, left, right], 1), 1)
    m3a, m3b, c3, far, near_core = fence((m3a, m3b, c3, far, near_core))
    f0 = shift_z(m3a[:depth, :y_cols], 1)
    f1 = shift_z(m3b[depth:, :y_cols], -1)
    c4 = swap_dp(m3a[:, y_cols:], 1)
    far_core = swap_head(far, 1)

    coord = jnp.stack([z, yl, head, x]).astype(jnp.int32)
    projected = project(
        coord,
        (pair, left, right, far, near_core, far_core),
        (pair_y, z0, z1a, z1b, m1a, m1b, m2a, m2b, m3a, m3b, f0, f1, c1, c2, c3, c4),
        rows,
        depth,
        y_cols + 2 * q_width,
    )
    acc_y = projected[:, :y_cols]
    acc_z = projected[:, y_cols:]

    kv_width = teacher_wk.shape[1]
    student_w = jnp.concatenate([student_wq, student_wk, student_wv], axis=1)
    student = dot(student_states, student_w).astype(BF)
    wide_w = jnp.pad(student_w, ((0, 128), (0, 128)))
    wide_w = wide_w.at[student_w.shape[0], student_w.shape[1]].set(1.0)
    unit = student_states.shape[1] // 16
    columns = []
    for e in range(4):
        blocks = []
        for r in range(4):
            owner = ((d ^ e) + 4 * r) % 16
            blocks.append(lax.dynamic_slice(student_states, (0, owner * unit), (rows, unit)))
        columns.append(cat(blocks, 1))
    sq = student_wq.shape[1]
    sk = student_wk.shape[1]
    length = lengths[0]
    valid_rows = jnp.arange(rows, dtype=jnp.int32) < length
    head0 = sq // 4
    key_kl, key_grad = relation_grad(
        acc_z[:, :kv_width], student[:, sq : sq + sk], 4, valid_rows
    )
    value_kl, value_grad = relation_grad(
        acc_z[:, kv_width : 2 * kv_width], student[:, sq + sk :], 4, valid_rows
    )
    first_kl, first_grad = relation_grad(
        acc_z[:, 2 * kv_width :], student[:, :head0], 1, valid_rows
    )
    rest_kl, rest_grad = relation_grad(acc_y, student[:, head0:sq], 3, valid_rows)
    grads = jnp.concatenate([first_grad, rest_grad, key_grad, value_grad], axis=1)

    loss = (key_kl + value_kl + first_kl + rest_kl) / (3.0 * R * length.astype(F32))
    width = student_states.shape[1]
    with_loss = cat([grads, jnp.full((rows, 128), loss, F32).astype(BF)], 1)

    piece = rows // 16
    order = []
    for core_bit in (0, 1):
        for x_step in range(4):
            for yh_bit in (0, 1):
                owner = (head ^ (2 * yh_bit + core_bit)) * 4 + (x + x_step) % 4
                order.append(
                    lax.dynamic_slice(with_loss, (owner * piece, 0), (piece, with_loss.shape[1]))
                )
    ordered = cat(order, 0)

    def state_term(part):
        return lax.dot_general(
            part, wide_w, (((1,), (1,)), ((), ())), preferred_element_type=F32
        ).astype(BF)

    def weight_term(e, grads):
        return lax.dot_general(
            grads, columns[e], (((0,), (0,)), ((), ())), preferred_element_type=F32
        )

    term_out, grads = fence((state_term(ordered[half:]), grads))
    from_core = swap_head(term_out, 1)
    terms = [weight_term(e, grads).astype(BF) for e in (3, 1, 2)]
    *terms, ordered = fence((*terms, ordered))
    received = [swap_dp(term, e) for term, e in zip(terms, (3, 1, 2))]
    summed = (state_term(ordered[:half]).astype(F32) + from_core.astype(F32)).astype(BF)
    summed, grads = fence((summed, grads))
    slab = half // 4
    sent = [shift_x(summed[step * slab : (step + 1) * slab], step) for step in (2, 1, 3)]
    square = weight_term(0, grads)
    for part in received:
        square = square + part.astype(F32)
    chunks = [square[:, r * unit : (r + 1) * unit] for r in range(4)]
    weight_grad = chunks[0]
    for r in (2, 1, 3):
        moved = lax.ppermute(
            chunks[r].astype(BF), "dp", [(i, (i + 4 * r) % 16) for i in range(16)]
        )
        weight_grad = weight_grad + moved.astype(F32)
    weight_grad = weight_grad.T
    total = summed[:slab].astype(F32)
    for part in sent:
        total = total + part.astype(F32)
    total = total[:piece] + swap_head(total[piece:].astype(BF), 2).astype(F32)
    grad_states = total[:, :width]
    seq_loss = total[0, width : width + 1]

    return (
        weight_grad[:, :sq],
        weight_grad[:, sq : sq + sk],
        weight_grad[:, sq + sk :],
        grad_states,
        seq_loss,
    )


def solution(mesh):
    in_specs = (
        P("dp", ("head", "mp")),
        P("dp", ("head", "mp")),
        P("dp", ("head", "mp")),
        P("dp", ("head", "mp")),
        P("dp", None),
        P(None, ("head", "mp")),
        P(None, ("head", "mp")),
        P(None, ("head", "mp")),
        P("dp"),
    )
    out_specs = (
        P("dp", ("head", "mp")),
        P("dp", ("head", "mp")),
        P("dp", ("head", "mp")),
        P(("dp", "head", "mp"), None),
        P("dp"),
    )
    return jax.shard_map(
        per_device, mesh=mesh, in_specs=in_specs, out_specs=out_specs, check_vma=False
    )
```

```python
import functools
import math

import jax
import jax.numpy as jnp
import numpy as np
from jax import lax
from jax.experimental import pallas as pl
from jax.experimental.pallas import tpu as pltpu
from jax.sharding import PartitionSpec as P

R = 64

LOSS_SCALE = 16.0
MASK_VALUE = -1000000000.0

BF = jnp.bfloat16
F32 = jnp.float32


def shift_z(a, step):
    return lax.ppermute(a, "dp", [(d, (d + 2 * step) % 16) for d in range(16)])


def swap_dp(a, bits):
    return lax.ppermute(a, "dp", [(d, d ^ bits) for d in range(16)])


def swap_head(a, bits):
    return lax.ppermute(a, "head", [(h, h ^ bits) for h in range(4)])


def shift_x(a, step):
    return lax.ppermute(a, "mp", [(m, (m + step) % 4) for m in range(4)])


def dot(a, b):
    return jnp.dot(a, b, preferred_element_type=F32)


OFFSETS = (0, -1, 1, -2, 2, -3, 3, 4)


class Loader:
    def __init__(self, coord, states, a_v, w_v, sems):
        self.z, self.yl = coord[0], coord[1]
        self.states, self.a_v, self.w_v, self.sems = states, a_v, w_v, sems
        self.count = 0
        self.slots = []

    def copy(self, src, dst):
        made = pltpu.make_async_copy(src, dst, self.sems.at[self.count])
        self.count += 1
        made.start()
        return made

    def load(self, offset, y_parts, own, crossed):
        slot, w_v = len(self.slots), self.w_v
        depth, z_cols = w_v.shape[2], w_v.shape[3] // 5
        y_cols = 3 * z_cols
        owner = (self.z + offset + 8) & 7
        first = pl.multiple_of(owner * 2 * depth, 128)
        made = [self.copy(self.states.at[:, pl.ds(first, 2 * depth)], self.a_v.at[slot])]
        for side, (ref, row) in enumerate(y_parts):
            src = ref.at[pl.ds(row, depth), pl.ds(0, y_cols)]
            made.append(self.copy(src, w_v.at[slot, side, :, pl.ds(0, y_cols)]))
        for fold in (0, 1):
            cols = pl.ds(y_cols + fold * z_cols, z_cols)
            for (ref, row, col), side in ((own, self.yl), (crossed, 1 - self.yl)):
                src = ref.at[pl.ds(row + fold * depth, depth), pl.ds(col, z_cols)]
                made.append(self.copy(src, w_v.at[slot, side, :, cols]))
        self.slots.append(made)

    def term(self, slot):
        for made in self.slots[slot]:
            made.wait()
        a, w = self.a_v[slot], self.w_v[slot]
        return dot(a, w.reshape(w.shape[0] * w.shape[1], w.shape[2]))


def near_kernel(coord, states, pair_y, z0, z1a, z1b, m1a, m1b, m2a, m2b, c1, c2, acc, a_v, w_v, sems):
    depth, y_cols = w_v.shape[2], pair_y.shape[1]
    loader = Loader(coord, states, a_v, w_v, sems)
    pieces = (
        (pair_y, (z0, 0, 0), (c1, 0)),
        (m1a, (z1a, 0, 0), (c1, 2)),
        (m1b, (z1b, 0, 0), (c1, 4)),
        (m2a, (m1a, 0, y_cols), (c2, 0)),
        (m2b, (m1b, 0, y_cols), (c2, 2)),
    )
    for offset, (y_ref, own, (crossed, place)) in zip(OFFSETS, pieces):
        loader.load(
            offset, ((y_ref, 0), (y_ref, depth)), own, (crossed, place * depth, 0)
        )
    acc[...] = loader.term(0)
    for slot in range(1, 5):
        acc[...] += loader.term(slot)


def far_kernel(coord, before, states, m2a, m2b, m3a, m3b, c3, acc, a_v, w_v, sems):
    depth, y_cols = w_v.shape[2], w_v.shape[3] // 5 * 3
    loader = Loader(coord, states, a_v, w_v, sems)
    loader.load(-3, ((m3a, 0), (m3a, depth)), (m2a, 0, y_cols), (c3, 0, 0))
    loader.load(3, ((m3b, 0), (m3b, depth)), (m2b, 0, y_cols), (c3, 2 * depth, 0))
    acc[...] = before[...] + loader.term(0)
    acc[...] += loader.term(1)


BLOCK = 64


def relation_head(teacher, student, teacher_rows, student_rows, widths, length, valid_keys, sg_v):
    rows = teacher.shape[0]
    nt = (((1,), (1,)), ((), ()))
    teacher_scale, student_scale = (1.0 / math.sqrt(w) for w in widths)
    kl = jnp.zeros((1, 1), F32)
    for start in range(0, rows, BLOCK):
        part = slice(start, start + BLOCK)
        ts = lax.dot_general(teacher_rows[part], teacher, nt, preferred_element_type=F32)
        ss = lax.dot_general(student_rows[part], student, nt, preferred_element_type=F32)
        ts = jnp.where(valid_keys, ts * teacher_scale, MASK_VALUE)
        ss = jnp.where(valid_keys, ss * student_scale, MASK_VALUE)
        t_max = jnp.max(ts, axis=-1, keepdims=True)
        s_max = jnp.max(ss, axis=-1, keepdims=True)
        te = jnp.exp(ts - t_max)
        se = jnp.exp(ss - s_max)
        t_sum = jnp.sum(te, axis=-1, keepdims=True)
        s_sum = jnp.sum(se, axis=-1, keepdims=True)
        cross = jnp.sum(te * (ts - ss), axis=-1, keepdims=True) / t_sum
        row_kl = cross - (t_max + jnp.log(t_sum)) + (s_max + jnp.log(s_sum))
        row = lax.broadcasted_iota(jnp.int32, (BLOCK, 1), 0) + start
        valid = row < length
        kl = kl + jnp.sum(jnp.where(valid, row_kl, 0.0), axis=0, keepdims=True)
        t_gain = jnp.where(valid, LOSS_SCALE / t_sum, 0.0)
        s_gain = jnp.where(valid, LOSS_SCALE / s_sum, 0.0)
        sg_v[part, :] = (se * s_gain - te * t_gain).astype(BF)
    return kl


def head_grad(sg_v, student, width):
    sg = sg_v[...]
    tn = (((0,), (0,)), ((), ()))
    both = dot(sg, student) + lax.dot_general(sg, student, tn, preferred_element_type=F32)
    return both * (1.0 / math.sqrt(width))


def finish_kernel(
    widths, coord, before, student_ref, select_ref, states, m3a, f0, f1, c4,
    grads_out, ordered_out, a_v, w_v, t_v, g_v, o_v, sg_v, sems,
):
    depth, y_cols = w_v.shape[2], w_v.shape[3] // 5 * 3
    q_widths, k_widths = widths
    head, x, length = coord[2], coord[3], coord[4]
    rows = t_v.shape[0]
    loader = Loader(coord, states, a_v, w_v, sems)
    loader.load(4, ((f0, 0), (f1, 0)), (m3a, 0, y_cols), (c4, 0, 0))
    t_v[...] = (before[...] + loader.term(0)).astype(BF)
    keys = lax.broadcasted_iota(jnp.int32, (1, rows), 1)
    valid_keys = keys < length

    def q_head(i, kl):
        lanes = pl.ds(pl.multiple_of((i + i // 3) * 128, 128), 128)
        teacher, student = t_v[:, lanes], student_ref[:, lanes]
        kl = kl + relation_head(
            teacher, student, teacher, student, q_widths, length, valid_keys, sg_v
        )
        g_v[:, lanes] = head_grad(sg_v, student, q_widths[1]).astype(BF)
        return kl

    kl = lax.fori_loop(0, 4, q_head, jnp.zeros((1, 1), F32))
    lanes = pl.ds(384, 128)
    lane = lax.broadcasted_iota(jnp.int32, (rows, 128), 1)
    o_v[:, pl.ds(0, 128)] = jnp.zeros((rows, 128), F32)

    def kv_head(i, kl):
        teacher, student = t_v[:, lanes], student_ref[:, lanes]
        t_first, s_first = i * k_widths[0], i * k_widths[1]
        t_mine = (lane >= t_first) & (lane < t_first + k_widths[0])
        s_mine = (lane >= s_first) & (lane < s_first + k_widths[1])
        t_rows = jnp.where(t_mine, teacher.astype(F32), 0.0).astype(BF)
        s_rows = jnp.where(s_mine, student.astype(F32), 0.0).astype(BF)
        kl = kl + relation_head(
            teacher, student, t_rows, s_rows, k_widths, length, valid_keys, sg_v
        )
        o_v[:, pl.ds(0, 128)] += head_grad(sg_v, s_rows, k_widths[1])
        return kl

    kl = lax.fori_loop(0, 8, kv_head, kl)
    g_v[:, lanes] = o_v[:, pl.ds(0, 128)].astype(BF)
    loss = kl / (3.0 * R * length.astype(F32))
    packed = dot(g_v[...], select_ref[...])
    lane = lax.broadcasted_iota(jnp.int32, packed.shape, 1)
    packed = jnp.where(lane == q_widths[1] * 4 + k_widths[1] * 8, loss, packed)
    o_v[...] = packed
    grads_out[...] = packed.astype(BF)
    piece = rows // 16
    for place in range(8):
        core_bit, x_step = place // 4, place % 4
        halves = []
        for yh_bit in (0, 1):
            owner = (head ^ (2 * yh_bit + core_bit)) * 4 + ((x + x_step) & 3)
            halves.append(o_v[pl.ds(pl.multiple_of(owner * piece, 8), piece), :])
        ordered_out[pl.ds(place * 2 * piece, 2 * piece), :] = jnp.concatenate(halves, 0).astype(BF)


ANY = pl.BlockSpec(memory_space=pl.ANY)
WHOLE = pl.BlockSpec(memory_space=pltpu.VMEM)
SCALARS = pl.BlockSpec(memory_space=pltpu.SMEM)


def call(kernel, name, args, specs, outs, slots, rows, depth, cols, scratch=(), more_flops=0):
    return pl.pallas_call(
        kernel,
        out_shape=outs,
        in_specs=specs,
        out_specs=jax.tree.map(lambda _: WHOLE, outs),
        scratch_shapes=[
            pltpu.VMEM((slots, rows, 2 * depth), BF),
            pltpu.VMEM((slots, 2, depth, cols), BF),
            *scratch,
            pltpu.SemaphoreType.DMA((7 * slots,)),
        ],
        compiler_params=pltpu.CompilerParams(vmem_limit_bytes=28 * 1024 * 1024),
        cost_estimate=pl.CostEstimate(
            flops=slots * 4 * rows * depth * cols + more_flops,
            bytes_accessed=slots * 4 * depth * (rows + cols),
            transcendentals=0,
        ),
        name=name,
    )(*args)


def per_device(
    teacher_states,
    teacher_wq,
    teacher_wk,
    teacher_wv,
    student_states,
    student_wq,
    student_wk,
    student_wv,
    lengths,
):
    d = lax.axis_index("dp")
    head = lax.axis_index("head")
    x = lax.axis_index("mp")
    z, yl = d // 2, d % 2
    rows = student_states.shape[0]
    depth = teacher_wq.shape[0]
    q_width = teacher_wq.shape[1] // 4

    depth = teacher_wq.shape[0]
    part_y = teacher_wq[:, q_width:]
    z0 = jnp.concatenate(
        [jnp.concatenate([teacher_wk, teacher_wv], axis=1), teacher_wq[:, :q_width]], axis=0
    )
    y_cols = part_y.shape[1]
    cat, fence = jnp.concatenate, lax.optimization_barrier

    sq, sk = student_wq.shape[1], student_wk.shape[1]
    q_head, width = sq // 4, student_states.shape[1]
    length = lengths[0]
    states = lax.all_gather(teacher_states, ("head", "mp"), axis=1, tiled=True)

    other_y = swap_dp(part_y, 1)
    z1a, z1b = shift_z(z0, 1), shift_z(z0, -1)
    other_y, z1a, z1b = fence((other_y, z1a, z1b))
    pair_y = jnp.where(yl == 0, cat([part_y, other_y], 0), cat([other_y, part_y], 0))
    m1a = shift_z(cat([pair_y, z1a], 1), 1)
    m1b = shift_z(cat([pair_y, z1b], 1), -1)
    c1 = swap_dp(cat([z0, z1a, z1b], 0), 1)
    student_w = cat([student_wq, student_wk, student_wv], 1)
    wide_w = jnp.pad(student_w, ((0, 128), (0, 96)))
    wide_w = wide_w.at[width, sq + 2 * sk].set(1.0)
    m1a, m1b, c1, wide_w = fence((m1a, m1b, c1, wide_w))
    m2a, m2b = shift_z(m1a, 1), shift_z(m1b, -1)
    c2 = swap_dp(cat([m1a[:, y_cols:], m1b[:, y_cols:]], 0), 1)
    unit = width // 16
    columns = []
    for e in range(4):
        blocks = []
        for r in range(4):
            owner = ((d ^ e) + 4 * r) % 16
            blocks.append(lax.dynamic_slice(student_states, (0, owner * unit), (rows, unit)))
        columns.append(cat(blocks, 1))
    m2a, m2b, c2, *columns = fence((m2a, m2b, c2, *columns))
    m3a, m3b = shift_z(m2a, 1), shift_z(m2b, -1)
    c3 = swap_dp(cat([m2a[:, y_cols:], m2b[:, y_cols:]], 0), 1)
    padded = [student_wq[:, i * q_head : (i + 1) * q_head] for i in (1, 2, 3, 0)]
    padded.insert(3, cat([student_wk, student_wv], 1))
    padded = cat([jnp.pad(part, ((0, 0), (0, 128 - part.shape[1]))) for part in padded], 1)
    student = dot(student_states, padded).astype(BF)
    coord = jnp.stack([z, yl, head, x, length]).astype(jnp.int32)
    cols = y_cols + 2 * q_width
    acc_shape = jax.ShapeDtypeStruct((rows, cols), F32)
    near = call(
        near_kernel, "near",
        (coord, states, pair_y, z0, z1a, z1b, m1a, m1b, m2a, m2b, c1, c2),
        [SCALARS] + [ANY] * 11, acc_shape, 5, rows, depth, cols,
    )
    m3a, m3b, c3, near, student = fence((m3a, m3b, c3, near, student))
    f0 = shift_z(m3a[:depth, :y_cols], 1)
    f1 = shift_z(m3b[depth:, :y_cols], -1)
    c4 = swap_dp(m3a[:, y_cols:], 1)
    acc = call(
        far_kernel, "far", (coord, near, states, m2a, m2b, m3a, m3b, c3),
        [SCALARS, WHOLE] + [ANY] * 6, acc_shape, 2, rows, depth, cols,
    )

    select = np.zeros((cols, 384), np.float32)
    for i, block in enumerate((4, 0, 1, 2)):
        for j in range(q_head):
            select[block * 128 + j, i * q_head + j] = 1.0
    for j in range(2 * sk):
        select[3 * 128 + j, sq + j] = 1.0
    widths = ((q_width, q_head), (teacher_wk.shape[1] // 4, sk // 4))
    out = jax.ShapeDtypeStruct((rows, 384), BF)
    with_loss, ordered = call(
        functools.partial(finish_kernel, widths), "finish",
        (coord, acc, student, jnp.asarray(select, BF), states, m3a, f0, f1, c4),
        [SCALARS, WHOLE, WHOLE, WHOLE] + [ANY] * 5, (out, out), 1, rows, depth, cols,
        scratch=(
            pltpu.VMEM((rows, cols), BF),
            pltpu.VMEM((rows, cols), BF),
            pltpu.VMEM((rows, 384), F32),
            pltpu.VMEM((rows, rows), BF),
        ),
        more_flops=12 * 8 * rows * rows * 128,
    )
    grads = with_loss[:, : sq + 2 * sk]
    half = rows // 2

    piece = rows // 16

    def state_term(part):
        return lax.dot_general(
            part, wide_w, (((1,), (1,)), ((), ())), preferred_element_type=F32
        ).astype(BF)

    def weight_term(e, grads):
        return lax.dot_general(
            grads, columns[e], (((0,), (0,)), ((), ())), preferred_element_type=F32
        )

    term_out, grads = fence((state_term(ordered[half:]), grads))
    from_core = swap_head(term_out, 1)
    terms = [weight_term(e, grads).astype(BF) for e in (3, 1, 2)]
    *terms, ordered = fence((*terms, ordered))
    received = [swap_dp(term, e) for term, e in zip(terms, (3, 1, 2))]
    summed = (state_term(ordered[:half]).astype(F32) + from_core.astype(F32)).astype(BF)
    summed, grads = fence((summed, grads))
    slab = half // 4
    sent = [shift_x(summed[step * slab : (step + 1) * slab], step) for step in (2, 1, 3)]
    first_square = weight_term(0, grads)
    *received, first_square = fence((*received, *sent, first_square))
    received, sent = received[:3], received[3:]
    square = first_square
    for part in received:
        square = square + part.astype(F32)
    chunks = [square[:, r * unit : (r + 1) * unit] for r in range(4)]
    total = summed[:slab].astype(F32)
    for part in sent:
        total = total + part.astype(F32)
    last = swap_head(total[piece:].astype(BF), 2)
    weight_grad = chunks[0]
    for r in (2, 1, 3):
        moved = lax.ppermute(
            chunks[r].astype(BF), "dp", [(i, (i + 4 * r) % 16) for i in range(16)]
        )
        weight_grad = weight_grad + moved.astype(F32)
    weight_grad = weight_grad.T
    total = total[:piece] + last.astype(F32)
    grad_states = total[:, :width]
    seq_loss = total[0, width : width + 1]

    return (
        weight_grad[:, :sq],
        weight_grad[:, sq : sq + sk],
        weight_grad[:, sq + sk :],
        grad_states,
        seq_loss,
    )


def solution(mesh):
    in_specs = (
        P("dp", ("head", "mp")),
        P("dp", ("head", "mp")),
        P("dp", ("head", "mp")),
        P("dp", ("head", "mp")),
        P("dp", None),
        P(None, ("head", "mp")),
        P(None, ("head", "mp")),
        P(None, ("head", "mp")),
        P("dp"),
    )
    out_specs = (
        P("dp", ("head", "mp")),
        P("dp", ("head", "mp")),
        P("dp", ("head", "mp")),
        P(("dp", "head", "mp"), None),
        P("dp"),
    )
    return jax.shard_map(
        per_device, mesh=mesh, in_specs=in_specs, out_specs=out_specs, check_vma=False
    )
```

```python
import functools
import math

import jax
import jax.numpy as jnp
import numpy as np
from jax import lax
from jax.experimental import pallas as pl
from jax.experimental.pallas import tpu as pltpu
from jax.sharding import PartitionSpec as P

R = 64

LOSS_SCALE = 16.0
MASK_VALUE = -1000000000.0

BF = jnp.bfloat16
F32 = jnp.float32


def shift_z(a, step):
    return lax.ppermute(a, "dp", [(d, (d + 2 * step) % 16) for d in range(16)])


def swap_dp(a, bits):
    return lax.ppermute(a, "dp", [(d, d ^ bits) for d in range(16)])


def swap_head(a, bits):
    return lax.ppermute(a, "head", [(h, h ^ bits) for h in range(4)])


def shift_x(a, step):
    return lax.ppermute(a, "mp", [(m, (m + step) % 4) for m in range(4)])


def dot(a, b):
    return jnp.dot(a, b, preferred_element_type=F32)


OFFSETS = (0, -1, 1, -2, 2, -3, 3, 4)


class Loader:
    def __init__(self, coord, states, a_v, w_v, sems):
        self.z, self.yl = coord[0], coord[1]
        self.states, self.a_v, self.w_v, self.sems = states, a_v, w_v, sems
        self.count = 0
        self.slots = []

    def copy(self, src, dst):
        made = pltpu.make_async_copy(src, dst, self.sems.at[self.count])
        self.count += 1
        made.start()
        return made

    def load(self, offset, y_parts, own, crossed):
        slot, w_v = len(self.slots), self.w_v
        depth, z_cols = w_v.shape[2], w_v.shape[3] // 5
        y_cols = 3 * z_cols
        owner = (self.z + offset + 8) & 7
        first = pl.multiple_of(owner * 2 * depth, 128)
        made = [self.copy(self.states.at[:, pl.ds(first, 2 * depth)], self.a_v.at[slot])]
        for side, (ref, row) in enumerate(y_parts or ()):
            src = ref.at[pl.ds(row, depth), pl.ds(0, y_cols)]
            made.append(self.copy(src, w_v.at[slot, side, :, pl.ds(0, y_cols)]))
        if own is not None:
            for fold in (0, 1):
                cols = pl.ds(y_cols + fold * z_cols, z_cols)
                for (ref, row, col), side in ((own, self.yl), (crossed, 1 - self.yl)):
                    src = ref.at[pl.ds(row + fold * depth, depth), pl.ds(col, z_cols)]
                    made.append(self.copy(src, w_v.at[slot, side, :, cols]))
        self.slots.append(made)

    def term(self, slot, cols=slice(None)):
        for made in self.slots[slot]:
            made.wait()
        a, w = self.a_v[slot], self.w_v[slot, :, :, cols]
        return dot(a, w.reshape(w.shape[0] * w.shape[1], w.shape[2]))


def near_kernel(coord, states, pair_y, z0, z1a, z1b, m1a, m1b, m2a, m2b, c1, c2, acc, a_v, w_v, sems):
    depth, y_cols = w_v.shape[2], pair_y.shape[1]
    loader = Loader(coord, states, a_v, w_v, sems)
    pieces = (
        (pair_y, (z0, 0, 0), (c1, 0)),
        (m1a, (z1a, 0, 0), (c1, 2)),
        (m1b, (z1b, 0, 0), (c1, 4)),
        (m2a, (m1a, 0, y_cols), (c2, 0)),
        (m2b, (m1b, 0, y_cols), (c2, 2)),
    )
    for offset, (y_ref, own, (crossed, place)) in zip(OFFSETS, pieces):
        loader.load(
            offset, ((y_ref, 0), (y_ref, depth)), own, (crossed, place * depth, 0)
        )
    acc[...] = loader.term(0)
    for slot in range(1, 5):
        acc[...] += loader.term(slot)


BLOCK = 64


def relation_head(teacher, student, teacher_rows, student_rows, widths, length, valid_keys, sg_v):
    rows = teacher.shape[0]
    nt = (((1,), (1,)), ((), ()))
    teacher_scale, student_scale = (1.0 / math.sqrt(w) for w in widths)
    kl = jnp.zeros((1, 1), F32)
    for start in range(0, rows, BLOCK):
        part = slice(start, start + BLOCK)
        ts = lax.dot_general(teacher_rows[part], teacher, nt, preferred_element_type=F32)
        ss = lax.dot_general(student_rows[part], student, nt, preferred_element_type=F32)
        ts = jnp.where(valid_keys, ts * teacher_scale, MASK_VALUE)
        ss = jnp.where(valid_keys, ss * student_scale, MASK_VALUE)
        t_max = jnp.max(ts, axis=-1, keepdims=True)
        s_max = jnp.max(ss, axis=-1, keepdims=True)
        te = jnp.exp(ts - t_max)
        se = jnp.exp(ss - s_max)
        t_sum = jnp.sum(te, axis=-1, keepdims=True)
        s_sum = jnp.sum(se, axis=-1, keepdims=True)
        cross = jnp.sum(te * (ts - ss), axis=-1, keepdims=True) / t_sum
        row_kl = cross - (t_max + jnp.log(t_sum)) + (s_max + jnp.log(s_sum))
        row = lax.broadcasted_iota(jnp.int32, (BLOCK, 1), 0) + start
        valid = row < length
        kl = kl + jnp.sum(jnp.where(valid, row_kl, 0.0), axis=0, keepdims=True)
        t_gain = jnp.where(valid, LOSS_SCALE / t_sum, 0.0)
        s_gain = jnp.where(valid, LOSS_SCALE / s_sum, 0.0)
        sg_v[part, :] = (se * s_gain - te * t_gain).astype(BF)
    return kl


def head_grad(sg_v, student, width):
    sg = sg_v[...]
    tn = (((0,), (0,)), ((), ()))
    both = dot(sg, student) + lax.dot_general(sg, student, tn, preferred_element_type=F32)
    return both * (1.0 / math.sqrt(width))


def finish_z_kernel(
    widths, coord, before, student_ref, select_ref, states, m2a, m2b, m3a, m3b, c3, d4,
    acc_out, grads_out, kl_out, a_v, w_v, t_v, g_v, o_v, sg_v, sems,
):
    depth, y_cols = w_v.shape[2], w_v.shape[3] // 5 * 3
    q_widths, k_widths = widths
    length = coord[4]
    rows = t_v.shape[0]
    loader = Loader(coord, states, a_v, w_v, sems)
    loader.load(-3, ((m3a, 0), (m3a, depth)), (m2a, 0, y_cols), (c3, 0, 0))
    loader.load(3, ((m3b, 0), (m3b, depth)), (m2b, 0, y_cols), (c3, 2 * depth, 0))
    loader.load(4, None, (m3a, 0, y_cols), (d4, 0, 0))
    total = before[...] + loader.term(0) + loader.term(1)
    acc_out[...] = total[:, :y_cols]
    t_v[...] = (total[:, y_cols:] + loader.term(2, slice(y_cols, None))).astype(BF)
    valid_keys = lax.broadcasted_iota(jnp.int32, (1, rows), 1) < length

    first_lanes = pl.ds(128, 128)
    teacher, student = t_v[:, first_lanes], student_ref[:, pl.ds(y_cols + 128, 128)]
    kl = relation_head(teacher, student, teacher, student, q_widths, length, valid_keys, sg_v)
    g_v[:, first_lanes] = head_grad(sg_v, student, q_widths[1]).astype(BF)

    lane = lax.broadcasted_iota(jnp.int32, (rows, 128), 1)
    o_v[...] = jnp.zeros_like(o_v)

    def kv_head(i, kl):
        teacher, student = t_v[:, pl.ds(0, 128)], student_ref[:, pl.ds(y_cols, 128)]
        t_first, s_first = i * k_widths[0], i * k_widths[1]
        t_mine = (lane >= t_first) & (lane < t_first + k_widths[0])
        s_mine = (lane >= s_first) & (lane < s_first + k_widths[1])
        t_rows = jnp.where(t_mine, teacher.astype(F32), 0.0).astype(BF)
        s_rows = jnp.where(s_mine, student.astype(F32), 0.0).astype(BF)
        kl = kl + relation_head(
            teacher, student, t_rows, s_rows, k_widths, length, valid_keys, sg_v
        )
        o_v[...] += head_grad(sg_v, s_rows, k_widths[1])
        return kl

    kl = lax.fori_loop(0, 8, kv_head, kl)
    g_v[:, pl.ds(0, 128)] = o_v[...].astype(BF)
    grads_out[...] = dot(g_v[...], select_ref[...]).astype(BF)
    kl_out[...] = jnp.broadcast_to(kl, kl_out.shape)


def finish_y_kernel(
    widths, coord, before, student_ref, select_ref, z_grads, z_kl, states, f0, f1,
    grads_out, ordered_out, a_v, w_v, t_v, g_v, o_v, sg_v, sems,
):
    y_cols = w_v.shape[3] // 5 * 3
    q_widths = widths[0]
    head, x, length = coord[2], coord[3], coord[4]
    rows = t_v.shape[0]
    loader = Loader(coord, states, a_v, w_v, sems)
    loader.load(4, ((f0, 0), (f1, 0)), None, None)
    t_v[...] = (before[...] + loader.term(0, slice(0, y_cols))).astype(BF)
    valid_keys = lax.broadcasted_iota(jnp.int32, (1, rows), 1) < length

    def q_head(i, kl):
        lanes = pl.ds(pl.multiple_of(i * 128, 128), 128)
        teacher, student = t_v[:, lanes], student_ref[:, lanes]
        kl = kl + relation_head(
            teacher, student, teacher, student, q_widths, length, valid_keys, sg_v
        )
        g_v[:, lanes] = head_grad(sg_v, student, q_widths[1]).astype(BF)
        return kl

    kl = lax.fori_loop(0, 3, q_head, z_kl[:1, :1])
    loss = kl / (3.0 * R * length.astype(F32))
    packed = dot(g_v[...], select_ref[...])
    lane = lax.broadcasted_iota(jnp.int32, packed.shape, 1)
    packed = jnp.where(lane == 3 * q_widths[1], loss, packed)
    grads_out[...] = packed.astype(BF)
    o_v[:, pl.ds(0, 128)] = z_grads[...].astype(F32)
    o_v[:, pl.ds(128, 256)] = packed
    piece = rows // 16
    for place in range(8):
        core_bit, x_step = place // 4, place % 4
        halves = []
        for yh_bit in (0, 1):
            owner = (head ^ (2 * yh_bit + core_bit)) * 4 + ((x + x_step) & 3)
            halves.append(o_v[pl.ds(pl.multiple_of(owner * piece, 8), piece), :])
        ordered_out[pl.ds(place * 2 * piece, 2 * piece), :] = jnp.concatenate(halves, 0).astype(BF)


ANY = pl.BlockSpec(memory_space=pl.ANY)
WHOLE = pl.BlockSpec(memory_space=pltpu.VMEM)
SCALARS = pl.BlockSpec(memory_space=pltpu.SMEM)


def call(kernel, name, args, specs, outs, slots, rows, depth, cols, scratch=(), more_flops=0):
    return pl.pallas_call(
        kernel,
        out_shape=outs,
        in_specs=specs,
        out_specs=jax.tree.map(lambda _: WHOLE, outs),
        scratch_shapes=[
            pltpu.VMEM((slots, rows, 2 * depth), BF),
            pltpu.VMEM((slots, 2, depth, cols), BF),
            *scratch,
            pltpu.SemaphoreType.DMA((7 * slots,)),
        ],
        compiler_params=pltpu.CompilerParams(vmem_limit_bytes=28 * 1024 * 1024),
        cost_estimate=pl.CostEstimate(
            flops=slots * 4 * rows * depth * cols + more_flops,
            bytes_accessed=slots * 4 * depth * (rows + cols),
            transcendentals=0,
        ),
        name=name,
    )(*args)


def per_device(
    teacher_states,
    teacher_wq,
    teacher_wk,
    teacher_wv,
    student_states,
    student_wq,
    student_wk,
    student_wv,
    lengths,
):
    d = lax.axis_index("dp")
    head = lax.axis_index("head")
    x = lax.axis_index("mp")
    z, yl = d // 2, d % 2
    rows = student_states.shape[0]
    depth = teacher_wq.shape[0]
    q_width = teacher_wq.shape[1] // 4

    depth = teacher_wq.shape[0]
    part_y = teacher_wq[:, q_width:]
    part_y, teacher_wk, teacher_wv = lax.optimization_barrier((part_y, teacher_wk, teacher_wv))
    z0 = jnp.concatenate(
        [jnp.concatenate([teacher_wk, teacher_wv], axis=1), teacher_wq[:, :q_width]], axis=0
    )
    y_cols = part_y.shape[1]
    cat, fence = jnp.concatenate, lax.optimization_barrier

    sq, sk = student_wq.shape[1], student_wk.shape[1]
    q_head, width = sq // 4, student_states.shape[1]
    length = lengths[0]
    states = lax.all_gather(teacher_states, ("head", "mp"), axis=1, tiled=True)

    other_y = swap_dp(part_y, 1)
    z1a, z1b = shift_z(z0, 1), shift_z(z0, -1)
    other_y, z1a, z1b = fence((other_y, z1a, z1b))
    pair_y = jnp.where(yl == 0, cat([part_y, other_y], 0), cat([other_y, part_y], 0))
    m1a = shift_z(cat([pair_y, z1a], 1), 1)
    m1b = shift_z(cat([pair_y, z1b], 1), -1)
    c1 = swap_dp(cat([z0, z1a, z1b], 0), 1)
    z_width = 2 * sk + q_head
    wide_w = cat(
        [
            cat([student_wk, student_wv, student_wq[:, :q_head]], 1),
            jnp.zeros((width, 128 - z_width), BF),
            student_wq[:, q_head:],
            jnp.zeros((width, 256 - 3 * q_head), BF),
        ],
        1,
    )
    wide_w = jnp.pad(wide_w, ((0, 128), (0, 0)))
    wide_w = wide_w.at[width, 128 + 3 * q_head].set(1.0)
    m1a, m1b, c1, wide_w = fence((m1a, m1b, c1, wide_w))
    m2a, m2b = shift_z(m1a, 1), shift_z(m1b, -1)
    c2 = swap_dp(cat([m1a[:, y_cols:], m1b[:, y_cols:]], 0), 1)
    unit = width // 16
    columns = []
    for e in range(4):
        blocks = []
        for r in range(4):
            owner = ((d ^ e) + 4 * r) % 16
            blocks.append(lax.dynamic_slice(student_states, (0, owner * unit), (rows, unit)))
        columns.append(cat(blocks, 1))
    m2a, m2b, c2, *columns = fence((m2a, m2b, c2, *columns))
    m3a, m3b = shift_z(m2a, 1), shift_z(m2b[:, :y_cols], -1)
    c3 = swap_dp(cat([m2a[:, y_cols:], m2b[:, y_cols:]], 0), 1)
    d4 = lax.ppermute(m2b[:, y_cols:], "dp", [(i, ((i - 2) % 16) ^ 1) for i in range(16)])
    padded = [student_wq[:, i * q_head : (i + 1) * q_head] for i in (1, 2, 3, 0)]
    padded.insert(3, cat([student_wk, student_wv], 1))
    padded = cat([jnp.pad(part, ((0, 0), (0, 128 - part.shape[1]))) for part in padded], 1)
    student = dot(student_states, padded).astype(BF)
    coord = jnp.stack([z, yl, head, x, length]).astype(jnp.int32)
    cols = y_cols + 2 * q_width
    acc_shape = jax.ShapeDtypeStruct((rows, cols), F32)
    near = call(
        near_kernel, "near",
        (coord, states, pair_y, z0, z1a, z1b, m1a, m1b, m2a, m2b, c1, c2),
        [SCALARS] + [ANY] * 11, acc_shape, 5, rows, depth, cols,
    )
    m3a, m3b, c3, d4, near, student = fence((m3a, m3b, c3, d4, near, student))
    f0 = shift_z(m3a[:depth, :y_cols], 1)
    f1 = shift_z(m3b[depth:], -1)

    select_z = np.zeros((256, 128), np.float32)
    for j in range(2 * sk):
        select_z[j, j] = 1.0
    for j in range(q_head):
        select_z[128 + j, 2 * sk + j] = 1.0
    select_y = np.zeros((y_cols, 256), np.float32)
    for i in range(3):
        for j in range(q_head):
            select_y[i * 128 + j, i * q_head + j] = 1.0
    widths = ((q_width, q_head), (teacher_wk.shape[1] // 4, sk // 4))

    def shape(columns, dtype=BF):
        return jax.ShapeDtypeStruct((rows, columns), dtype)

    acc, grads_z, kl_z = call(
        functools.partial(finish_z_kernel, widths), "finish_z",
        (coord, near, student, jnp.asarray(select_z, BF), states, m2a, m2b, m3a, m3b, c3, d4),
        [SCALARS, WHOLE, WHOLE, WHOLE] + [ANY] * 7,
        (shape(y_cols, F32), shape(128), jax.ShapeDtypeStruct((8, 128), F32)),
        3, rows, depth, cols,
        scratch=(
            pltpu.VMEM((rows, 256), BF),
            pltpu.VMEM((rows, 256), BF),
            pltpu.VMEM((rows, 128), F32),
            pltpu.VMEM((rows, rows), BF),
        ),
        more_flops=9 * 8 * rows * rows * 128,
    )

    def weight_term(e, grads):
        return lax.dot_general(
            grads, columns[e], (((0,), (0,)), ((), ())), preferred_element_type=F32
        )

    terms_z = [weight_term(e, grads_z).astype(BF) for e in (3, 1, 2)]
    *terms_z, acc = fence((*terms_z, acc))
    received_z = [swap_dp(term, e) for term, e in zip(terms_z, (3, 1, 2))]
    grads_y, ordered = call(
        functools.partial(finish_y_kernel, widths), "finish_y",
        (coord, acc, student, jnp.asarray(select_y, BF), grads_z, kl_z, states, f0, f1),
        [SCALARS, WHOLE, WHOLE, WHOLE, WHOLE, WHOLE] + [ANY] * 3, (shape(256), shape(384)),
        1, rows, depth, cols,
        scratch=(
            pltpu.VMEM((rows, y_cols), BF),
            pltpu.VMEM((rows, y_cols), BF),
            pltpu.VMEM((rows, 384), F32),
            pltpu.VMEM((rows, rows), BF),
        ),
        more_flops=3 * 8 * rows * rows * 128,
    )
    grads = grads_y[:, :176]
    half = rows // 2

    piece = rows // 16

    def state_term(part):
        return lax.dot_general(
            part, wide_w, (((1,), (1,)), ((), ())), preferred_element_type=F32
        ).astype(BF)

    term_out, grads = fence((state_term(ordered[half:]), grads))
    from_core = swap_head(term_out, 1)
    terms = [weight_term(e, grads).astype(BF) for e in (3, 1, 2)]
    *terms, ordered = fence((*terms, ordered))
    received = [swap_dp(term, e) for term, e in zip(terms, (3, 1, 2))]
    summed = (state_term(ordered[:half]).astype(F32) + from_core.astype(F32)).astype(BF)
    summed, grads = fence((summed, grads))
    slab = half // 4
    sent = [shift_x(summed[step * slab : (step + 1) * slab], step) for step in (2, 1, 3)]
    first_square = weight_term(0, grads)
    square_z = weight_term(0, grads_z)
    for part in received_z:
        square_z = square_z + part.astype(F32)
    *received, first_square = fence((*received, *sent, first_square))
    received, sent = received[:3], received[3:]
    square = first_square
    for part in received:
        square = square + part.astype(F32)
    square = cat([square_z, square], 0)
    chunks = [square[:, r * unit : (r + 1) * unit] for r in range(4)]
    total = summed[:slab].astype(F32)
    for part in sent:
        total = total + part.astype(F32)
    last = swap_head(total[piece:].astype(BF), 2)
    weight_grad = chunks[0]
    for r in (2, 1, 3):
        moved = lax.ppermute(
            chunks[r].astype(BF), "dp", [(i, (i + 4 * r) % 16) for i in range(16)]
        )
        weight_grad = weight_grad + moved.astype(F32)
    weight_grad = weight_grad.T
    total = total[:piece] + last.astype(F32)
    grad_states = total[:, :width]
    seq_loss = total[0, width : width + 1]

    return (
        cat([weight_grad[:, 2 * sk : z_width], weight_grad[:, 128 : 128 + 3 * q_head]], 1),
        weight_grad[:, :sk],
        weight_grad[:, sk : 2 * sk],
        grad_states,
        seq_loss,
    )


def solution(mesh):
    in_specs = (
        P("dp", ("head", "mp")),
        P("dp", ("head", "mp")),
        P("dp", ("head", "mp")),
        P("dp", ("head", "mp")),
        P("dp", None),
        P(None, ("head", "mp")),
        P(None, ("head", "mp")),
        P(None, ("head", "mp")),
        P("dp"),
    )
    out_specs = (
        P("dp", ("head", "mp")),
        P("dp", ("head", "mp")),
        P("dp", ("head", "mp")),
        P(("dp", "head", "mp"), None),
        P("dp"),
    )
    return jax.shard_map(
        per_device, mesh=mesh, in_specs=in_specs, out_specs=out_specs, check_vma=False
    )
```

```python
import functools
import math

import jax
import jax.numpy as jnp
import numpy as np
from jax import lax
from jax.experimental import pallas as pl
from jax.experimental.pallas import tpu as pltpu
from jax.sharding import PartitionSpec as P

R = 64

LOSS_SCALE = 16.0
MASK_VALUE = -1000000000.0

BF = jnp.bfloat16
F32 = jnp.float32


def shift_z(a, step):
    return lax.ppermute(a, "dp", [(d, (d + 2 * step) % 16) for d in range(16)])


def swap_dp(a, bits):
    return lax.ppermute(a, "dp", [(d, d ^ bits) for d in range(16)])


def swap_head(a, bits):
    return lax.ppermute(a, "head", [(h, h ^ bits) for h in range(4)])


def shift_x(a, step):
    return lax.ppermute(a, "mp", [(m, (m + step) % 4) for m in range(4)])


def dot(a, b):
    return jnp.dot(a, b, preferred_element_type=F32)


OFFSETS = (0, -1, 1, -2, 2, -3, 3, 4)


class Loader:
    def __init__(self, coord, states, a_v, w_v, sems):
        self.z, self.yl = coord[0], coord[1]
        self.states, self.a_v, self.w_v, self.sems = states, a_v, w_v, sems
        self.count = 0
        self.slots = []

    def copy(self, src, dst):
        made = pltpu.make_async_copy(src, dst, self.sems.at[self.count])
        self.count += 1
        made.start()
        return made

    def load(self, offset, y_parts, own, crossed):
        slot, w_v = len(self.slots), self.w_v
        depth, cols = w_v.shape[2:]
        y_cols = cols // 5 * 3
        owner = (self.z + offset + 8) & 7
        first = pl.multiple_of(owner * 2 * depth, 128)
        made = [self.copy(self.states.at[:, pl.ds(first, 2 * depth)], self.a_v.at[slot])]
        for side, ref in enumerate(y_parts):
            src = ref.at[:, pl.ds(0, y_cols)]
            made.append(self.copy(src, w_v.at[slot, side, :, pl.ds(0, y_cols)]))
        z_lanes = pl.ds(y_cols, cols - y_cols)
        for (ref, row, col), side in ((own, self.yl), (crossed, 1 - self.yl)):
            src = ref.at[pl.ds(row, depth), pl.ds(col, cols - y_cols)]
            made.append(self.copy(src, w_v.at[slot, side, :, z_lanes]))
        self.slots.append(made)

    def term(self, slot):
        for made in self.slots[slot]:
            made.wait()
        a, w = self.a_v[slot], self.w_v[slot]
        return dot(a, w.reshape(w.shape[0] * w.shape[1], w.shape[2]))


def near_kernel(
    coord, states, top, bottom, z0, z1a, z1b, t1a, t1b, b1a, b1b, t2a, t2b, b2a, b2b, c1, c2,
    acc, a_v, w_v, sems,
):
    depth, y_cols = top.shape
    loader = Loader(coord, states, a_v, w_v, sems)
    loader.load(0, (top, bottom), (z0, 0, 0), (c1, 0, 0))
    loader.load(-1, (t1a, b1a), (z1a, 0, 0), (c1, depth, 0))
    loader.load(1, (t1b, b1b), (z1b, 0, 0), (c1, 2 * depth, 0))
    loader.load(-2, (t2a, b2a), (t1a, 0, y_cols), (c2, 0, 0))
    loader.load(2, (t2b, b2b), (t1b, 0, y_cols), (c2, depth, 0))
    acc[...] = loader.term(0)
    for slot in range(1, 5):
        acc[...] += loader.term(slot)


def far_kernel(coord, before, states, t2a, t2b, t3a, t3b, b3a, b3b, c3, acc, a_v, w_v, sems):
    depth, y_cols = b3a.shape
    loader = Loader(coord, states, a_v, w_v, sems)
    loader.load(-3, (t3a, b3a), (t2a, 0, y_cols), (c3, 0, 0))
    loader.load(3, (t3b, b3b), (t2b, 0, y_cols), (c3, depth, 0))
    acc[...] = before[...] + loader.term(0)
    acc[...] += loader.term(1)


BLOCK = 64


HEADS = 12
NT = (((1,), (1,)), ((), ()))
TN = (((0,), (0,)), ((), ()))


def place_of(i, of_query, of_other):
    query = i < 4
    block = jnp.where(query, i + i // 3, 3)
    first = jnp.where(query, 0, (i - 4) * of_other)
    return block, first, jnp.where(query, 128, of_other), query


def only(cols, first, width):
    lane = lax.broadcasted_iota(jnp.int32, cols.shape, 1)
    mine = (lane >= first) & (lane < first + width)
    return jnp.where(mine, cols.astype(F32), 0.0).astype(BF)


def scale_of(query, widths):
    scales = [1.0 / (math.sqrt(w) * math.log(2.0)) for w in widths]
    return jnp.where(query, scales[0], scales[1])


def student_kernel(widths, coord, student_ref, log_out, prob_out):
    length, rows = coord[4], student_ref.shape[0]
    _, first, width, query = place_of(pl.program_id(0), *widths)
    scale = scale_of(query, widths)
    student = student_ref[...]
    mine = only(student, first, width)
    valid_keys = lax.broadcasted_iota(jnp.int32, (1, rows), 1) < length
    for start in range(0, rows, BLOCK):
        part = slice(start, start + BLOCK)
        scores = lax.dot_general(mine[part], student, NT, preferred_element_type=F32)
        scores = jnp.where(valid_keys, scores * scale, MASK_VALUE)
        scores = scores - jnp.max(scores, axis=-1, keepdims=True)
        weight = jnp.exp2(scores)
        total = jnp.sum(weight, axis=-1, keepdims=True)
        log_out[0, part, :] = scores - jnp.log2(total)
        valid = lax.broadcasted_iota(jnp.int32, (BLOCK, 1), 0) + start < length
        prob_out[0, part, :] = weight * jnp.where(valid, LOSS_SCALE / total, 0.0)


def finish_kernel(
    widths, coord, before, student_ref, select_ref, states, t3a, ft, fb, c4, logs, probs,
    grads_out, ordered_out, a_v, w_v, t_v, g_v, o_v, sg_v, log_v, prob_v, head_sems, sems,
):
    depth, y_cols = fb.shape
    t_widths, s_widths = widths
    head, x, length = coord[2], coord[3], coord[4]
    rows = t_v.shape[0]
    loader = Loader(coord, states, a_v, w_v, sems)
    loader.load(4, (ft, fb), (t3a, 0, y_cols), (c4, 0, 0))

    def head_copies(i):
        return (
            pltpu.make_async_copy(logs.at[i], log_v.at[i], head_sems.at[0, i]),
            pltpu.make_async_copy(probs.at[i], prob_v.at[i], head_sems.at[1, i]),
        )

    for i in range(HEADS):
        for made in head_copies(i):
            made.start()
    t_v[...] = (before[...] + loader.term(0)).astype(BF)
    valid_keys = lax.broadcasted_iota(jnp.int32, (1, rows), 1) < length
    o_v[...] = jnp.zeros_like(o_v)

    def one_head(i, kl):
        block, t_first, t_width, query = place_of(i, *t_widths)
        _, s_first, s_width, _ = place_of(i, *s_widths)
        scale = scale_of(query, t_widths)
        lanes = pl.ds(pl.multiple_of(block * 128, 128), 128)
        teacher = t_v[:, lanes]
        mine = only(teacher, t_first, t_width)
        for made in head_copies(i):
            made.wait()
        for start in range(0, rows, BLOCK):
            part = slice(start, start + BLOCK)
            scores = lax.dot_general(mine[part], teacher, NT, preferred_element_type=F32)
            scores = jnp.where(valid_keys, scores * scale, MASK_VALUE)
            top = jnp.max(scores, axis=-1, keepdims=True)
            weight = jnp.exp2(scores - top)
            total = jnp.sum(weight, axis=-1, keepdims=True)
            cross = jnp.sum(weight * (scores - log_v[i, part, :]), axis=-1, keepdims=True)
            row_kl = cross / total - (top + jnp.log2(total))
            valid = lax.broadcasted_iota(jnp.int32, (BLOCK, 1), 0) + start < length
            kl = kl + jnp.sum(jnp.where(valid, row_kl, 0.0), axis=0, keepdims=True)
            gain = jnp.where(valid, LOSS_SCALE / total, 0.0)
            sg_v[part, :] = (prob_v[i, part, :] - weight * gain).astype(BF)
        student = only(student_ref[:, lanes], s_first, s_width)
        sg = sg_v[...]
        both = dot(sg, student) + lax.dot_general(sg, student, TN, preferred_element_type=F32)
        over = [1.0 / math.sqrt(w) for w in s_widths]
        o_v[:, lanes] += both * jnp.where(query, over[0], over[1])
        return kl

    kl = lax.fori_loop(0, HEADS, one_head, jnp.zeros((1, 1), F32))
    g_v[...] = o_v[...].astype(BF)
    loss = kl * math.log(2.0) / (3.0 * R * length.astype(F32))
    packed = dot(g_v[...], select_ref[...])
    lane = lax.broadcasted_iota(jnp.int32, packed.shape, 1)
    packed = jnp.where(lane == s_widths[0] * 4 + s_widths[1] * 8, loss, packed)
    o_v[:, pl.ds(0, packed.shape[1])] = packed
    grads_out[...] = packed.astype(BF)
    piece = rows // 16
    for place in range(8):
        core_bit, x_step = place // 4, place % 4
        halves = []
        for yh_bit in (0, 1):
            owner = (head ^ (2 * yh_bit + core_bit)) * 4 + ((x + x_step) & 3)
            own_rows = pl.ds(pl.multiple_of(owner * piece, 8), piece)
            halves.append(o_v[own_rows, pl.ds(0, packed.shape[1])])
        ordered_out[pl.ds(place * 2 * piece, 2 * piece), :] = jnp.concatenate(halves, 0).astype(BF)


ANY = pl.BlockSpec(memory_space=pl.ANY)
WHOLE = pl.BlockSpec(memory_space=pltpu.VMEM)
SCALARS = pl.BlockSpec(memory_space=pltpu.SMEM)


def call(
    kernel, name, args, specs, outs, slots, rows, depth, cols, scratch=(), more_flops=0, megabytes=28
):
    return pl.pallas_call(
        kernel,
        out_shape=outs,
        in_specs=specs,
        out_specs=jax.tree.map(lambda _: WHOLE, outs),
        scratch_shapes=[
            pltpu.VMEM((slots, rows, 2 * depth), BF),
            pltpu.VMEM((slots, 2, depth, cols), BF),
            *scratch,
            pltpu.SemaphoreType.DMA((5 * slots,)),
        ],
        compiler_params=pltpu.CompilerParams(vmem_limit_bytes=megabytes * 1024 * 1024),
        cost_estimate=pl.CostEstimate(
            flops=slots * 4 * rows * depth * cols + more_flops,
            bytes_accessed=slots * 4 * depth * (rows + cols),
            transcendentals=0,
        ),
        name=name,
    )(*args)


def per_device(
    teacher_states,
    teacher_wq,
    teacher_wk,
    teacher_wv,
    student_states,
    student_wq,
    student_wk,
    student_wv,
    lengths,
):
    d = lax.axis_index("dp")
    head = lax.axis_index("head")
    x = lax.axis_index("mp")
    z, yl = d // 2, d % 2
    rows = student_states.shape[0]
    depth = teacher_wq.shape[0]
    q_width = teacher_wq.shape[1] // 4

    depth = teacher_wq.shape[0]
    part_y = teacher_wq[:, q_width:]
    z0 = jnp.concatenate([teacher_wk, teacher_wv, teacher_wq[:, :q_width]], axis=1)
    y_cols = part_y.shape[1]
    cat, fence = jnp.concatenate, lax.optimization_barrier

    sq, sk = student_wq.shape[1], student_wk.shape[1]
    q_head, width = sq // 4, student_states.shape[1]
    length = lengths[0]
    states = lax.all_gather(teacher_states, ("head", "mp"), axis=1, tiled=True)

    other_y = swap_dp(part_y, 1)
    z1a, z1b = shift_z(z0, 1), shift_z(z0, -1)
    other_y, z1a, z1b = fence((other_y, z1a, z1b))
    first_yl = yl == 0
    top = jnp.where(first_yl, part_y, other_y)
    bottom = jnp.where(first_yl, other_y, part_y)
    b1a, b1b = shift_z(bottom, 1), shift_z(bottom, -1)
    t1a = shift_z(cat([top, z1a], 1), 1)
    t1b = shift_z(cat([top, z1b], 1), -1)
    c1 = swap_dp(cat([z0, z1a, z1b], 0), 1)
    student_w = cat([student_wq, student_wk, student_wv], 1)
    wide_w = jnp.pad(student_w, ((0, 128), (0, 96)))
    wide_w = wide_w.at[width, sq + 2 * sk].set(1.0)
    padded = [student_wq[:, i * q_head : (i + 1) * q_head] for i in (1, 2, 3, 0)]
    padded.insert(3, cat([student_wk, student_wv], 1))
    padded = cat([jnp.pad(part, ((0, 0), (0, 128 - part.shape[1]))) for part in padded], 1)
    student = dot(student_states, padded).astype(BF)
    coord = jnp.stack([z, yl, head, x, length]).astype(jnp.int32)
    widths = ((q_width, teacher_wk.shape[1] // 4), (q_head, sk // 4))
    t1a, t1b, c1, wide_w, student = fence((t1a, t1b, c1, wide_w, student))
    b2a, b2b = shift_z(b1a, 1), shift_z(b1b, -1)
    t2a, t2b = shift_z(t1a, 1), shift_z(t1b, -1)
    c2 = swap_dp(cat([t1a[:, y_cols:], t1b[:, y_cols:]], 0), 1)
    unit = width // 16
    columns = []
    for e in range(4):
        blocks = []
        for r in range(4):
            owner = ((d ^ e) + 4 * r) % 16
            blocks.append(lax.dynamic_slice(student_states, (0, owner * unit), (rows, unit)))
        columns.append(cat(blocks, 1))
    score_shape = jax.ShapeDtypeStruct((HEADS, rows, rows), F32)
    score_spec = pl.BlockSpec((1, rows, rows), lambda i: (i, 0, 0))
    logs, probs = pl.pallas_call(
        functools.partial(student_kernel, widths[1]),
        grid=(HEADS,),
        out_shape=(score_shape, score_shape),
        in_specs=[
            SCALARS,
            pl.BlockSpec((rows, 128), lambda i: (0, jnp.where(i < 4, i + i // 3, 3))),
        ],
        out_specs=(score_spec, score_spec),
        compiler_params=pltpu.CompilerParams(vmem_limit_bytes=16 * 1024 * 1024),
        cost_estimate=pl.CostEstimate(
            flops=HEADS * 20 * rows * rows,
            bytes_accessed=HEADS * 8 * rows * rows,
            transcendentals=HEADS * rows * rows,
        ),
        name="student",
    )(coord, student)
    t2a, t2b, c2, logs, probs, *columns = fence((t2a, t2b, c2, logs, probs, *columns))
    b3a, b3b = shift_z(b2a, 1), shift_z(b2b, -1)
    t3a, t3b = shift_z(t2a, 1), shift_z(t2b[:, :y_cols], -1)
    c3 = swap_dp(cat([t2a[:, y_cols:], t2b[:, y_cols:]], 0), 1)
    cols = y_cols + 2 * q_width
    acc_shape = jax.ShapeDtypeStruct((rows, cols), F32)
    near_parts = (
        states, top, bottom, z0, z1a, z1b, t1a, t1b, b1a, b1b, t2a, t2b, b2a, b2b, c1, c2,
    )
    near = call(
        near_kernel, "near", (coord, *near_parts), [SCALARS] + [ANY] * len(near_parts),
        acc_shape, 5, rows, depth, cols,
    )
    t3a, t3b, b3a, b3b, c3, near = fence((t3a, t3b, b3a, b3b, c3, near))
    fb, ft = shift_z(b3a, 1), shift_z(t3b, -1)
    c4 = swap_dp(t3a[:, y_cols:], 1)
    far_parts = (states, t2a, t2b, t3a, t3b, b3a, b3b, c3)
    acc = call(
        far_kernel, "far", (coord, near, *far_parts),
        [SCALARS, WHOLE] + [ANY] * len(far_parts), acc_shape, 2, rows, depth, cols,
    )

    select = np.zeros((cols, 384), np.float32)
    for i, block in enumerate((4, 0, 1, 2)):
        for j in range(q_head):
            select[block * 128 + j, i * q_head + j] = 1.0
    for j in range(2 * sk):
        select[3 * 128 + j, sq + j] = 1.0
    out = jax.ShapeDtypeStruct((rows, 384), BF)
    with_loss, ordered = call(
        functools.partial(finish_kernel, widths), "finish",
        (coord, acc, student, jnp.asarray(select, BF), states, t3a, ft, fb, c4, logs, probs),
        [SCALARS, WHOLE, WHOLE, WHOLE] + [ANY] * 7, (out, out), 1, rows, depth, cols,
        scratch=(
            pltpu.VMEM((rows, cols), BF),
            pltpu.VMEM((rows, cols), BF),
            pltpu.VMEM((rows, cols), F32),
            pltpu.VMEM((rows, rows), BF),
            pltpu.VMEM((HEADS, rows, rows), F32),
            pltpu.VMEM((HEADS, rows, rows), F32),
            pltpu.SemaphoreType.DMA((2, HEADS)),
        ),
        more_flops=HEADS * 8 * rows * rows * 128,
        megabytes=34,
    )
    grads = with_loss[:, : sq + 2 * sk]
    half = rows // 2

    piece = rows // 16

    def state_term(part):
        return lax.dot_general(
            part, wide_w, (((1,), (1,)), ((), ())), preferred_element_type=F32
        ).astype(BF)

    def weight_term(e, grads):
        return lax.dot_general(
            grads, columns[e], (((0,), (0,)), ((), ())), preferred_element_type=F32
        )

    term_out, grads = fence((state_term(ordered[half:]), grads))
    from_core = swap_head(term_out, 1)
    terms = [weight_term(e, grads).astype(BF) for e in (3, 1, 2)]
    *terms, ordered = fence((*terms, ordered))
    received = [swap_dp(term, e) for term, e in zip(terms, (3, 1, 2))]
    summed = (state_term(ordered[:half]).astype(F32) + from_core.astype(F32)).astype(BF)
    summed, grads = fence((summed, grads))
    slab = half // 4
    sent = [shift_x(summed[step * slab : (step + 1) * slab], step) for step in (2, 1, 3)]
    first_square = weight_term(0, grads)
    *received, first_square = fence((*received, *sent, first_square))
    received, sent = received[:3], received[3:]
    square = first_square
    for part in received:
        square = square + part.astype(F32)
    chunks = [square[:, r * unit : (r + 1) * unit] for r in range(4)]
    total = summed[:slab].astype(F32)
    for part in sent:
        total = total + part.astype(F32)
    last = swap_head(total[piece:].astype(BF), 2)
    weight_grad = chunks[0]
    for r in (2, 1, 3):
        moved = lax.ppermute(
            chunks[r].astype(BF), "dp", [(i, (i + 4 * r) % 16) for i in range(16)]
        )
        weight_grad = weight_grad + moved.astype(F32)
    weight_grad = weight_grad.T
    total = total[:piece] + last.astype(F32)
    grad_states = total[:, :width]
    seq_loss = total[0, width : width + 1]

    return (
        weight_grad[:, :sq],
        weight_grad[:, sq : sq + sk],
        weight_grad[:, sq + sk :],
        grad_states,
        seq_loss,
    )


def solution(mesh):
    in_specs = (
        P("dp", ("head", "mp")),
        P("dp", ("head", "mp")),
        P("dp", ("head", "mp")),
        P("dp", ("head", "mp")),
        P("dp", None),
        P(None, ("head", "mp")),
        P(None, ("head", "mp")),
        P(None, ("head", "mp")),
        P("dp"),
    )
    out_specs = (
        P("dp", ("head", "mp")),
        P("dp", ("head", "mp")),
        P("dp", ("head", "mp")),
        P(("dp", "head", "mp"), None),
        P("dp"),
    )
    return jax.shard_map(
        per_device, mesh=mesh, in_specs=in_specs, out_specs=out_specs, check_vma=False
    )
```

```python
import functools
import math

import jax
import jax.numpy as jnp
import numpy as np
from jax import lax
from jax.experimental import pallas as pl
from jax.experimental.pallas import tpu as pltpu
from jax.sharding import PartitionSpec as P

R = 64

LOSS_SCALE = 16.0
MASK_VALUE = -1000000000.0

BF = jnp.bfloat16
F32 = jnp.float32


def shift_z(a, step):
    return lax.ppermute(a, "dp", [(d, (d + 2 * step) % 16) for d in range(16)])


def swap_dp(a, bits):
    return lax.ppermute(a, "dp", [(d, d ^ bits) for d in range(16)])


def swap_head(a, bits):
    return lax.ppermute(a, "head", [(h, h ^ bits) for h in range(4)])


def shift_x(a, step):
    return lax.ppermute(a, "mp", [(m, (m + step) % 4) for m in range(4)])


def dot(a, b):
    return jnp.dot(a, b, preferred_element_type=F32)


OFFSETS = (0, -1, 1, -2, 2, -3, 3, 4)


class Loader:
    def __init__(self, coord, states, a_v, w_v, sems):
        self.z, self.yl = coord[0], coord[1]
        self.states, self.a_v, self.w_v, self.sems = states, a_v, w_v, sems
        self.count = 0
        self.slots = []

    def copy(self, src, dst):
        made = pltpu.make_async_copy(src, dst, self.sems.at[self.count])
        self.count += 1
        made.start()
        return made

    def load(self, offset, y_parts, y_rows, own, crossed):
        slot, w_v = len(self.slots), self.w_v
        depth, z_cols = w_v.shape[2], w_v.shape[3] // 5
        y_cols = 3 * z_cols
        owner = (self.z + offset + 8) & 7
        first = pl.multiple_of(owner * 2 * depth, 128)
        made = [self.copy(self.states.at[:, pl.ds(first, 2 * depth)], self.a_v.at[slot])]
        for i, ref in enumerate(y_parts):
            side = i if y_rows is not None else (self.yl if i == 0 else 1 - self.yl)
            src = ref.at[pl.ds(y_rows[i] if y_rows is not None else 0, depth), pl.ds(0, y_cols)]
            made.append(self.copy(src, w_v.at[slot, side, :, pl.ds(0, y_cols)]))
        for fold in (0, 1):
            cols = pl.ds(y_cols + fold * z_cols, z_cols)
            for (ref, row, col), side in ((own, self.yl), (crossed, 1 - self.yl)):
                src = ref.at[pl.ds(row + fold * depth, depth), pl.ds(col, z_cols)]
                made.append(self.copy(src, w_v.at[slot, side, :, cols]))
        self.slots.append(made)

    def term(self, slot):
        for made in self.slots[slot]:
            made.wait()
        a, w = self.a_v[slot], self.w_v[slot]
        return dot(a, w.reshape(w.shape[0] * w.shape[1], w.shape[2]))


def near_kernel(coord, states, pair_y, z0, z1a, z1b, m1a, m1b, m2a, m2b, c1, c2, acc, a_v, w_v, sems):
    depth, y_cols = w_v.shape[2], pair_y.shape[1]
    loader = Loader(coord, states, a_v, w_v, sems)
    pieces = (
        (pair_y, (z0, 0, 0), (c1, 0)),
        (m1a, (z1a, 0, 0), (c1, 2)),
        (m1b, (z1b, 0, 0), (c1, 4)),
        (m2a, (m1a, 0, y_cols), (c2, 0)),
        (m2b, (m1b, 0, y_cols), (c2, 2)),
    )
    for offset, (y_ref, own, (crossed, place)) in zip(OFFSETS, pieces):
        loader.load(
            offset, (y_ref, y_ref), (0, depth), own, (crossed, place * depth, 0)
        )
    acc[...] = loader.term(0)
    for slot in range(1, 5):
        acc[...] += loader.term(slot)


BLOCK = 384


HEADS = 12
NT = (((1,), (1,)), ((), ()))
TN = (((0,), (0,)), ((), ()))


def place_of(i, of_query, of_other):
    query = i < 4
    block = jnp.where(query, i + i // 3, 3)
    first = jnp.where(query, 0, (i - 4) * of_other)
    return block, first, jnp.where(query, 128, of_other), query


def only(cols, first, width):
    lane = lax.broadcasted_iota(jnp.int32, cols.shape, 1)
    mine = (lane >= first) & (lane < first + width)
    return jnp.where(mine, cols.astype(F32), 0.0).astype(BF)


def scale_of(query, widths):
    scales = [1.0 / (math.sqrt(w) * math.log(2.0)) for w in widths]
    return jnp.where(query, scales[0], scales[1])


def finish_kernel(
    widths, coord, before, student_ref, select_ref, states, m2a, m2b, m3a, m3b, c3, y4, x4, d4,
    grads_out, ordered_out, a_v, w_v, t_v, g_v, o_v, sg_v, turned_v, sems,
):
    depth, y_cols = y4.shape
    t_widths, s_widths = widths
    head, x, length = coord[2], coord[3], coord[4]
    rows = t_v.shape[0]
    loader = Loader(coord, states, a_v, w_v, sems)
    loader.load(-3, (m3a, m3a), (0, depth), (m2a, 0, y_cols), (c3, 0, 0))
    loader.load(3, (m3b, m3b), (0, depth), (m2b, 0, y_cols), (c3, 2 * depth, 0))
    loader.load(4, (y4, x4), None, (m3a, 0, y_cols), (d4, 0, 0))

    t_v[...] = (before[...] + loader.term(0) + loader.term(1) + loader.term(2)).astype(BF)
    valid_keys = lax.broadcasted_iota(jnp.int32, (1, rows), 1) < length
    o_v[...] = jnp.zeros_like(o_v)
    turned_v[...] = jnp.zeros_like(turned_v)

    def one_head(i, kl):
        block, t_first, t_width, query = place_of(i, *t_widths)
        _, s_first, s_width, _ = place_of(i, *s_widths)
        scale, s_scale = scale_of(query, t_widths), scale_of(query, s_widths)
        lanes = pl.ds(pl.multiple_of(block * 128, 128), 128)
        teacher = t_v[:, lanes]
        mine = only(teacher, t_first, t_width)
        student = student_ref[:, lanes]
        s_mine = only(student, s_first, s_width)
        for start in range(0, rows, BLOCK):
            part = slice(start, start + BLOCK)
            scores = lax.dot_general(mine[part], teacher, NT, preferred_element_type=F32)
            scores = jnp.where(valid_keys, scores * scale, MASK_VALUE)
            top = jnp.max(scores, axis=-1, keepdims=True)
            weight = jnp.exp2(scores - top)
            total = jnp.sum(weight, axis=-1, keepdims=True)
            other = lax.dot_general(s_mine[part], student, NT, preferred_element_type=F32)
            other = jnp.where(valid_keys, other * s_scale, MASK_VALUE)
            s_top = jnp.max(other, axis=-1, keepdims=True)
            s_weight = jnp.exp2(other - s_top)
            s_total = jnp.sum(s_weight, axis=-1, keepdims=True)
            cross = jnp.sum(weight * (scores - other), axis=-1, keepdims=True)
            row_kl = cross / total - (top + jnp.log2(total)) + (s_top + jnp.log2(s_total))
            valid = lax.broadcasted_iota(jnp.int32, (BLOCK, 1), 0) + start < length
            kl = kl + jnp.sum(jnp.where(valid, row_kl, 0.0), axis=0, keepdims=True)
            gain = jnp.where(valid, LOSS_SCALE / total, 0.0)
            s_gain = jnp.where(valid, LOSS_SCALE / s_total, 0.0)
            sg_v[part, :] = (s_weight * s_gain - weight * gain).astype(BF)
        sg = sg_v[...]
        o_v[:, lanes] += dot(sg, s_mine)
        turned_v[block] += lax.dot_general(s_mine, sg, TN, preferred_element_type=F32)
        return kl

    kl = lax.fori_loop(0, HEADS, one_head, jnp.zeros((1, 1), F32))
    over = [1.0 / math.sqrt(w) for w in s_widths]
    for block in range(5):
        lanes = slice(block * 128, block * 128 + 128)
        both = o_v[:, lanes] + turned_v[block].T
        g_v[:, lanes] = (both * over[block == 3]).astype(BF)
    loss = kl * math.log(2.0) / (3.0 * R * length.astype(F32))
    packed = dot(g_v[...], select_ref[...])
    lane = lax.broadcasted_iota(jnp.int32, packed.shape, 1)
    packed = jnp.where(lane == s_widths[0] * 4 + s_widths[1] * 8, loss, packed)
    o_v[:, pl.ds(0, packed.shape[1])] = packed
    grads_out[...] = packed.astype(BF)
    piece = rows // 16
    for place in range(8):
        core_bit, x_step = place // 4, place % 4
        halves = []
        for yh_bit in (0, 1):
            owner = (head ^ (2 * yh_bit + core_bit)) * 4 + ((x + x_step) & 3)
            own_rows = pl.ds(pl.multiple_of(owner * piece, 8), piece)
            halves.append(o_v[own_rows, pl.ds(0, packed.shape[1])])
        ordered_out[pl.ds(place * 2 * piece, 2 * piece), :] = jnp.concatenate(halves, 0).astype(BF)


ANY = pl.BlockSpec(memory_space=pl.ANY)
WHOLE = pl.BlockSpec(memory_space=pltpu.VMEM)
SCALARS = pl.BlockSpec(memory_space=pltpu.SMEM)


def call(kernel, name, args, specs, outs, slots, rows, depth, cols, scratch=(), more_flops=0):
    return pl.pallas_call(
        kernel,
        out_shape=outs,
        in_specs=specs,
        out_specs=jax.tree.map(lambda _: WHOLE, outs),
        scratch_shapes=[
            pltpu.VMEM((slots, rows, 2 * depth), BF),
            pltpu.VMEM((slots, 2, depth, cols), BF),
            *scratch,
            pltpu.SemaphoreType.DMA((7 * slots,)),
        ],
        compiler_params=pltpu.CompilerParams(vmem_limit_bytes=28 * 1024 * 1024),
        cost_estimate=pl.CostEstimate(
            flops=slots * 4 * rows * depth * cols + more_flops,
            bytes_accessed=slots * 4 * depth * (rows + cols),
            transcendentals=0,
        ),
        name=name,
    )(*args)


def per_device(
    teacher_states,
    teacher_wq,
    teacher_wk,
    teacher_wv,
    student_states,
    student_wq,
    student_wk,
    student_wv,
    lengths,
):
    d = lax.axis_index("dp")
    head = lax.axis_index("head")
    x = lax.axis_index("mp")
    z, yl = d // 2, d % 2
    rows = student_states.shape[0]
    depth = teacher_wq.shape[0]
    q_width = teacher_wq.shape[1] // 4

    depth = teacher_wq.shape[0]
    part_y = teacher_wq[:, q_width:]
    z0 = jnp.concatenate(
        [jnp.concatenate([teacher_wk, teacher_wv], axis=1), teacher_wq[:, :q_width]], axis=0
    )
    y_cols = part_y.shape[1]
    cat, fence = jnp.concatenate, lax.optimization_barrier

    sq, sk = student_wq.shape[1], student_wk.shape[1]
    q_head, width = sq // 4, student_states.shape[1]
    length = lengths[0]
    states = lax.all_gather(teacher_states, ("head", "mp"), axis=1, tiled=True)

    other_y = swap_dp(teacher_wq, 1)[:, q_width:]
    z1a, z1b = shift_z(z0, 1), shift_z(z0, -1)
    y4 = shift_z(part_y, 4)
    other_y, z1a, z1b = fence((other_y, z1a, z1b))
    pair_y = jnp.where(yl == 0, cat([part_y, other_y], 0), cat([other_y, part_y], 0))
    m1a = shift_z(cat([pair_y, z1a], 1), 1)
    m1b = shift_z(cat([pair_y, z1b], 1), -1)
    z0c, z1ac, z1bc, y4 = fence((z0, z1a, z1b, y4))
    c1 = swap_dp(cat([z0c, z1ac, z1bc], 0), 1)
    student_w = cat([student_wq, student_wk, student_wv], 1)
    wide_w = jnp.pad(student_w, ((0, 128), (0, 96)))
    wide_w = wide_w.at[width, sq + 2 * sk].set(1.0)
    m1a, m1b, c1, wide_w, y4 = fence((m1a, m1b, c1, wide_w, y4))
    m2a, m2b = shift_z(m1a, 1), shift_z(m1b, -1)
    c2 = swap_dp(cat([m1a[:, y_cols:], m1b[:, y_cols:]], 0), 1)
    x4 = swap_dp(y4, 1)
    unit = width // 16
    columns = []
    for e in range(4):
        blocks = []
        for r in range(4):
            owner = ((d ^ e) + 4 * r) % 16
            blocks.append(lax.dynamic_slice(student_states, (0, owner * unit), (rows, unit)))
        columns.append(cat(blocks, 1))
    m2a, m2b, c2, x4, *columns = fence((m2a, m2b, c2, x4, *columns))
    m3a, m3b = shift_z(m2a, 1), shift_z(m2b[:, :y_cols], -1)
    d4 = lax.ppermute(m2b[:, y_cols:], "dp", [(i, ((i - 2) % 16) ^ 1) for i in range(16)])
    c3 = swap_dp(cat([m2a[:, y_cols:], m2b[:, y_cols:]], 0), 1)
    padded = [student_wq[:, i * q_head : (i + 1) * q_head] for i in (1, 2, 3, 0)]
    padded.insert(3, cat([student_wk, student_wv], 1))
    padded = cat([jnp.pad(part, ((0, 0), (0, 128 - part.shape[1]))) for part in padded], 1)
    student = dot(student_states, padded).astype(BF)
    coord = jnp.stack([z, yl, head, x, length]).astype(jnp.int32)
    cols = y_cols + 2 * q_width
    acc_shape = jax.ShapeDtypeStruct((rows, cols), F32)
    near = call(
        near_kernel, "near",
        (coord, states, pair_y, z0, z1a, z1b, m1a, m1b, m2a, m2b, c1, c2),
        [SCALARS] + [ANY] * 11, acc_shape, 5, rows, depth, cols,
    )
    select = np.zeros((cols, 384), np.float32)
    for i, block in enumerate((4, 0, 1, 2)):
        for j in range(q_head):
            select[block * 128 + j, i * q_head + j] = 1.0
    for j in range(2 * sk):
        select[3 * 128 + j, sq + j] = 1.0
    widths = ((q_width, teacher_wk.shape[1] // 4), (q_head, sk // 4))
    out = jax.ShapeDtypeStruct((rows, 384), BF)
    far_parts = (states, m2a, m2b, m3a, m3b, c3, y4, x4, d4)
    with_loss, ordered = call(
        functools.partial(finish_kernel, widths), "finish",
        (coord, near, student, jnp.asarray(select, BF), *far_parts),
        [SCALARS, WHOLE, WHOLE, WHOLE] + [ANY] * len(far_parts), (out, out), 3, rows, depth, cols,
        scratch=(
            pltpu.VMEM((rows, cols), BF),
            pltpu.VMEM((rows, cols), BF),
            pltpu.VMEM((rows, cols), F32),
            pltpu.VMEM((rows, rows), BF),
            pltpu.VMEM((5, 128, rows), F32),
        ),
        more_flops=12 * 8 * rows * rows * 128,
    )
    grads = with_loss[:, : sq + 2 * sk]
    half = rows // 2

    piece = rows // 16

    def state_term(part):
        return lax.dot_general(
            part, wide_w, (((1,), (1,)), ((), ())), preferred_element_type=F32
        ).astype(BF)

    def weight_term(e, grads):
        return lax.dot_general(
            grads, columns[e], (((0,), (0,)), ((), ())), preferred_element_type=F32
        )

    terms = [weight_term(e, grads).astype(BF) for e in (3, 2, 1)]
    *terms, ordered = fence((*terms, ordered))
    received = [swap_dp(term, e) for term, e in zip(terms, (3, 2, 1))]
    from_core = swap_head(state_term(ordered[half:]), 1)
    summed = (state_term(ordered[:half]).astype(F32) + from_core.astype(F32)).astype(BF)
    summed, grads = fence((summed, grads))
    slab = half // 4
    sent = [shift_x(summed[step * slab : (step + 1) * slab], step) for step in (2, 1, 3)]
    first_square = weight_term(0, grads)
    *received, first_square = fence((*received, *sent, first_square))
    received, sent = received[:3], received[3:]
    square = first_square
    for part in received:
        square = square + part.astype(F32)
    chunks = [square[:, r * unit : (r + 1) * unit] for r in range(4)]
    total = summed[:slab].astype(F32)
    for part in sent:
        total = total + part.astype(F32)
    last = swap_head(total[piece:].astype(BF), 2)
    weight_grad = chunks[0]
    for r in (2, 1, 3):
        moved = lax.ppermute(
            chunks[r].astype(BF), "dp", [(i, (i + 4 * r) % 16) for i in range(16)]
        )
        weight_grad = weight_grad + moved.astype(F32)
    weight_grad = weight_grad.T
    total = total[:piece] + last.astype(F32)
    grad_states = total[:, :width]
    seq_loss = total[0, width : width + 1]

    return (
        weight_grad[:, :sq],
        weight_grad[:, sq : sq + sk],
        weight_grad[:, sq + sk :],
        grad_states,
        seq_loss,
    )


def solution(mesh):
    in_specs = (
        P("dp", ("head", "mp")),
        P("dp", ("head", "mp")),
        P("dp", ("head", "mp")),
        P("dp", ("head", "mp")),
        P("dp", None),
        P(None, ("head", "mp")),
        P(None, ("head", "mp")),
        P(None, ("head", "mp")),
        P("dp"),
    )
    out_specs = (
        P("dp", ("head", "mp")),
        P("dp", ("head", "mp")),
        P("dp", ("head", "mp")),
        P(("dp", "head", "mp"), None),
        P("dp"),
    )
    return jax.shard_map(
        per_device, mesh=mesh, in_specs=in_specs, out_specs=out_specs, check_vma=False
    )
```

```python
import functools
import math

import jax
import jax.numpy as jnp
import numpy as np
from jax import lax
from jax.experimental import pallas as pl
from jax.experimental.pallas import tpu as pltpu
from jax.sharding import PartitionSpec as P

R = 64

LOSS_SCALE = 16.0
MASK_VALUE = -1000000000.0

BF = jnp.bfloat16
F32 = jnp.float32


def shift_z(a, step):
    return lax.ppermute(a, "dp", [(d, (d + 2 * step) % 16) for d in range(16)])


def swap_dp(a, bits):
    return lax.ppermute(a, "dp", [(d, d ^ bits) for d in range(16)])


def swap_head(a, bits):
    return lax.ppermute(a, "head", [(h, h ^ bits) for h in range(4)])


def shift_x(a, step):
    return lax.ppermute(a, "mp", [(m, (m + step) % 4) for m in range(4)])


def dot(a, b):
    return jnp.dot(a, b, preferred_element_type=F32)


OFFSETS = (0, -1, 1, -2, 2, -3, 3, 4)


class Loader:
    def __init__(self, coord, states, a_v, w_v, sems):
        self.z, self.yl = coord[0], coord[1]
        self.states, self.a_v, self.w_v, self.sems = states, a_v, w_v, sems
        self.count = 0
        self.slots = []

    def copy(self, src, dst):
        made = pltpu.make_async_copy(src, dst, self.sems.at[self.count])
        self.count += 1
        made.start()
        return made

    def load(self, offset, own, other, crossed):
        slot, w_v = len(self.slots), self.w_v
        cols = w_v.shape[3]
        y_cols = cols // 5 * 3
        owner = (self.z + offset + 8) & 7
        first = pl.multiple_of(owner * 2 * w_v.shape[2], 128)
        src = self.states.at[:, pl.ds(first, 2 * w_v.shape[2])]
        made = [self.copy(src, self.a_v.at[slot])]
        for parts, side, lane, wide in (
            (own, self.yl, 0, cols),
            (other, 1 - self.yl, 0, y_cols),
            (crossed, 1 - self.yl, y_cols, cols - y_cols),
        ):
            start = 0
            for ref, row, count in parts:
                dst = w_v.at[slot, side, pl.ds(start, count), pl.ds(lane, wide)]
                made.append(self.copy(ref.at[pl.ds(row, count), :], dst))
                start += count
        self.slots.append(made)

    def term(self, slot):
        for made in self.slots[slot]:
            made.wait()
        a, w = self.a_v[slot], self.w_v[slot]
        return dot(a, w.reshape(w.shape[0] * w.shape[1], w.shape[2]))


def near_kernel(
    coord, states, w0, o1a, o1b, o2a, o2b, x0, y1a, y1b, y2a, y2b, c0, c1, c2, acc, a_v, w_v, sems
):
    depth = w_v.shape[2]
    loader = Loader(coord, states, a_v, w_v, sems)
    pieces = (
        (w0, x0, (c0, 0)), (o1a, y1a, (c1, 0)), (o1b, y1b, (c1, 1)), (o2a, y2a, (c2, 0)),
        (o2b, y2b, (c2, 1)),
    )
    for offset, (own, other, (crossed, place)) in zip(OFFSETS, pieces):
        loader.load(
            offset, ((own, 0, depth),), ((other, 0, depth),), ((crossed, place * depth, depth),)
        )
    acc[...] = loader.term(0)
    for slot in range(1, 5):
        acc[...] += loader.term(slot)


def far_kernel(coord, before, states, o3a, o3b, y3a, y3b, c3a, c3b, acc, a_v, w_v, sems):
    depth = w_v.shape[2]
    loader = Loader(coord, states, a_v, w_v, sems)
    loader.load(-3, ((o3a, 0, depth),), ((y3a, 0, depth),), ((c3a, 0, depth),))
    loader.load(3, ((o3b, 0, depth),), ((y3b, 0, depth),), ((c3b, 0, depth),))
    acc[...] = before[...] + loader.term(0)
    acc[...] += loader.term(1)


BLOCK = 384


HEADS = 12
NT = (((1,), (1,)), ((), ()))
TN = (((0,), (0,)), ((), ()))


def place_of(i, of_query, of_other):
    query = i < 4
    block = jnp.where(query, i + i // 3, 3)
    first = jnp.where(query, 0, (i - 4) * of_other)
    return block, first, jnp.where(query, 128, of_other), query


def only(cols, first, width):
    lane = lax.broadcasted_iota(jnp.int32, cols.shape, 1)
    mine = (lane >= first) & (lane < first + width)
    return jnp.where(mine, cols.astype(F32), 0.0).astype(BF)


def scale_of(query, widths):
    scales = [1.0 / (math.sqrt(w) * math.log(2.0)) for w in widths]
    return jnp.where(query, scales[0], scales[1])


def finish_kernel(
    widths, coord, before, student_ref, select_ref, states, o4a, o4b, y4a, y4b, c4,
    grads_out, ordered_out, a_v, w_v, t_v, g_v, o_v, sg_v, turned_v, sems,
):
    half = y4a.shape[0]
    t_widths, s_widths = widths
    head, x, length = coord[2], coord[3], coord[4]
    rows = t_v.shape[0]
    loader = Loader(coord, states, a_v, w_v, sems)
    loader.load(
        4, ((o4a, 0, half), (o4b, 0, half)), ((y4a, 0, half), (y4b, 0, half)),
        ((c4, 0, 2 * half),),
    )

    t_v[...] = (before[...] + loader.term(0)).astype(BF)
    valid_keys = lax.broadcasted_iota(jnp.int32, (1, rows), 1) < length
    o_v[...] = jnp.zeros_like(o_v)
    turned_v[...] = jnp.zeros_like(turned_v)

    def one_head(i, kl):
        block, t_first, t_width, query = place_of(i, *t_widths)
        _, s_first, s_width, _ = place_of(i, *s_widths)
        scale, s_scale = scale_of(query, t_widths), scale_of(query, s_widths)
        lanes = pl.ds(pl.multiple_of(block * 128, 128), 128)
        teacher = t_v[:, lanes]
        mine = only(teacher, t_first, t_width)
        student = student_ref[:, lanes]
        s_mine = only(student, s_first, s_width)
        for start in range(0, rows, BLOCK):
            part = slice(start, start + BLOCK)
            scores = lax.dot_general(mine[part], teacher, NT, preferred_element_type=F32)
            scores = jnp.where(valid_keys, scores * scale, MASK_VALUE)
            top = jnp.max(scores, axis=-1, keepdims=True)
            weight = jnp.exp2(scores - top)
            total = jnp.sum(weight, axis=-1, keepdims=True)
            other = lax.dot_general(s_mine[part], student, NT, preferred_element_type=F32)
            other = jnp.where(valid_keys, other * s_scale, MASK_VALUE)
            s_top = jnp.max(other, axis=-1, keepdims=True)
            s_weight = jnp.exp2(other - s_top)
            s_total = jnp.sum(s_weight, axis=-1, keepdims=True)
            cross = jnp.sum(weight * (scores - other), axis=-1, keepdims=True)
            row_kl = cross / total - (top + jnp.log2(total)) + (s_top + jnp.log2(s_total))
            valid = lax.broadcasted_iota(jnp.int32, (BLOCK, 1), 0) + start < length
            kl = kl + jnp.sum(jnp.where(valid, row_kl, 0.0), axis=0, keepdims=True)
            gain = jnp.where(valid, LOSS_SCALE / total, 0.0)
            s_gain = jnp.where(valid, LOSS_SCALE / s_total, 0.0)
            sg_v[part, :] = (s_weight * s_gain - weight * gain).astype(BF)
        sg = sg_v[...]
        o_v[:, lanes] += dot(sg, s_mine)
        turned_v[block] += lax.dot_general(s_mine, sg, TN, preferred_element_type=F32)
        return kl

    kl = lax.fori_loop(0, HEADS, one_head, jnp.zeros((1, 1), F32))
    over = [1.0 / math.sqrt(w) for w in s_widths]
    for block in range(5):
        lanes = slice(block * 128, block * 128 + 128)
        both = o_v[:, lanes] + turned_v[block].T
        g_v[:, lanes] = (both * over[block == 3]).astype(BF)
    loss = kl * math.log(2.0) / (3.0 * R * length.astype(F32))
    packed = dot(g_v[...], select_ref[...])
    lane = lax.broadcasted_iota(jnp.int32, packed.shape, 1)
    packed = jnp.where(lane == s_widths[0] * 4 + s_widths[1] * 8, loss, packed)
    o_v[:, pl.ds(0, packed.shape[1])] = packed
    grads_out[...] = packed.astype(BF)
    piece = rows // 16
    for place in range(8):
        core_bit, x_step = place // 4, place % 4
        halves = []
        for yh_bit in (0, 1):
            owner = (head ^ (2 * yh_bit + core_bit)) * 4 + ((x + x_step) & 3)
            own_rows = pl.ds(pl.multiple_of(owner * piece, 8), piece)
            halves.append(o_v[own_rows, pl.ds(0, packed.shape[1])])
        ordered_out[pl.ds(place * 2 * piece, 2 * piece), :] = jnp.concatenate(halves, 0).astype(BF)


ANY = pl.BlockSpec(memory_space=pl.ANY)
WHOLE = pl.BlockSpec(memory_space=pltpu.VMEM)
SCALARS = pl.BlockSpec(memory_space=pltpu.SMEM)


def call(kernel, name, args, specs, outs, slots, rows, depth, cols, scratch=(), more_flops=0):
    return pl.pallas_call(
        kernel,
        out_shape=outs,
        in_specs=specs,
        out_specs=jax.tree.map(lambda _: WHOLE, outs),
        scratch_shapes=[
            pltpu.VMEM((slots, rows, 2 * depth), BF),
            pltpu.VMEM((slots, 2, depth, cols), BF),
            *scratch,
            pltpu.SemaphoreType.DMA((7 * slots,)),
        ],
        compiler_params=pltpu.CompilerParams(vmem_limit_bytes=28 * 1024 * 1024),
        cost_estimate=pl.CostEstimate(
            flops=slots * 4 * rows * depth * cols + more_flops,
            bytes_accessed=slots * 4 * depth * (rows + cols),
            transcendentals=0,
        ),
        name=name,
    )(*args)


def per_device(
    teacher_states,
    teacher_wq,
    teacher_wk,
    teacher_wv,
    student_states,
    student_wq,
    student_wk,
    student_wv,
    lengths,
):
    d = lax.axis_index("dp")
    head = lax.axis_index("head")
    x = lax.axis_index("mp")
    z, yl = d // 2, d % 2
    rows = student_states.shape[0]
    depth = teacher_wq.shape[0]
    q_width = teacher_wq.shape[1] // 4

    depth = teacher_wq.shape[0]
    part_y = teacher_wq[:, q_width:]
    z0 = jnp.concatenate([teacher_wk, teacher_wv, teacher_wq[:, :q_width]], axis=1)
    w0 = jnp.concatenate([part_y, z0], axis=1)
    y_cols = part_y.shape[1]
    cat, fence = jnp.concatenate, lax.optimization_barrier
    sq, sk = student_wq.shape[1], student_wk.shape[1]
    q_head, width = sq // 4, student_states.shape[1]
    length = lengths[0]
    states = lax.all_gather(teacher_states, ("head", "mp"), axis=1, tiled=True)

    o1a, o1b = shift_z(w0, 1), shift_z(w0, -1)
    x0, c0 = swap_dp(part_y, 1), swap_dp(z0, 1)
    o1a, o1b, x0, c0 = fence((o1a, o1b, x0, c0))
    o2a, o2b = shift_z(o1a, 1), shift_z(o1b, -1)
    y1a, y1b = shift_z(x0, 1), shift_z(x0, -1)
    c1 = swap_dp(cat([o1a[:, y_cols:], o1b[:, y_cols:]], 0), 1)
    student_w = cat([student_wq, student_wk, student_wv], 1)
    wide_w = jnp.pad(student_w, ((0, 128), (0, 96)))
    wide_w = wide_w.at[width, sq + 2 * sk].set(1.0)
    o2a, o2b, y1a, y1b, c1, wide_w = fence((o2a, o2b, y1a, y1b, c1, wide_w))
    o3a, o3b = shift_z(o2a, 1), shift_z(o2b, -1)
    y2a, y2b = shift_z(y1a, 1), shift_z(y1b, -1)
    c2 = swap_dp(cat([o2a[:, y_cols:], o2b[:, y_cols:]], 0), 1)
    unit = width // 16
    columns = []
    for e in range(4):
        blocks = []
        for r in range(4):
            owner = ((d ^ e) + 4 * r) % 16
            blocks.append(lax.dynamic_slice(student_states, (0, owner * unit), (rows, unit)))
        columns.append(cat(blocks, 1))
    padded = [student_wq[:, i * q_head : (i + 1) * q_head] for i in (1, 2, 3, 0)]
    padded.insert(3, cat([student_wk, student_wv], 1))
    padded = cat([jnp.pad(part, ((0, 0), (0, 128 - part.shape[1]))) for part in padded], 1)
    student = dot(student_states, padded).astype(BF)
    o3a, o3b, y2a, y2b, c2, student, *columns = fence(
        (o3a, o3b, y2a, y2b, c2, student, *columns)
    )
    part = depth // 2
    y3a, y3b = shift_z(y2a, 1), shift_z(y2b, -1)
    o4a, o4b = shift_z(o3a[:part], 1), shift_z(o3b[part:], -1)
    c3a, c3b = swap_dp(o3a[:, y_cols:], 1), swap_dp(o3b[:, y_cols:], 1)
    coord = jnp.stack([z, yl, head, x, length]).astype(jnp.int32)
    cols = y_cols + 2 * q_width
    acc_shape = jax.ShapeDtypeStruct((rows, cols), F32)
    near_parts = (states, w0, o1a, o1b, o2a, o2b, x0, y1a, y1b, y2a, y2b, c0, c1, c2)
    near = call(
        near_kernel, "near", (coord, *near_parts), [SCALARS] + [ANY] * len(near_parts),
        acc_shape, 5, rows, depth, cols,
    )
    y3a, y3b, o4a, o4b, c3a, c3b = fence((y3a, y3b, o4a, o4b, c3a, c3b))
    y4a, y4b = shift_z(y3a[:part], 1), shift_z(y3b[part:], -1)
    c4 = swap_dp(cat([o4a[:, y_cols:], o4b[:, y_cols:]], 0), 1)
    acc = call(
        far_kernel, "far", (coord, near, states, o3a, o3b, y3a, y3b, c3a, c3b),
        [SCALARS, WHOLE] + [ANY] * 7, acc_shape, 2, rows, depth, cols,
    )

    select = np.zeros((cols, 384), np.float32)
    for i, block in enumerate((4, 0, 1, 2)):
        for j in range(q_head):
            select[block * 128 + j, i * q_head + j] = 1.0
    for j in range(2 * sk):
        select[3 * 128 + j, sq + j] = 1.0
    widths = ((q_width, teacher_wk.shape[1] // 4), (q_head, sk // 4))
    out = jax.ShapeDtypeStruct((rows, 384), BF)
    with_loss, ordered = call(
        functools.partial(finish_kernel, widths), "finish",
        (coord, acc, student, jnp.asarray(select, BF), states, o4a, o4b, y4a, y4b, c4),
        [SCALARS, WHOLE, WHOLE, WHOLE] + [ANY] * 6, (out, out), 1, rows, depth, cols,
        scratch=(
            pltpu.VMEM((rows, cols), BF),
            pltpu.VMEM((rows, cols), BF),
            pltpu.VMEM((rows, cols), F32),
            pltpu.VMEM((rows, rows), BF),
            pltpu.VMEM((5, 128, rows), F32),
        ),
        more_flops=12 * 8 * rows * rows * 128,
    )
    grads = with_loss[:, : sq + 2 * sk]
    half = rows // 2

    piece = rows // 16

    def state_term(part):
        return lax.dot_general(
            part, wide_w, (((1,), (1,)), ((), ())), preferred_element_type=F32
        ).astype(BF)

    def weight_term(e, grads):
        return lax.dot_general(
            grads, columns[e], (((0,), (0,)), ((), ())), preferred_element_type=F32
        )

    terms = [weight_term(e, grads).astype(BF) for e in (3, 2, 1)]
    *terms, ordered = fence((*terms, ordered))
    received = [swap_dp(term, e) for term, e in zip(terms, (3, 2, 1))]
    from_core = swap_head(state_term(ordered[half:]), 1)
    summed = (state_term(ordered[:half]).astype(F32) + from_core.astype(F32)).astype(BF)
    summed, grads = fence((summed, grads))
    slab = half // 4
    sent = [shift_x(summed[step * slab : (step + 1) * slab], step) for step in (2, 1, 3)]
    first_square = weight_term(0, grads)
    *received, first_square = fence((*received, *sent, first_square))
    received, sent = received[:3], received[3:]
    square = first_square
    for part in received:
        square = square + part.astype(F32)
    chunks = [square[:, r * unit : (r + 1) * unit] for r in range(4)]
    total = summed[:slab].astype(F32)
    for part in sent:
        total = total + part.astype(F32)
    last = swap_head(total[piece:].astype(BF), 2)
    weight_grad = chunks[0]
    for r in (2, 1, 3):
        moved = lax.ppermute(
            chunks[r].astype(BF), "dp", [(i, (i + 4 * r) % 16) for i in range(16)]
        )
        weight_grad = weight_grad + moved.astype(F32)
    weight_grad = weight_grad.T
    total = total[:piece] + last.astype(F32)
    grad_states = total[:, :width]
    seq_loss = total[0, width : width + 1]

    return (
        weight_grad[:, :sq],
        weight_grad[:, sq : sq + sk],
        weight_grad[:, sq + sk :],
        grad_states,
        seq_loss,
    )


def solution(mesh):
    in_specs = (
        P("dp", ("head", "mp")),
        P("dp", ("head", "mp")),
        P("dp", ("head", "mp")),
        P("dp", ("head", "mp")),
        P("dp", None),
        P(None, ("head", "mp")),
        P(None, ("head", "mp")),
        P(None, ("head", "mp")),
        P("dp"),
    )
    out_specs = (
        P("dp", ("head", "mp")),
        P("dp", ("head", "mp")),
        P("dp", ("head", "mp")),
        P(("dp", "head", "mp"), None),
        P("dp"),
    )
    return jax.shard_map(
        per_device, mesh=mesh, in_specs=in_specs, out_specs=out_specs, check_vma=False
    )
```

```python
import functools
import math

import jax
import jax.numpy as jnp
import numpy as np
from jax import lax
from jax.experimental import pallas as pl
from jax.experimental.pallas import tpu as pltpu
from jax.sharding import PartitionSpec as P

R = 64

LOSS_SCALE = 16.0
MASK_VALUE = -1000000000.0

BF = jnp.bfloat16
F32 = jnp.float32


def shift_z(a, step):
    return lax.ppermute(a, "dp", [(d, (d + 2 * step) % 16) for d in range(16)])


def swap_dp(a, bits):
    return lax.ppermute(a, "dp", [(d, d ^ bits) for d in range(16)])


def swap_head(a, bits):
    return lax.ppermute(a, "head", [(h, h ^ bits) for h in range(4)])


def shift_x(a, step):
    return lax.ppermute(a, "mp", [(m, (m + step) % 4) for m in range(4)])


def dot(a, b):
    return jnp.dot(a, b, preferred_element_type=F32)


OFFSETS = (0, -1, 1, -2, 2, -3, 3, 4)


class Loader:
    def __init__(self, coord, states, a_v, w_v, sems):
        self.z, self.yl = coord[0], coord[1]
        self.states, self.a_v, self.w_v, self.sems = states, a_v, w_v, sems
        self.count = 0
        self.slots = []

    def copy(self, src, dst):
        made = pltpu.make_async_copy(src, dst, self.sems.at[self.count])
        self.count += 1
        made.start()
        return made

    def load(self, offset, y_parts, own, crossed):
        slot, w_v = len(self.slots), self.w_v
        depth, z_cols = w_v.shape[2], w_v.shape[3] // 5
        y_cols = 3 * z_cols
        owner = (self.z + offset + 8) & 7
        first = pl.multiple_of(owner * 2 * depth, 128)
        made = [self.copy(self.states.at[:, pl.ds(first, 2 * depth)], self.a_v.at[slot])]
        for side, (ref, row) in enumerate(y_parts):
            src = ref.at[pl.ds(row, depth), pl.ds(0, y_cols)]
            made.append(self.copy(src, w_v.at[slot, side, :, pl.ds(0, y_cols)]))
        for fold in (0, 1):
            cols = pl.ds(y_cols + fold * z_cols, z_cols)
            for (ref, row, col), side in ((own, self.yl), (crossed, 1 - self.yl)):
                src = ref.at[pl.ds(row + fold * depth, depth), pl.ds(col, z_cols)]
                made.append(self.copy(src, w_v.at[slot, side, :, cols]))
        self.slots.append(made)

    def term(self, slot):
        for made in self.slots[slot]:
            made.wait()
        a, w = self.a_v[slot], self.w_v[slot]
        return dot(a, w.reshape(w.shape[0] * w.shape[1], w.shape[2]))


def near_kernel(coord, states, pair_y, z0, z1a, z1b, m1a, m1b, m2a, m2b, c1, c2, acc, a_v, w_v, sems):
    depth, y_cols = w_v.shape[2], pair_y.shape[1]
    loader = Loader(coord, states, a_v, w_v, sems)
    pieces = (
        (pair_y, (z0, 0, 0), (c1, 0)),
        (m1a, (z1a, 0, 0), (c1, 2)),
        (m1b, (z1b, 0, 0), (c1, 4)),
        (m2a, (m1a, 0, y_cols), (c2, 0)),
        (m2b, (m1b, 0, y_cols), (c2, 2)),
    )
    for offset, (y_ref, own, (crossed, place)) in zip(OFFSETS, pieces):
        loader.load(
            offset, ((y_ref, 0), (y_ref, depth)), own, (crossed, place * depth, 0)
        )
    acc[...] = loader.term(0)
    for slot in range(1, 5):
        acc[...] += loader.term(slot)


def far_kernel(coord, before, states, m2a, m2b, m3a, m3b, c3, acc, a_v, w_v, sems):
    depth, y_cols = w_v.shape[2], w_v.shape[3] // 5 * 3
    loader = Loader(coord, states, a_v, w_v, sems)
    loader.load(-3, ((m3a, 0), (m3a, depth)), (m2a, 0, y_cols), (c3, 0, 0))
    loader.load(3, ((m3b, 0), (m3b, depth)), (m2b, 0, y_cols), (c3, 2 * depth, 0))
    acc[...] = before[...] + loader.term(0)
    acc[...] += loader.term(1)


BLOCK = 384


HEADS = 12
NT = (((1,), (1,)), ((), ()))
TN = (((0,), (0,)), ((), ()))


def place_of(i, of_query, of_other):
    query = i < 4
    block = jnp.where(query, i + i // 3, 3)
    first = jnp.where(query, 0, (i - 4) * of_other)
    return block, first, jnp.where(query, 128, of_other), query


def only(cols, first, width):
    lane = lax.broadcasted_iota(jnp.int32, cols.shape, 1)
    mine = (lane >= first) & (lane < first + width)
    return jnp.where(mine, cols.astype(F32), 0.0).astype(BF)


def scale_of(query, widths):
    scales = [1.0 / (math.sqrt(w) * math.log(2.0)) for w in widths]
    return jnp.where(query, scales[0], scales[1])


def finish_kernel(
    widths, coord, before, student_ref, select_ref, states, m3a, f0, f1, c4,
    grads_out, ordered_out, a_v, w_v, t_v, g_v, o_v, sg_v, turned_v, sems,
):
    depth, y_cols = f0.shape
    t_widths, s_widths = widths
    head, x, length = coord[2], coord[3], coord[4]
    rows = t_v.shape[0]
    loader = Loader(coord, states, a_v, w_v, sems)
    loader.load(4, ((f0, 0), (f1, 0)), (m3a, 0, y_cols), (c4, 0, 0))

    t_v[...] = (before[...] + loader.term(0)).astype(BF)
    valid_keys = lax.broadcasted_iota(jnp.int32, (1, rows), 1) < length
    o_v[...] = jnp.zeros_like(o_v)
    turned_v[...] = jnp.zeros_like(turned_v)

    def one_head(i, kl):
        block, t_first, t_width, query = place_of(i, *t_widths)
        _, s_first, s_width, _ = place_of(i, *s_widths)
        scale, s_scale = scale_of(query, t_widths), scale_of(query, s_widths)
        lanes = pl.ds(pl.multiple_of(block * 128, 128), 128)
        teacher = t_v[:, lanes]
        mine = only(teacher, t_first, t_width)
        student = student_ref[:, lanes]
        s_mine = only(student, s_first, s_width)
        for start in range(0, rows, BLOCK):
            part = slice(start, start + BLOCK)
            scores = lax.dot_general(mine[part], teacher, NT, preferred_element_type=F32)
            scores = jnp.where(valid_keys, scores * scale, MASK_VALUE)
            top = jnp.max(scores, axis=-1, keepdims=True)
            weight = jnp.exp2(scores - top)
            total = jnp.sum(weight, axis=-1, keepdims=True)
            other = lax.dot_general(s_mine[part], student, NT, preferred_element_type=F32)
            other = jnp.where(valid_keys, other * s_scale, MASK_VALUE)
            s_top = jnp.max(other, axis=-1, keepdims=True)
            s_weight = jnp.exp2(other - s_top)
            s_total = jnp.sum(s_weight, axis=-1, keepdims=True)
            cross = jnp.sum(weight * (scores - other), axis=-1, keepdims=True)
            row_kl = cross / total - (top + jnp.log2(total)) + (s_top + jnp.log2(s_total))
            valid = lax.broadcasted_iota(jnp.int32, (BLOCK, 1), 0) + start < length
            kl = kl + jnp.sum(jnp.where(valid, row_kl, 0.0), axis=0, keepdims=True)
            gain = jnp.where(valid, LOSS_SCALE / total, 0.0)
            s_gain = jnp.where(valid, LOSS_SCALE / s_total, 0.0)
            sg_v[part, :] = (s_weight * s_gain - weight * gain).astype(BF)
        sg = sg_v[...]
        o_v[:, lanes] += dot(sg, s_mine)
        turned_v[block] += lax.dot_general(s_mine, sg, TN, preferred_element_type=F32)
        return kl

    kl = lax.fori_loop(0, HEADS, one_head, jnp.zeros((1, 1), F32))
    over = [1.0 / math.sqrt(w) for w in s_widths]
    for block in range(5):
        lanes = slice(block * 128, block * 128 + 128)
        both = o_v[:, lanes] + turned_v[block].T
        g_v[:, lanes] = (both * over[block == 3]).astype(BF)
    loss = kl * math.log(2.0) / (3.0 * R * length.astype(F32))
    packed = dot(g_v[...], select_ref[...])
    lane = lax.broadcasted_iota(jnp.int32, packed.shape, 1)
    packed = jnp.where(lane == s_widths[0] * 4 + s_widths[1] * 8, loss, packed)
    o_v[:, pl.ds(0, packed.shape[1])] = packed
    grads_out[...] = packed.astype(BF)
    piece = rows // 16
    for place in range(8):
        core_bit, x_step = place // 4, place % 4
        halves = []
        for yh_bit in (0, 1):
            owner = (head ^ (2 * yh_bit + core_bit)) * 4 + ((x + x_step) & 3)
            own_rows = pl.ds(pl.multiple_of(owner * piece, 8), piece)
            halves.append(o_v[own_rows, pl.ds(0, packed.shape[1])])
        ordered_out[pl.ds(place * 2 * piece, 2 * piece), :] = jnp.concatenate(halves, 0).astype(BF)


ANY = pl.BlockSpec(memory_space=pl.ANY)
WHOLE = pl.BlockSpec(memory_space=pltpu.VMEM)
SCALARS = pl.BlockSpec(memory_space=pltpu.SMEM)


def call(kernel, name, args, specs, outs, slots, rows, depth, cols, scratch=(), more_flops=0):
    return pl.pallas_call(
        kernel,
        out_shape=outs,
        in_specs=specs,
        out_specs=jax.tree.map(lambda _: WHOLE, outs),
        scratch_shapes=[
            pltpu.VMEM((slots, rows, 2 * depth), BF),
            pltpu.VMEM((slots, 2, depth, cols), BF),
            *scratch,
            pltpu.SemaphoreType.DMA((7 * slots,)),
        ],
        compiler_params=pltpu.CompilerParams(vmem_limit_bytes=28 * 1024 * 1024),
        cost_estimate=pl.CostEstimate(
            flops=slots * 4 * rows * depth * cols + more_flops,
            bytes_accessed=slots * 4 * depth * (rows + cols),
            transcendentals=0,
        ),
        name=name,
    )(*args)


def per_device(
    teacher_states,
    teacher_wq,
    teacher_wk,
    teacher_wv,
    student_states,
    student_wq,
    student_wk,
    student_wv,
    lengths,
):
    d = lax.axis_index("dp")
    head = lax.axis_index("head")
    x = lax.axis_index("mp")
    z, yl = d // 2, d % 2
    rows = student_states.shape[0]
    depth = teacher_wq.shape[0]
    q_width = teacher_wq.shape[1] // 4

    depth = teacher_wq.shape[0]
    part_y = teacher_wq[:, q_width:]
    z0 = jnp.concatenate(
        [jnp.concatenate([teacher_wk, teacher_wv], axis=1), teacher_wq[:, :q_width]], axis=0
    )
    y_cols = part_y.shape[1]
    cat, fence = jnp.concatenate, lax.optimization_barrier

    sq, sk = student_wq.shape[1], student_wk.shape[1]
    q_head, width = sq // 4, student_states.shape[1]
    length = lengths[0]
    states = lax.all_gather(teacher_states, ("head", "mp"), axis=1, tiled=True)

    other_y = swap_dp(part_y, 1)
    z1a, z1b = shift_z(z0, 1), shift_z(z0, -1)
    other_y, z1a, z1b = fence((other_y, z1a, z1b))
    pair_y = jnp.where(yl == 0, cat([part_y, other_y], 0), cat([other_y, part_y], 0))
    m1a = shift_z(cat([pair_y, z1a], 1), 1)
    m1b = shift_z(cat([pair_y, z1b], 1), -1)
    c1 = swap_dp(cat([z0, z1a, z1b], 0), 1)
    student_w = cat([student_wq, student_wk, student_wv], 1)
    wide_w = jnp.pad(student_w, ((0, 128), (0, 96)))
    wide_w = wide_w.at[width, sq + 2 * sk].set(1.0)
    m1a, m1b, c1, wide_w = fence((m1a, m1b, c1, wide_w))
    m2a, m2b = shift_z(m1a, 1), shift_z(m1b, -1)
    c2 = swap_dp(cat([m1a[:, y_cols:], m1b[:, y_cols:]], 0), 1)
    unit = width // 16
    columns = []
    for e in range(4):
        blocks = []
        for r in range(4):
            owner = ((d ^ e) + 4 * r) % 16
            blocks.append(lax.dynamic_slice(student_states, (0, owner * unit), (rows, unit)))
        columns.append(cat(blocks, 1))
    m2a, m2b, c2, *columns = fence((m2a, m2b, c2, *columns))
    m3a, m3b = shift_z(m2a, 1), shift_z(m2b, -1)
    c3 = swap_dp(cat([m2a[:, y_cols:], m2b[:, y_cols:]], 0), 1)
    padded = [student_wq[:, i * q_head : (i + 1) * q_head] for i in (1, 2, 3, 0)]
    padded.insert(3, cat([student_wk, student_wv], 1))
    padded = cat([jnp.pad(part, ((0, 0), (0, 128 - part.shape[1]))) for part in padded], 1)
    student = dot(student_states, padded).astype(BF)
    coord = jnp.stack([z, yl, head, x, length]).astype(jnp.int32)
    cols = y_cols + 2 * q_width
    acc_shape = jax.ShapeDtypeStruct((rows, cols), F32)
    near = call(
        near_kernel, "near",
        (coord, states, pair_y, z0, z1a, z1b, m1a, m1b, m2a, m2b, c1, c2),
        [SCALARS] + [ANY] * 11, acc_shape, 5, rows, depth, cols,
    )
    m3a, m3b, c3, near, student = fence((m3a, m3b, c3, near, student))
    f0 = shift_z(m3a[:depth, :y_cols], 1)
    f1 = shift_z(m3b[depth:, :y_cols], -1)
    c4 = swap_dp(m3a[:, y_cols:], 1)
    acc = call(
        far_kernel, "far", (coord, near, states, m2a, m2b, m3a, m3b, c3),
        [SCALARS, WHOLE] + [ANY] * 6, acc_shape, 2, rows, depth, cols,
    )

    select = np.zeros((cols, 384), np.float32)
    for i, block in enumerate((4, 0, 1, 2)):
        for j in range(q_head):
            select[block * 128 + j, i * q_head + j] = 1.0
    for j in range(2 * sk):
        select[3 * 128 + j, sq + j] = 1.0
    widths = ((q_width, teacher_wk.shape[1] // 4), (q_head, sk // 4))
    out = jax.ShapeDtypeStruct((rows, 384), BF)
    with_loss, ordered = call(
        functools.partial(finish_kernel, widths), "finish",
        (coord, acc, student, jnp.asarray(select, BF), states, m3a, f0, f1, c4),
        [SCALARS, WHOLE, WHOLE, WHOLE] + [ANY] * 5, (out, out), 1, rows, depth, cols,
        scratch=(
            pltpu.VMEM((rows, cols), BF),
            pltpu.VMEM((rows, cols), BF),
            pltpu.VMEM((rows, cols), F32),
            pltpu.VMEM((rows, rows), BF),
            pltpu.VMEM((5, 128, rows), F32),
        ),
        more_flops=12 * 8 * rows * rows * 128,
    )
    grads = with_loss[:, : sq + 2 * sk]
    half = rows // 2

    piece = rows // 16

    def state_term(part):
        return lax.dot_general(
            part, wide_w, (((1,), (1,)), ((), ())), preferred_element_type=F32
        ).astype(BF)

    def weight_term(e, grads):
        return lax.dot_general(
            grads, columns[e], (((0,), (0,)), ((), ())), preferred_element_type=F32
        )

    terms = [weight_term(e, grads).astype(BF) for e in (3, 2, 1)]
    *terms, ordered = fence((*terms, ordered))
    received = [swap_dp(term, e) for term, e in zip(terms, (3, 2, 1))]
    from_core = swap_head(state_term(ordered[half:]), 1)
    summed = (state_term(ordered[:half]).astype(F32) + from_core.astype(F32)).astype(BF)
    summed, grads = fence((summed, grads))
    slab = half // 4
    sent = [shift_x(summed[step * slab : (step + 1) * slab], step) for step in (2, 1, 3)]
    first_square = weight_term(0, grads)
    *received, first_square = fence((*received, *sent, first_square))
    received, sent = received[:3], received[3:]
    square = first_square
    for part in received:
        square = square + part.astype(F32)
    chunks = [square[:, r * unit : (r + 1) * unit] for r in range(4)]
    total = summed[:slab].astype(F32)
    for part in sent:
        total = total + part.astype(F32)
    last = swap_head(total[piece:].astype(BF), 2)
    weight_grad = chunks[0]
    for r in (2, 1, 3):
        moved = lax.ppermute(
            chunks[r].astype(BF), "dp", [(i, (i + 4 * r) % 16) for i in range(16)]
        )
        weight_grad = weight_grad + moved.astype(F32)
    weight_grad = weight_grad.T
    total = total[:piece] + last.astype(F32)
    grad_states = total[:, :width]
    seq_loss = total[0, width : width + 1]

    return (
        weight_grad[:, :sq],
        weight_grad[:, sq : sq + sk],
        weight_grad[:, sq + sk :],
        grad_states,
        seq_loss,
    )


def solution(mesh):
    in_specs = (
        P("dp", ("head", "mp")),
        P("dp", ("head", "mp")),
        P("dp", ("head", "mp")),
        P("dp", ("head", "mp")),
        P("dp", None),
        P(None, ("head", "mp")),
        P(None, ("head", "mp")),
        P(None, ("head", "mp")),
        P("dp"),
    )
    out_specs = (
        P("dp", ("head", "mp")),
        P("dp", ("head", "mp")),
        P("dp", ("head", "mp")),
        P(("dp", "head", "mp"), None),
        P("dp"),
    )
    return jax.shard_map(
        per_device, mesh=mesh, in_specs=in_specs, out_specs=out_specs, check_vma=False
    )
```

```python
import functools
import math

import jax
import jax.numpy as jnp
import numpy as np
from jax import lax
from jax.experimental import pallas as pl
from jax.experimental.pallas import tpu as pltpu
from jax.sharding import PartitionSpec as P

R = 64

LOSS_SCALE = 16.0
MASK_VALUE = -1000000000.0

BF = jnp.bfloat16
F32 = jnp.float32


def shift_z(a, step):
    return lax.ppermute(a, "dp", [(d, (d + 2 * step) % 16) for d in range(16)])


def swap_dp(a, bits):
    return lax.ppermute(a, "dp", [(d, d ^ bits) for d in range(16)])


def swap_head(a, bits):
    return lax.ppermute(a, "head", [(h, h ^ bits) for h in range(4)])


def shift_x(a, step):
    return lax.ppermute(a, "mp", [(m, (m + step) % 4) for m in range(4)])


def dot(a, b):
    return jnp.dot(a, b, preferred_element_type=F32)


OFFSETS = (0, -1, 1, -2, 2, -3, 3, 4)


class Loader:
    def __init__(self, coord, states, a_v, w_v, sems):
        self.z, self.yl, self.head, self.x = coord[0], coord[1], coord[2], coord[3]
        self.states, self.a_v, self.w_v, self.sems = states, a_v, w_v, sems
        self.count = 0
        self.slots = []

    def copy(self, src, dst):
        made = pltpu.make_async_copy(src, dst, self.sems.at[self.count])
        self.count += 1
        made.start()
        return made

    def copy_state(self, owner, dst):
        far = (owner - self.x) & 3
        place = jnp.where(far == 3, 1, jnp.where(far == 0, 0, far + 1))
        yh_bit = (owner >> 3) ^ (self.head >> 1)
        first = pl.multiple_of((place * 2 + yh_bit) * dst.shape[1], 128)
        other_core = ((owner >> 2) & 1) ^ (self.head & 1)
        sem = self.sems.at[self.count]
        self.count += 1
        made = [
            pltpu.make_async_copy(ref.at[:, pl.ds(first, dst.shape[1])], dst, sem)
            for ref in self.states
        ]
        pl.when(other_core == 0)(made[0].start)
        pl.when(other_core == 1)(made[1].start)
        return made[0]

    def load(self, offset, y_parts, own, crossed):
        slot, w_v = len(self.slots), self.w_v
        depth, z_cols = w_v.shape[2], w_v.shape[3] // 5
        y_cols = 3 * z_cols
        owner = (self.z + offset + 8) & 7
        made = [
            self.copy_state(2 * owner + side, self.a_v.at[slot, :, pl.ds(side * depth, depth)])
            for side in (0, 1)
        ]
        for side, (ref, row) in enumerate(y_parts):
            src = ref.at[pl.ds(row, depth), pl.ds(0, y_cols)]
            made.append(self.copy(src, w_v.at[slot, side, :, pl.ds(0, y_cols)]))
        for fold in (0, 1):
            cols = pl.ds(y_cols + fold * z_cols, z_cols)
            for (ref, row, col), side in ((own, self.yl), (crossed, 1 - self.yl)):
                src = ref.at[pl.ds(row + fold * depth, depth), pl.ds(col, z_cols)]
                made.append(self.copy(src, w_v.at[slot, side, :, cols]))
        self.slots.append(made)

    def term(self, slot):
        for made in self.slots[slot]:
            made.wait()
        a, w = self.a_v[slot], self.w_v[slot]
        return dot(a, w.reshape(w.shape[0] * w.shape[1], w.shape[2]))


def near_kernel(
    coord, mine, other, pair_y, z0, z1a, z1b, m1a, m1b, m2a, m2b, c1, c2, acc, a_v, w_v, sems
):
    depth, y_cols = w_v.shape[2], pair_y.shape[1]
    loader = Loader(coord, (mine, other), a_v, w_v, sems)
    pieces = (
        (pair_y, (z0, 0, 0), (c1, 0)),
        (m1a, (z1a, 0, 0), (c1, 2)),
        (m1b, (z1b, 0, 0), (c1, 4)),
        (m2a, (m1a, 0, y_cols), (c2, 0)),
        (m2b, (m1b, 0, y_cols), (c2, 2)),
    )
    for offset, (y_ref, own, (crossed, place)) in zip(OFFSETS, pieces):
        loader.load(
            offset, ((y_ref, 0), (y_ref, depth)), own, (crossed, place * depth, 0)
        )
    acc[...] = loader.term(0)
    for slot in range(1, 5):
        acc[...] += loader.term(slot)


def far_kernel(coord, before, mine, other, m2a, m2b, m3a, m3b, c3, acc, a_v, w_v, sems):
    depth, y_cols = w_v.shape[2], w_v.shape[3] // 5 * 3
    loader = Loader(coord, (mine, other), a_v, w_v, sems)
    loader.load(-3, ((m3a, 0), (m3a, depth)), (m2a, 0, y_cols), (c3, 0, 0))
    loader.load(3, ((m3b, 0), (m3b, depth)), (m2b, 0, y_cols), (c3, 2 * depth, 0))
    acc[...] = before[...] + loader.term(0)
    acc[...] += loader.term(1)


BLOCK = 384


HEADS = 12
NT = (((1,), (1,)), ((), ()))
TN = (((0,), (0,)), ((), ()))


def place_of(i, of_query, of_other):
    query = i < 4
    block = jnp.where(query, i + i // 3, 3)
    first = jnp.where(query, 0, (i - 4) * of_other)
    return block, first, jnp.where(query, 128, of_other), query


def only(cols, first, width):
    lane = lax.broadcasted_iota(jnp.int32, cols.shape, 1)
    mine = (lane >= first) & (lane < first + width)
    return jnp.where(mine, cols.astype(F32), 0.0).astype(BF)


def scale_of(query, widths):
    scales = [1.0 / (math.sqrt(w) * math.log(2.0)) for w in widths]
    return jnp.where(query, scales[0], scales[1])


def finish_kernel(
    widths, coord, before, student_ref, select_ref, mine_a, other_a, m3a, f0, f1, c4,
    grads_out, ordered_out, a_v, w_v, t_v, g_v, o_v, sg_v, turned_v, sems,
):
    depth, y_cols = f0.shape
    t_widths, s_widths = widths
    head, x, length = coord[2], coord[3], coord[4]
    rows = t_v.shape[0]
    loader = Loader(coord, (mine_a, other_a), a_v, w_v, sems)
    loader.load(4, ((f0, 0), (f1, 0)), (m3a, 0, y_cols), (c4, 0, 0))

    t_v[...] = (before[...] + loader.term(0)).astype(BF)
    valid_keys = lax.broadcasted_iota(jnp.int32, (1, rows), 1) < length
    o_v[...] = jnp.zeros_like(o_v)
    turned_v[...] = jnp.zeros_like(turned_v)

    def one_head(i, kl):
        block, t_first, t_width, query = place_of(i, *t_widths)
        _, s_first, s_width, _ = place_of(i, *s_widths)
        scale, s_scale = scale_of(query, t_widths), scale_of(query, s_widths)
        lanes = pl.ds(pl.multiple_of(block * 128, 128), 128)
        teacher = t_v[:, lanes]
        mine = only(teacher, t_first, t_width)
        student = student_ref[:, lanes]
        s_mine = only(student, s_first, s_width)
        for start in range(0, rows, BLOCK):
            part = slice(start, start + BLOCK)
            scores = lax.dot_general(mine[part], teacher, NT, preferred_element_type=F32)
            scores = jnp.where(valid_keys, scores * scale, MASK_VALUE)
            top = jnp.max(scores, axis=-1, keepdims=True)
            weight = jnp.exp2(scores - top)
            total = jnp.sum(weight, axis=-1, keepdims=True)
            other = lax.dot_general(s_mine[part], student, NT, preferred_element_type=F32)
            other = jnp.where(valid_keys, other * s_scale, MASK_VALUE)
            s_top = jnp.max(other, axis=-1, keepdims=True)
            s_weight = jnp.exp2(other - s_top)
            s_total = jnp.sum(s_weight, axis=-1, keepdims=True)
            cross = jnp.sum(weight * (scores - other), axis=-1, keepdims=True)
            row_kl = cross / total - (top + jnp.log2(total)) + (s_top + jnp.log2(s_total))
            valid = lax.broadcasted_iota(jnp.int32, (BLOCK, 1), 0) + start < length
            kl = kl + jnp.sum(jnp.where(valid, row_kl, 0.0), axis=0, keepdims=True)
            gain = jnp.where(valid, LOSS_SCALE / total, 0.0)
            s_gain = jnp.where(valid, LOSS_SCALE / s_total, 0.0)
            sg_v[part, :] = (s_weight * s_gain - weight * gain).astype(BF)
        sg = sg_v[...]
        o_v[:, lanes] += dot(sg, s_mine)
        turned_v[block] += lax.dot_general(s_mine, sg, TN, preferred_element_type=F32)
        return kl

    kl = lax.fori_loop(0, HEADS, one_head, jnp.zeros((1, 1), F32))
    over = [1.0 / math.sqrt(w) for w in s_widths]
    for block in range(5):
        lanes = slice(block * 128, block * 128 + 128)
        both = o_v[:, lanes] + turned_v[block].T
        g_v[:, lanes] = (both * over[block == 3]).astype(BF)
    loss = kl * math.log(2.0) / (3.0 * R * length.astype(F32))
    packed = dot(g_v[...], select_ref[...])
    lane = lax.broadcasted_iota(jnp.int32, packed.shape, 1)
    packed = jnp.where(lane == s_widths[0] * 4 + s_widths[1] * 8, loss, packed)
    o_v[:, pl.ds(0, packed.shape[1])] = packed
    grads_out[...] = packed.astype(BF)
    piece = rows // 16
    for place in range(8):
        core_bit, x_step = place // 4, place % 4
        halves = []
        for yh_bit in (0, 1):
            owner = (head ^ (2 * yh_bit + core_bit)) * 4 + ((x + x_step) & 3)
            own_rows = pl.ds(pl.multiple_of(owner * piece, 8), piece)
            halves.append(o_v[own_rows, pl.ds(0, packed.shape[1])])
        ordered_out[pl.ds(place * 2 * piece, 2 * piece), :] = jnp.concatenate(halves, 0).astype(BF)


ANY = pl.BlockSpec(memory_space=pl.ANY)
WHOLE = pl.BlockSpec(memory_space=pltpu.VMEM)
SCALARS = pl.BlockSpec(memory_space=pltpu.SMEM)


def call(kernel, name, args, specs, outs, slots, rows, depth, cols, scratch=(), more_flops=0):
    return pl.pallas_call(
        kernel,
        out_shape=outs,
        in_specs=specs,
        out_specs=jax.tree.map(lambda _: WHOLE, outs),
        scratch_shapes=[
            pltpu.VMEM((slots, rows, 2 * depth), BF),
            pltpu.VMEM((slots, 2, depth, cols), BF),
            *scratch,
            pltpu.SemaphoreType.DMA((8 * slots,)),
        ],
        compiler_params=pltpu.CompilerParams(vmem_limit_bytes=28 * 1024 * 1024),
        cost_estimate=pl.CostEstimate(
            flops=slots * 4 * rows * depth * cols + more_flops,
            bytes_accessed=slots * 4 * depth * (rows + cols),
            transcendentals=0,
        ),
        name=name,
    )(*args)


def per_device(
    teacher_states,
    teacher_wq,
    teacher_wk,
    teacher_wv,
    student_states,
    student_wq,
    student_wk,
    student_wv,
    lengths,
):
    d = lax.axis_index("dp")
    head = lax.axis_index("head")
    x = lax.axis_index("mp")
    z, yl = d // 2, d % 2
    rows = student_states.shape[0]
    depth = teacher_wq.shape[0]
    q_width = teacher_wq.shape[1] // 4

    depth = teacher_wq.shape[0]
    part_y = teacher_wq[:, q_width:]
    z0 = jnp.concatenate(
        [jnp.concatenate([teacher_wk, teacher_wv], axis=1), teacher_wq[:, :q_width]], axis=0
    )
    y_cols = part_y.shape[1]
    cat, fence = jnp.concatenate, lax.optimization_barrier

    sq, sk = student_wq.shape[1], student_wk.shape[1]
    q_head, width = sq // 4, student_states.shape[1]
    length = lengths[0]

    other_y = swap_dp(part_y, 1)
    z1a, z1b = shift_z(z0, 1), shift_z(z0, -1)
    pair = cat([teacher_states, swap_head(teacher_states, 2)], 1)
    other_y, z1a, z1b = fence((other_y, z1a, z1b))
    pair_y = jnp.where(yl == 0, cat([part_y, other_y], 0), cat([other_y, part_y], 0))
    m1a = shift_z(cat([pair_y, z1a], 1), 1)
    m1b = shift_z(cat([pair_y, z1b], 1), -1)
    c1 = swap_dp(cat([z0, z1a, z1b], 0), 1)
    left, right = shift_x(pair, 1), shift_x(pair, -1)
    student_w = cat([student_wq, student_wk, student_wv], 1)
    wide_w = jnp.pad(student_w, ((0, 128), (0, 96)))
    wide_w = wide_w.at[width, sq + 2 * sk].set(1.0)
    padded = [student_wq[:, i * q_head : (i + 1) * q_head] for i in (1, 2, 3, 0)]
    padded.insert(3, cat([student_wk, student_wv], 1))
    padded = cat([jnp.pad(part, ((0, 0), (0, 128 - part.shape[1]))) for part in padded], 1)
    m1a, m1b, c1, wide_w, padded, left, right = fence(
        (m1a, m1b, c1, wide_w, padded, left, right)
    )
    m2a, m2b = shift_z(m1a, 1), shift_z(m1b, -1)
    c2 = swap_dp(cat([m1a[:, y_cols:], m1b[:, y_cols:]], 0), 1)
    part = rows // 2
    far = cat([shift_x(left[:part], 1), shift_x(right[part:], -1)], 0)
    unit = width // 16
    columns = []
    for e in range(4):
        blocks = []
        for r in range(4):
            owner = ((d ^ e) + 4 * r) % 16
            blocks.append(lax.dynamic_slice(student_states, (0, owner * unit), (rows, unit)))
        columns.append(cat(blocks, 1))
    student = dot(student_states, padded).astype(BF)
    m2a, m2b, c2, far, student, *columns = fence((m2a, m2b, c2, far, student, *columns))
    mine = cat([pair, left, right, far], 1)
    other = swap_head(mine, 1)
    m3a, m3b = shift_z(m2a, 1), shift_z(m2b, -1)
    c3 = swap_dp(cat([m2a[:, y_cols:], m2b[:, y_cols:]], 0), 1)
    coord = jnp.stack([z, yl, head, x, length]).astype(jnp.int32)
    cols = y_cols + 2 * q_width
    acc_shape = jax.ShapeDtypeStruct((rows, cols), F32)
    near = call(
        near_kernel, "near",
        (coord, mine, other, pair_y, z0, z1a, z1b, m1a, m1b, m2a, m2b, c1, c2),
        [SCALARS] + [ANY] * 12, acc_shape, 5, rows, depth, cols,
    )
    m3a, m3b, c3, near, student = fence((m3a, m3b, c3, near, student))
    f0 = shift_z(m3a[:depth, :y_cols], 1)
    f1 = shift_z(m3b[depth:, :y_cols], -1)
    c4 = swap_dp(m3a[:, y_cols:], 1)
    acc = call(
        far_kernel, "far", (coord, near, mine, other, m2a, m2b, m3a, m3b, c3),
        [SCALARS, WHOLE] + [ANY] * 7, acc_shape, 2, rows, depth, cols,
    )

    select = np.zeros((cols, 384), np.float32)
    for i, block in enumerate((4, 0, 1, 2)):
        for j in range(q_head):
            select[block * 128 + j, i * q_head + j] = 1.0
    for j in range(2 * sk):
        select[3 * 128 + j, sq + j] = 1.0
    widths = ((q_width, teacher_wk.shape[1] // 4), (q_head, sk // 4))
    out = jax.ShapeDtypeStruct((rows, 384), BF)
    with_loss, ordered = call(
        functools.partial(finish_kernel, widths), "finish",
        (coord, acc, student, jnp.asarray(select, BF), mine, other, m3a, f0, f1, c4),
        [SCALARS, WHOLE, WHOLE, WHOLE] + [ANY] * 6, (out, out), 1, rows, depth, cols,
        scratch=(
            pltpu.VMEM((rows, cols), BF),
            pltpu.VMEM((rows, cols), BF),
            pltpu.VMEM((rows, cols), F32),
            pltpu.VMEM((rows, rows), BF),
            pltpu.VMEM((5, 128, rows), F32),
        ),
        more_flops=12 * 8 * rows * rows * 128,
    )
    grads = with_loss[:, : sq + 2 * sk]
    half = rows // 2

    piece = rows // 16

    def state_term(part):
        return lax.dot_general(
            part, wide_w, (((1,), (1,)), ((), ())), preferred_element_type=F32
        ).astype(BF)

    def weight_term(e, grads):
        return lax.dot_general(
            grads, columns[e], (((0,), (0,)), ((), ())), preferred_element_type=F32
        )

    terms = [weight_term(e, grads).astype(BF) for e in (3, 2, 1)]
    *terms, ordered = fence((*terms, ordered))
    received = [swap_dp(term, e) for term, e in zip(terms, (3, 2, 1))]
    from_core = swap_head(state_term(ordered[half:]), 1)
    summed = (state_term(ordered[:half]).astype(F32) + from_core.astype(F32)).astype(BF)
    summed, grads = fence((summed, grads))
    slab = half // 4
    sent = [shift_x(summed[step * slab : (step + 1) * slab], step) for step in (2, 1, 3)]
    first_square = weight_term(0, grads)
    *received, first_square = fence((*received, *sent, first_square))
    received, sent = received[:3], received[3:]
    square = first_square
    for part in received:
        square = square + part.astype(F32)
    chunks = [square[:, r * unit : (r + 1) * unit] for r in range(4)]
    total = summed[:slab].astype(F32)
    for part in sent:
        total = total + part.astype(F32)
    last = swap_head(total[piece:].astype(BF), 2)
    weight_grad = chunks[0]
    for r in (2, 1, 3):
        moved = lax.ppermute(
            chunks[r].astype(BF), "dp", [(i, (i + 4 * r) % 16) for i in range(16)]
        )
        weight_grad = weight_grad + moved.astype(F32)
    weight_grad = weight_grad.T
    total = total[:piece] + last.astype(F32)
    grad_states = total[:, :width]
    seq_loss = total[0, width : width + 1]

    return (
        weight_grad[:, :sq],
        weight_grad[:, sq : sq + sk],
        weight_grad[:, sq + sk :],
        grad_states,
        seq_loss,
    )


def solution(mesh):
    in_specs = (
        P("dp", ("head", "mp")),
        P("dp", ("head", "mp")),
        P("dp", ("head", "mp")),
        P("dp", ("head", "mp")),
        P("dp", None),
        P(None, ("head", "mp")),
        P(None, ("head", "mp")),
        P(None, ("head", "mp")),
        P("dp"),
    )
    out_specs = (
        P("dp", ("head", "mp")),
        P("dp", ("head", "mp")),
        P("dp", ("head", "mp")),
        P(("dp", "head", "mp"), None),
        P("dp"),
    )
    return jax.shard_map(
        per_device, mesh=mesh, in_specs=in_specs, out_specs=out_specs, check_vma=False
    )
```

```python
import functools
import math

import jax
import jax.numpy as jnp
import numpy as np
from jax import lax
from jax.experimental import pallas as pl
from jax.experimental.pallas import tpu as pltpu
from jax.sharding import PartitionSpec as P

R = 64

LOSS_SCALE = 16.0
MASK_VALUE = -1000000000.0

BF = jnp.bfloat16
F32 = jnp.float32


def shift_z(a, step):
    return lax.ppermute(a, "dp", [(d, (d + 2 * step) % 16) for d in range(16)])


def swap_dp(a, bits):
    return lax.ppermute(a, "dp", [(d, d ^ bits) for d in range(16)])


def swap_head(a, bits):
    return lax.ppermute(a, "head", [(h, h ^ bits) for h in range(4)])


def shift_x(a, step):
    return lax.ppermute(a, "mp", [(m, (m + step) % 4) for m in range(4)])


def dot(a, b):
    return jnp.dot(a, b, preferred_element_type=F32)


OFFSETS = (0, -1, 1, -2, 2, -3, 3, 4)


class Loader:
    def __init__(self, coord, states, a_v, w_v, sems):
        self.z, self.yl, self.head, self.x = coord[0], coord[1], coord[2], coord[3]
        self.states, self.a_v, self.w_v, self.sems = states, a_v, w_v, sems
        self.count = 0
        self.slots = []

    def copy(self, src, dst):
        made = pltpu.make_async_copy(src, dst, self.sems.at[self.count])
        self.count += 1
        made.start()
        return made

    def copy_state(self, owner, dst):
        far = (owner - self.x) & 3
        place = jnp.where(far == 3, 1, jnp.where(far == 0, 0, far + 1))
        yh_bit = (owner >> 3) ^ (self.head >> 1)
        first = pl.multiple_of((place * 2 + yh_bit) * dst.shape[1], 128)
        other_core = ((owner >> 2) & 1) ^ (self.head & 1)
        sem = self.sems.at[self.count]
        self.count += 1
        made = [
            pltpu.make_async_copy(ref.at[:, pl.ds(first, dst.shape[1])], dst, sem)
            for ref in self.states
        ]
        pl.when(other_core == 0)(made[0].start)
        pl.when(other_core == 1)(made[1].start)
        return made[0]

    def load(self, offset, y_parts, own, crossed):
        slot, w_v = len(self.slots), self.w_v
        depth, z_cols = w_v.shape[2], w_v.shape[3] // 5
        y_cols = 3 * z_cols
        owner = (self.z + offset + 8) & 7
        made = [
            self.copy_state(2 * owner + side, self.a_v.at[slot, :, pl.ds(side * depth, depth)])
            for side in (0, 1)
        ]
        for side, (ref, row) in enumerate(y_parts):
            src = ref.at[pl.ds(row, depth), pl.ds(0, y_cols)]
            made.append(self.copy(src, w_v.at[slot, side, :, pl.ds(0, y_cols)]))
        for fold in (0, 1):
            cols = pl.ds(y_cols + fold * z_cols, z_cols)
            for (ref, row, col), side in ((own, self.yl), (crossed, 1 - self.yl)):
                src = ref.at[pl.ds(row + fold * depth, depth), pl.ds(col, z_cols)]
                made.append(self.copy(src, w_v.at[slot, side, :, cols]))
        self.slots.append(made)

    def term(self, slot):
        for made in self.slots[slot]:
            made.wait()
        a, w = self.a_v[slot], self.w_v[slot]
        return dot(a, w.reshape(w.shape[0] * w.shape[1], w.shape[2]))


def near_kernel(
    coord, mine, other, pair_y, z0, z1a, z1b, m1a, m1b, m2a, m2b, c1, c2, acc, a_v, w_v, sems
):
    depth, y_cols = w_v.shape[2], pair_y.shape[1]
    loader = Loader(coord, (mine, other), a_v, w_v, sems)
    pieces = (
        (pair_y, (z0, 0, 0), (c2, 4)),
        (m1a, (z1a, 0, 0), (c1, 0)),
        (m1b, (z1b, 0, 0), (c1, 2)),
        (m2a, (m1a, 0, y_cols), (c2, 0)),
        (m2b, (m1b, 0, y_cols), (c2, 2)),
    )
    for offset, (y_ref, own, (crossed, place)) in zip(OFFSETS, pieces):
        loader.load(
            offset, ((y_ref, 0), (y_ref, depth)), own, (crossed, place * depth, 0)
        )
    acc[...] = loader.term(0)
    for slot in range(1, 5):
        acc[...] += loader.term(slot)


def far_kernel(coord, before, mine, other, m2a, m2b, m3a, m3b, c3, acc, a_v, w_v, sems):
    depth, y_cols = w_v.shape[2], w_v.shape[3] // 5 * 3
    loader = Loader(coord, (mine, other), a_v, w_v, sems)
    loader.load(-3, ((m3a, 0), (m3a, depth)), (m2a, 0, y_cols), (c3, 0, 0))
    loader.load(3, ((m3b, 0), (m3b, depth)), (m2b, 0, y_cols), (c3, 2 * depth, 0))
    acc[...] = before[...] + loader.term(0)
    acc[...] += loader.term(1)


BLOCK = 384


HEADS = 12
NT = (((1,), (1,)), ((), ()))
TN = (((0,), (0,)), ((), ()))


def place_of(i, of_query, of_other):
    query = i < 4
    block = jnp.where(query, i + i // 3, 3)
    first = jnp.where(query, 0, (i - 4) * of_other)
    return block, first, jnp.where(query, 128, of_other), query


def only(cols, first, width):
    lane = lax.broadcasted_iota(jnp.int32, cols.shape, 1)
    mine = (lane >= first) & (lane < first + width)
    return jnp.where(mine, cols.astype(F32), 0.0).astype(BF)


def scale_of(query, widths):
    scales = [1.0 / (math.sqrt(w) * math.log(2.0)) for w in widths]
    return jnp.where(query, scales[0], scales[1])


def finish_kernel(
    widths, coord, before, student_ref, select_ref, mine_a, other_a, m3a, f0, f1, c4,
    grads_out, ordered_out, a_v, w_v, t_v, g_v, o_v, sg_v, turned_v, sems,
):
    depth, y_cols = f0.shape
    t_widths, s_widths = widths
    head, x, length = coord[2], coord[3], coord[4]
    rows = t_v.shape[0]
    loader = Loader(coord, (mine_a, other_a), a_v, w_v, sems)
    loader.load(4, ((f0, 0), (f1, 0)), (m3a, 0, y_cols), (c4, 0, 0))

    t_v[...] = (before[...] + loader.term(0)).astype(BF)
    valid_keys = lax.broadcasted_iota(jnp.int32, (1, rows), 1) < length
    o_v[...] = jnp.zeros_like(o_v)
    turned_v[...] = jnp.zeros_like(turned_v)

    def one_head(i, kl):
        block, t_first, t_width, query = place_of(i, *t_widths)
        _, s_first, s_width, _ = place_of(i, *s_widths)
        scale, s_scale = scale_of(query, t_widths), scale_of(query, s_widths)
        lanes = pl.ds(pl.multiple_of(block * 128, 128), 128)
        teacher = t_v[:, lanes]
        mine = only(teacher, t_first, t_width)
        student = student_ref[:, lanes]
        s_mine = only(student, s_first, s_width)
        for start in range(0, rows, BLOCK):
            part = slice(start, start + BLOCK)
            scores = lax.dot_general(mine[part], teacher, NT, preferred_element_type=F32)
            scores = jnp.where(valid_keys, scores * scale, MASK_VALUE)
            top = jnp.max(scores, axis=-1, keepdims=True)
            weight = jnp.exp2(scores - top)
            total = jnp.sum(weight, axis=-1, keepdims=True)
            other = lax.dot_general(s_mine[part], student, NT, preferred_element_type=F32)
            other = jnp.where(valid_keys, other * s_scale, MASK_VALUE)
            s_top = jnp.max(other, axis=-1, keepdims=True)
            s_weight = jnp.exp2(other - s_top)
            s_total = jnp.sum(s_weight, axis=-1, keepdims=True)
            cross = jnp.sum(weight * (scores - other), axis=-1, keepdims=True)
            row_kl = cross / total - (top + jnp.log2(total)) + (s_top + jnp.log2(s_total))
            valid = lax.broadcasted_iota(jnp.int32, (BLOCK, 1), 0) + start < length
            kl = kl + jnp.sum(jnp.where(valid, row_kl, 0.0), axis=0, keepdims=True)
            gain = jnp.where(valid, LOSS_SCALE / total, 0.0)
            s_gain = jnp.where(valid, LOSS_SCALE / s_total, 0.0)
            sg_v[part, :] = (s_weight * s_gain - weight * gain).astype(BF)
        sg = sg_v[...]
        o_v[:, lanes] += dot(sg, s_mine)
        turned_v[block] += lax.dot_general(s_mine, sg, TN, preferred_element_type=F32)
        return kl

    kl = lax.fori_loop(0, HEADS, one_head, jnp.zeros((1, 1), F32))
    over = [1.0 / math.sqrt(w) for w in s_widths]
    for block in range(5):
        lanes = slice(block * 128, block * 128 + 128)
        both = o_v[:, lanes] + turned_v[block].T
        g_v[:, lanes] = (both * over[block == 3]).astype(BF)
    loss = kl * math.log(2.0) / (3.0 * R * length.astype(F32))
    packed = dot(g_v[...], select_ref[...])
    lane = lax.broadcasted_iota(jnp.int32, packed.shape, 1)
    packed = jnp.where(lane == s_widths[0] * 4 + s_widths[1] * 8, loss, packed)
    o_v[:, pl.ds(0, packed.shape[1])] = packed
    grads_out[...] = packed.astype(BF)
    piece = rows // 16
    for place in range(8):
        core_bit, x_step = place // 4, place % 4
        halves = []
        for yh_bit in (0, 1):
            owner = (head ^ (2 * yh_bit + core_bit)) * 4 + ((x + x_step) & 3)
            own_rows = pl.ds(pl.multiple_of(owner * piece, 8), piece)
            halves.append(o_v[own_rows, pl.ds(0, packed.shape[1])])
        ordered_out[pl.ds(place * 2 * piece, 2 * piece), :] = jnp.concatenate(halves, 0).astype(BF)


ANY = pl.BlockSpec(memory_space=pl.ANY)
WHOLE = pl.BlockSpec(memory_space=pltpu.VMEM)
SCALARS = pl.BlockSpec(memory_space=pltpu.SMEM)


def call(kernel, name, args, specs, outs, slots, rows, depth, cols, scratch=(), more_flops=0):
    return pl.pallas_call(
        kernel,
        out_shape=outs,
        in_specs=specs,
        out_specs=jax.tree.map(lambda _: WHOLE, outs),
        scratch_shapes=[
            pltpu.VMEM((slots, rows, 2 * depth), BF),
            pltpu.VMEM((slots, 2, depth, cols), BF),
            *scratch,
            pltpu.SemaphoreType.DMA((8 * slots,)),
        ],
        compiler_params=pltpu.CompilerParams(vmem_limit_bytes=28 * 1024 * 1024),
        cost_estimate=pl.CostEstimate(
            flops=slots * 4 * rows * depth * cols + more_flops,
            bytes_accessed=slots * 4 * depth * (rows + cols),
            transcendentals=0,
        ),
        name=name,
    )(*args)


def per_device(
    teacher_states,
    teacher_wq,
    teacher_wk,
    teacher_wv,
    student_states,
    student_wq,
    student_wk,
    student_wv,
    lengths,
):
    d = lax.axis_index("dp")
    head = lax.axis_index("head")
    x = lax.axis_index("mp")
    z, yl = d // 2, d % 2
    rows = student_states.shape[0]
    depth = teacher_wq.shape[0]
    q_width = teacher_wq.shape[1] // 4

    depth = teacher_wq.shape[0]
    part_y = teacher_wq[:, q_width:]
    z0 = jnp.concatenate(
        [jnp.concatenate([teacher_wk, teacher_wv], axis=1), teacher_wq[:, :q_width]], axis=0
    )
    y_cols = part_y.shape[1]
    cat, fence = jnp.concatenate, lax.optimization_barrier

    sq, sk = student_wq.shape[1], student_wk.shape[1]
    q_head, width = sq // 4, student_states.shape[1]
    length = lengths[0]

    other_y = swap_dp(part_y, 1)
    z1a, z1b = shift_z(z0, 1), shift_z(z0, -1)
    pair = cat([teacher_states, swap_head(teacher_states, 2)], 1)
    other_y, z1a, z1b, student_wq, student_wk, student_wv = fence(
        (other_y, z1a, z1b, student_wq, student_wk, student_wv)
    )
    pair_y = jnp.where(yl == 0, cat([part_y, other_y], 0), cat([other_y, part_y], 0))
    m1a = shift_z(cat([pair_y, z1a], 1), 1)
    m1b = shift_z(cat([pair_y, z1b], 1), -1)
    c1 = swap_dp(cat([z1a, z1b], 0), 1)
    left, right = shift_x(pair, 1), shift_x(pair, -1)
    student_w = cat([student_wq, student_wk, student_wv], 1)
    wide_w = jnp.pad(student_w, ((0, 128), (0, 96)))
    wide_w = wide_w.at[width, sq + 2 * sk].set(1.0)
    padded = [student_wq[:, i * q_head : (i + 1) * q_head] for i in (1, 2, 3, 0)]
    padded.insert(3, cat([student_wk, student_wv], 1))
    padded = cat([jnp.pad(part, ((0, 0), (0, 128 - part.shape[1]))) for part in padded], 1)
    m1a, m1b, c1, wide_w, padded, left, right, student_states = fence(
        (m1a, m1b, c1, wide_w, padded, left, right, student_states)
    )
    m2a, m2b = shift_z(m1a, 1), shift_z(m1b, -1)
    c2 = swap_dp(cat([m1a[:, y_cols:], m1b[:, y_cols:], z0], 0), 1)
    part = rows // 2
    far = cat([shift_x(left[:part], 1), shift_x(right[part:], -1)], 0)
    unit = width // 16
    columns = []
    for e in range(4):
        blocks = []
        for r in range(4):
            owner = ((d ^ e) + 4 * r) % 16
            blocks.append(lax.dynamic_slice(student_states, (0, owner * unit), (rows, unit)))
        columns.append(cat(blocks, 1))
    student = dot(student_states, padded).astype(BF)
    m2a, m2b, c2, far, student, *columns = fence((m2a, m2b, c2, far, student, *columns))
    mine = cat([pair, left, right, far], 1)
    other = swap_head(mine, 1)
    m3a, m3b = shift_z(m2a, 1), shift_z(m2b, -1)
    c3 = swap_dp(cat([m2a[:, y_cols:], m2b[:, y_cols:]], 0), 1)
    coord = jnp.stack([z, yl, head, x, length]).astype(jnp.int32)
    cols = y_cols + 2 * q_width
    acc_shape = jax.ShapeDtypeStruct((rows, cols), F32)
    near = call(
        near_kernel, "near",
        (coord, mine, other, pair_y, z0, z1a, z1b, m1a, m1b, m2a, m2b, c1, c2),
        [SCALARS] + [ANY] * 12, acc_shape, 5, rows, depth, cols,
    )
    m3a, m3b, c3, near, student = fence((m3a, m3b, c3, near, student))
    f0 = shift_z(m3a[:depth, :y_cols], 1)
    f1 = shift_z(m3b[depth:, :y_cols], -1)
    c4 = swap_dp(m3a[:, y_cols:], 1)
    acc = call(
        far_kernel, "far", (coord, near, mine, other, m2a, m2b, m3a, m3b, c3),
        [SCALARS, WHOLE] + [ANY] * 7, acc_shape, 2, rows, depth, cols,
    )

    select = np.zeros((cols, 384), np.float32)
    for i, block in enumerate((4, 0, 1, 2)):
        for j in range(q_head):
            select[block * 128 + j, i * q_head + j] = 1.0
    for j in range(2 * sk):
        select[3 * 128 + j, sq + j] = 1.0
    widths = ((q_width, teacher_wk.shape[1] // 4), (q_head, sk // 4))
    out = jax.ShapeDtypeStruct((rows, 384), BF)
    with_loss, ordered = call(
        functools.partial(finish_kernel, widths), "finish",
        (coord, acc, student, jnp.asarray(select, BF), mine, other, m3a, f0, f1, c4),
        [SCALARS, WHOLE, WHOLE, WHOLE] + [ANY] * 6, (out, out), 1, rows, depth, cols,
        scratch=(
            pltpu.VMEM((rows, cols), BF),
            pltpu.VMEM((rows, cols), BF),
            pltpu.VMEM((rows, cols), F32),
            pltpu.VMEM((rows, rows), BF),
            pltpu.VMEM((5, 128, rows), F32),
        ),
        more_flops=12 * 8 * rows * rows * 128,
    )
    grads = with_loss[:, : sq + 2 * sk]
    half = rows // 2

    piece = rows // 16

    def state_term(part):
        return lax.dot_general(
            part, wide_w, (((1,), (1,)), ((), ())), preferred_element_type=F32
        ).astype(BF)

    def weight_term(e, grads):
        return lax.dot_general(
            grads, columns[e], (((0,), (0,)), ((), ())), preferred_element_type=F32
        )

    terms = [weight_term(e, grads).astype(BF) for e in (3, 2, 1)]
    *terms, ordered = fence((*terms, ordered))
    received = [swap_dp(term, e) for term, e in zip(terms, (3, 2, 1))]
    from_core = swap_head(state_term(ordered[half:]), 1)
    summed = (state_term(ordered[:half]).astype(F32) + from_core.astype(F32)).astype(BF)
    summed, grads = fence((summed, grads))
    slab = half // 4
    sent = [shift_x(summed[step * slab : (step + 1) * slab], step) for step in (2, 1, 3)]
    first_square = weight_term(0, grads)
    *received, first_square = fence((*received, *sent, first_square))
    received, sent = received[:3], received[3:]
    square = first_square
    for part in received:
        square = square + part.astype(F32)
    chunks = [square[:, r * unit : (r + 1) * unit] for r in range(4)]
    total = summed[:slab].astype(F32)
    for part in sent:
        total = total + part.astype(F32)
    last = swap_head(total[piece:].astype(BF), 2)
    weight_grad = chunks[0]
    for r in (2, 1, 3):
        moved = lax.ppermute(
            chunks[r].astype(BF), "dp", [(i, (i + 4 * r) % 16) for i in range(16)]
        )
        weight_grad = weight_grad + moved.astype(F32)
    weight_grad = weight_grad.T
    total = total[:piece] + last.astype(F32)
    grad_states = total[:, :width]
    seq_loss = total[0, width : width + 1]

    return (
        weight_grad[:, :sq],
        weight_grad[:, sq : sq + sk],
        weight_grad[:, sq + sk :],
        grad_states,
        seq_loss,
    )


def solution(mesh):
    in_specs = (
        P("dp", ("head", "mp")),
        P("dp", ("head", "mp")),
        P("dp", ("head", "mp")),
        P("dp", ("head", "mp")),
        P("dp", None),
        P(None, ("head", "mp")),
        P(None, ("head", "mp")),
        P(None, ("head", "mp")),
        P("dp"),
    )
    out_specs = (
        P("dp", ("head", "mp")),
        P("dp", ("head", "mp")),
        P("dp", ("head", "mp")),
        P(("dp", "head", "mp"), None),
        P("dp"),
    )
    return jax.shard_map(
        per_device, mesh=mesh, in_specs=in_specs, out_specs=out_specs, check_vma=False
    )
```

```python
import functools
import math

import jax
import jax.numpy as jnp
import numpy as np
from jax import lax
from jax.experimental import pallas as pl
from jax.experimental.pallas import tpu as pltpu
from jax.sharding import PartitionSpec as P

R = 64

LOSS_SCALE = 16.0
MASK_VALUE = -1000000000.0

BF = jnp.bfloat16
F32 = jnp.float32


def shift_z(a, step):
    return lax.ppermute(a, "dp", [(d, (d + 2 * step) % 16) for d in range(16)])


def swap_dp(a, bits):
    return lax.ppermute(a, "dp", [(d, d ^ bits) for d in range(16)])


def swap_head(a, bits):
    return lax.ppermute(a, "head", [(h, h ^ bits) for h in range(4)])


def shift_x(a, step):
    return lax.ppermute(a, "mp", [(m, (m + step) % 4) for m in range(4)])


def dot(a, b):
    return jnp.dot(a, b, preferred_element_type=F32)


OFFSETS = (0, -1, 1, -2, 2, -3, 3, 4)


class Loader:
    def __init__(self, coord, states, a_v, w_v, sems):
        self.z, self.yl, self.head, self.x = coord[0], coord[1], coord[2], coord[3]
        self.states, self.a_v, self.w_v, self.sems = states, a_v, w_v, sems
        self.count = 0
        self.slots = []

    def copy(self, src, dst):
        made = pltpu.make_async_copy(src, dst, self.sems.at[self.count])
        self.count += 1
        made.start()
        return made

    def copy_state(self, owner, dst):
        far = (owner - self.x) & 3
        place = jnp.where(far == 3, 1, jnp.where(far == 0, 0, far + 1))
        yh_bit = (owner >> 3) ^ (self.head >> 1)
        first = pl.multiple_of((place * 2 + yh_bit) * dst.shape[1], 128)
        other_core = ((owner >> 2) & 1) ^ (self.head & 1)
        sem = self.sems.at[self.count]
        self.count += 1
        made = [
            pltpu.make_async_copy(ref.at[:, pl.ds(first, dst.shape[1])], dst, sem)
            for ref in self.states
        ]
        pl.when(other_core == 0)(made[0].start)
        pl.when(other_core == 1)(made[1].start)
        return made[0]

    def load(self, offset, y_parts, own, crossed):
        slot, w_v = len(self.slots), self.w_v
        depth, z_cols = w_v.shape[2], w_v.shape[3] // 5
        y_cols = 3 * z_cols
        owner = (self.z + offset + 8) & 7
        made = [
            self.copy_state(2 * owner + side, self.a_v.at[slot, :, pl.ds(side * depth, depth)])
            for side in (0, 1)
        ]
        for side, (ref, row) in enumerate(y_parts):
            src = ref.at[pl.ds(row, depth), pl.ds(0, y_cols)]
            made.append(self.copy(src, w_v.at[slot, side, :, pl.ds(0, y_cols)]))
        for fold in (0, 1):
            cols = pl.ds(y_cols + fold * z_cols, z_cols)
            for (ref, row, col), side in ((own, self.yl), (crossed, 1 - self.yl)):
                src = ref.at[pl.ds(row + fold * depth, depth), pl.ds(col, z_cols)]
                made.append(self.copy(src, w_v.at[slot, side, :, cols]))
        self.slots.append(made)

    def term(self, slot):
        for made in self.slots[slot]:
            made.wait()
        a, w = self.a_v[slot], self.w_v[slot]
        return dot(a, w.reshape(w.shape[0] * w.shape[1], w.shape[2]))


def near_kernel(
    coord, mine, other, pair_y, z0, z1a, z1b, m1a, m1b, m2a, m2b, c1, c2, acc, a_v, w_v, sems
):
    depth, y_cols = w_v.shape[2], pair_y.shape[1]
    loader = Loader(coord, (mine, other), a_v, w_v, sems)
    pieces = (
        (pair_y, (z0, 0, 0), (c2, 4)),
        (m1a, (z1a, 0, 0), (c1, 0)),
        (m1b, (z1b, 0, 0), (c1, 2)),
        (m2a, (m1a, 0, y_cols), (c2, 0)),
        (m2b, (m1b, 0, y_cols), (c2, 2)),
    )
    for offset, (y_ref, own, (crossed, place)) in zip(OFFSETS, pieces):
        loader.load(
            offset, ((y_ref, 0), (y_ref, depth)), own, (crossed, place * depth, 0)
        )
    acc[...] = loader.term(0)
    for slot in range(1, 5):
        acc[...] += loader.term(slot)


def far_kernel(coord, before, mine, other, m2a, m2b, m3a, m3b, c3, acc, a_v, w_v, sems):
    depth, y_cols = w_v.shape[2], w_v.shape[3] // 5 * 3
    loader = Loader(coord, (mine, other), a_v, w_v, sems)
    loader.load(-3, ((m3a, 0), (m3a, depth)), (m2a, 0, y_cols), (c3, 0, 0))
    loader.load(3, ((m3b, 0), (m3b, depth)), (m2b, 0, y_cols), (c3, 2 * depth, 0))
    acc[...] = before[...] + loader.term(0)
    acc[...] += loader.term(1)


BLOCK = 384


HEADS = 12
NT = (((1,), (1,)), ((), ()))
TN = (((0,), (0,)), ((), ()))


def place_of(i, of_query, of_other):
    query = i < 4
    block = jnp.where(query, i + i // 3, 3)
    first = jnp.where(query, 0, (i - 4) * of_other)
    return block, first, jnp.where(query, 128, of_other), query


def only(cols, first, width):
    lane = lax.broadcasted_iota(jnp.int32, cols.shape, 1)
    mine = (lane >= first) & (lane < first + width)
    return jnp.where(mine, cols.astype(F32), 0.0).astype(BF)


def scale_of(query, widths):
    scales = [1.0 / (math.sqrt(w) * math.log(2.0)) for w in widths]
    return jnp.where(query, scales[0], scales[1])


def finish_kernel(
    widths, coord, before, student_ref, select_ref, mine_a, other_a, m3a, f0, f1, c4,
    grads_out, ordered_out, a_v, w_v, t_v, g_v, o_v, sg_v, turned_v, sems,
):
    depth, y_cols = f0.shape
    t_widths, s_widths = widths
    head, x, length = coord[2], coord[3], coord[4]
    rows = t_v.shape[0]
    loader = Loader(coord, (mine_a, other_a), a_v, w_v, sems)
    loader.load(4, ((f0, 0), (f1, 0)), (m3a, 0, y_cols), (c4, 0, 0))

    t_v[...] = (before[...] + loader.term(0)).astype(BF)
    valid_keys = lax.broadcasted_iota(jnp.int32, (1, rows), 1) < length
    o_v[...] = jnp.zeros_like(o_v)
    turned_v[...] = jnp.zeros_like(turned_v)

    def one_head(i, kl):
        block, t_first, t_width, query = place_of(i, *t_widths)
        _, s_first, s_width, _ = place_of(i, *s_widths)
        scale, s_scale = scale_of(query, t_widths), scale_of(query, s_widths)
        lanes = pl.ds(pl.multiple_of(block * 128, 128), 128)
        teacher = t_v[:, lanes]
        mine = only(teacher, t_first, t_width)
        student = student_ref[:, lanes]
        s_mine = only(student, s_first, s_width)
        for start in range(0, rows, BLOCK):
            part = slice(start, start + BLOCK)
            scores = lax.dot_general(mine[part], teacher, NT, preferred_element_type=F32)
            scores = jnp.where(valid_keys, scores * scale, MASK_VALUE)
            top = jnp.max(scores, axis=-1, keepdims=True)
            weight = jnp.exp2(scores - top)
            total = jnp.sum(weight, axis=-1, keepdims=True)
            other = lax.dot_general(s_mine[part], student, NT, preferred_element_type=F32)
            other = jnp.where(valid_keys, other * s_scale, MASK_VALUE)
            s_top = jnp.max(other, axis=-1, keepdims=True)
            s_weight = jnp.exp2(other - s_top)
            s_total = jnp.sum(s_weight, axis=-1, keepdims=True)
            cross = jnp.sum(weight * (scores - other), axis=-1, keepdims=True)
            row_kl = cross / total - (top + jnp.log2(total)) + (s_top + jnp.log2(s_total))
            valid = lax.broadcasted_iota(jnp.int32, (BLOCK, 1), 0) + start < length
            kl = kl + jnp.sum(jnp.where(valid, row_kl, 0.0), axis=0, keepdims=True)
            gain = jnp.where(valid, LOSS_SCALE / total, 0.0)
            s_gain = jnp.where(valid, LOSS_SCALE / s_total, 0.0)
            sg_v[part, :] = (s_weight * s_gain - weight * gain).astype(BF)
        sg = sg_v[...]
        o_v[:, lanes] += dot(sg, s_mine)
        turned_v[block] += lax.dot_general(s_mine, sg, TN, preferred_element_type=F32)
        return kl

    kl = lax.fori_loop(0, HEADS, one_head, jnp.zeros((1, 1), F32))
    over = [1.0 / math.sqrt(w) for w in s_widths]
    for block in range(5):
        lanes = slice(block * 128, block * 128 + 128)
        both = o_v[:, lanes] + turned_v[block].T
        g_v[:, lanes] = (both * over[block == 3]).astype(BF)
    loss = kl * math.log(2.0) / (3.0 * R * length.astype(F32))
    packed = dot(g_v[...], select_ref[...])
    lane = lax.broadcasted_iota(jnp.int32, packed.shape, 1)
    packed = jnp.where(lane == s_widths[0] * 4 + s_widths[1] * 8, loss, packed)
    o_v[:, pl.ds(0, packed.shape[1])] = packed
    grads_out[...] = packed.astype(BF)
    piece = rows // 16
    for place in range(8):
        core_bit, x_step = place // 4, place % 4
        halves = []
        for yh_bit in (0, 1):
            owner = (head ^ (2 * yh_bit + core_bit)) * 4 + ((x + x_step) & 3)
            own_rows = pl.ds(pl.multiple_of(owner * piece, 8), piece)
            halves.append(o_v[own_rows, pl.ds(0, packed.shape[1])])
        ordered_out[pl.ds(place * 2 * piece, 2 * piece), :] = jnp.concatenate(halves, 0).astype(BF)


ANY = pl.BlockSpec(memory_space=pl.ANY)
WHOLE = pl.BlockSpec(memory_space=pltpu.VMEM)
SCALARS = pl.BlockSpec(memory_space=pltpu.SMEM)


def call(kernel, name, args, specs, outs, slots, rows, depth, cols, scratch=(), more_flops=0):
    return pl.pallas_call(
        kernel,
        out_shape=outs,
        in_specs=specs,
        out_specs=jax.tree.map(lambda _: WHOLE, outs),
        scratch_shapes=[
            pltpu.VMEM((slots, rows, 2 * depth), BF),
            pltpu.VMEM((slots, 2, depth, cols), BF),
            *scratch,
            pltpu.SemaphoreType.DMA((8 * slots,)),
        ],
        compiler_params=pltpu.CompilerParams(vmem_limit_bytes=28 * 1024 * 1024),
        cost_estimate=pl.CostEstimate(
            flops=slots * 4 * rows * depth * cols + more_flops,
            bytes_accessed=slots * 4 * depth * (rows + cols),
            transcendentals=0,
        ),
        name=name,
    )(*args)


def per_device(
    teacher_states,
    teacher_wq,
    teacher_wk,
    teacher_wv,
    student_states,
    student_wq,
    student_wk,
    student_wv,
    lengths,
):
    d = lax.axis_index("dp")
    head = lax.axis_index("head")
    x = lax.axis_index("mp")
    z, yl = d // 2, d % 2
    rows = student_states.shape[0]
    depth = teacher_wq.shape[0]
    q_width = teacher_wq.shape[1] // 4

    depth = teacher_wq.shape[0]
    part_y = teacher_wq[:, q_width:]
    z0 = jnp.concatenate(
        [jnp.concatenate([teacher_wk, teacher_wv], axis=1), teacher_wq[:, :q_width]], axis=0
    )
    y_cols = part_y.shape[1]
    cat, fence = jnp.concatenate, lax.optimization_barrier

    sq, sk = student_wq.shape[1], student_wk.shape[1]
    q_head, width = sq // 4, student_states.shape[1]
    length = lengths[0]

    other_y = swap_dp(part_y, 1)
    z1a, z1b = shift_z(z0, 1), shift_z(z0, -1)
    pair = cat([teacher_states, swap_head(teacher_states, 2)], 1)
    other_y, z1a, z1b, student_wq, student_wk, student_wv = fence(
        (other_y, z1a, z1b, student_wq, student_wk, student_wv)
    )
    pair_y = jnp.where(yl == 0, cat([part_y, other_y], 0), cat([other_y, part_y], 0))
    m1a = shift_z(cat([pair_y, z1a], 1), 1)
    m1b = shift_z(cat([pair_y, z1b], 1), -1)
    c1 = swap_dp(cat([z1a, z1b], 0), 1)
    left, right = shift_x(pair, 1), shift_x(pair, -1)
    student_w = cat([student_wq, student_wk, student_wv], 1)
    wide_w = jnp.pad(student_w, ((0, 128), (0, 96)))
    wide_w = wide_w.at[width, sq + 2 * sk].set(1.0)
    padded = [student_wq[:, i * q_head : (i + 1) * q_head] for i in (1, 2, 3, 0)]
    padded.insert(3, cat([student_wk, student_wv], 1))
    padded = cat([jnp.pad(part, ((0, 0), (0, 128 - part.shape[1]))) for part in padded], 1)
    m1a, m1b, c1, wide_w, padded, student_states = fence(
        (m1a, m1b, c1, wide_w, padded, student_states)
    )
    m2a, m2b = shift_z(m1a, 1), shift_z(m1b, -1)
    c2 = swap_dp(cat([m1a[:, y_cols:], m1b[:, y_cols:], z0], 0), 1)
    part = rows // 2
    far = cat([shift_x(left[:part], 1), shift_x(right[part:], -1)], 0)
    unit = width // 16
    columns = []
    for e in range(4):
        blocks = []
        for r in range(4):
            owner = ((d ^ e) + 4 * r) % 16
            blocks.append(lax.dynamic_slice(student_states, (0, owner * unit), (rows, unit)))
        columns.append(cat(blocks, 1))
    student = dot(student_states, padded).astype(BF)
    m2a, m2b, c2, far, student, *columns = fence((m2a, m2b, c2, far, student, *columns))
    mine = cat([pair, left, right, far], 1)
    other = swap_head(mine, 1)
    m3a, m3b = shift_z(m2a, 1), shift_z(m2b, -1)
    c3 = swap_dp(cat([m2a[:, y_cols:], m2b[:, y_cols:]], 0), 1)
    coord = jnp.stack([z, yl, head, x, length]).astype(jnp.int32)
    cols = y_cols + 2 * q_width
    acc_shape = jax.ShapeDtypeStruct((rows, cols), F32)
    near = call(
        near_kernel, "near",
        (coord, mine, other, pair_y, z0, z1a, z1b, m1a, m1b, m2a, m2b, c1, c2),
        [SCALARS] + [ANY] * 12, acc_shape, 5, rows, depth, cols,
    )
    m3a, m3b, c3, near, student = fence((m3a, m3b, c3, near, student))
    f0 = shift_z(m3a[:depth, :y_cols], 1)
    f1 = shift_z(m3b[depth:, :y_cols], -1)
    c4 = swap_dp(m3a[:, y_cols:], 1)
    acc = call(
        far_kernel, "far", (coord, near, mine, other, m2a, m2b, m3a, m3b, c3),
        [SCALARS, WHOLE] + [ANY] * 7, acc_shape, 2, rows, depth, cols,
    )

    select = np.zeros((cols, 384), np.float32)
    for i, block in enumerate((4, 0, 1, 2)):
        for j in range(q_head):
            select[block * 128 + j, i * q_head + j] = 1.0
    for j in range(2 * sk):
        select[3 * 128 + j, sq + j] = 1.0
    widths = ((q_width, teacher_wk.shape[1] // 4), (q_head, sk // 4))
    out = jax.ShapeDtypeStruct((rows, 384), BF)
    with_loss, ordered = call(
        functools.partial(finish_kernel, widths), "finish",
        (coord, acc, student, jnp.asarray(select, BF), mine, other, m3a, f0, f1, c4),
        [SCALARS, WHOLE, WHOLE, WHOLE] + [ANY] * 6, (out, out), 1, rows, depth, cols,
        scratch=(
            pltpu.VMEM((rows, cols), BF),
            pltpu.VMEM((rows, cols), BF),
            pltpu.VMEM((rows, cols), F32),
            pltpu.VMEM((rows, rows), BF),
            pltpu.VMEM((5, 128, rows), F32),
        ),
        more_flops=12 * 8 * rows * rows * 128,
    )
    grads = with_loss[:, : sq + 2 * sk]
    half = rows // 2

    piece = rows // 16

    def state_term(part):
        return lax.dot_general(
            part, wide_w, (((1,), (1,)), ((), ())), preferred_element_type=F32
        ).astype(BF)

    def weight_term(e, grads):
        return lax.dot_general(
            grads, columns[e], (((0,), (0,)), ((), ())), preferred_element_type=F32
        )

    terms = [weight_term(e, grads).astype(BF) for e in (3, 2, 1)]
    *terms, ordered = fence((*terms, ordered))
    received = [swap_dp(term, e) for term, e in zip(terms, (3, 2, 1))]
    from_core = swap_head(state_term(ordered[half:]), 1)
    summed = (state_term(ordered[:half]).astype(F32) + from_core.astype(F32)).astype(BF)
    summed, grads = fence((summed, grads))
    slab = half // 4
    sent = [shift_x(summed[step * slab : (step + 1) * slab], step) for step in (2, 1, 3)]
    first_square = weight_term(0, grads)
    *received, first_square = fence((*received, *sent, first_square))
    received, sent = received[:3], received[3:]
    square = first_square
    for part in received:
        square = square + part.astype(F32)
    chunks = [square[:, r * unit : (r + 1) * unit] for r in range(4)]
    total = summed[:slab].astype(F32)
    for part in sent:
        total = total + part.astype(F32)
    last = swap_head(total[piece:].astype(BF), 2)
    weight_grad = chunks[0]
    for r in (2, 1, 3):
        moved = lax.ppermute(
            chunks[r].astype(BF), "dp", [(i, (i + 4 * r) % 16) for i in range(16)]
        )
        weight_grad = weight_grad + moved.astype(F32)
    weight_grad = weight_grad.T
    total = total[:piece] + last.astype(F32)
    grad_states = total[:, :width]
    seq_loss = total[0, width : width + 1]

    return (
        weight_grad[:, :sq],
        weight_grad[:, sq : sq + sk],
        weight_grad[:, sq + sk :],
        grad_states,
        seq_loss,
    )


def solution(mesh):
    in_specs = (
        P("dp", ("head", "mp")),
        P("dp", ("head", "mp")),
        P("dp", ("head", "mp")),
        P("dp", ("head", "mp")),
        P("dp", None),
        P(None, ("head", "mp")),
        P(None, ("head", "mp")),
        P(None, ("head", "mp")),
        P("dp"),
    )
    out_specs = (
        P("dp", ("head", "mp")),
        P("dp", ("head", "mp")),
        P("dp", ("head", "mp")),
        P(("dp", "head", "mp"), None),
        P("dp"),
    )
    return jax.shard_map(
        per_device, mesh=mesh, in_specs=in_specs, out_specs=out_specs, check_vma=False
    )
```

```python
import functools
import math

import jax
import jax.numpy as jnp
import numpy as np
from jax import lax
from jax.experimental import pallas as pl
from jax.experimental.pallas import tpu as pltpu
from jax.sharding import PartitionSpec as P

R = 64

LOSS_SCALE = 16.0
MASK_VALUE = -1000000000.0

BF = jnp.bfloat16
F32 = jnp.float32


def shift_z(a, step):
    return lax.ppermute(a, "dp", [(d, (d + 2 * step) % 16) for d in range(16)])


def swap_dp(a, bits):
    return lax.ppermute(a, "dp", [(d, d ^ bits) for d in range(16)])


def swap_head(a, bits):
    return lax.ppermute(a, "head", [(h, h ^ bits) for h in range(4)])


def shift_x(a, step):
    return lax.ppermute(a, "mp", [(m, (m + step) % 4) for m in range(4)])


def dot(a, b):
    return jnp.dot(a, b, preferred_element_type=F32)


OFFSETS = (0, -1, 1, -2, 2, -3, 3, 4)


class Loader:
    def __init__(self, coord, states, a_v, w_v, sems):
        self.z, self.yl, self.head, self.x = coord[0], coord[1], coord[2], coord[3]
        self.states, self.a_v, self.w_v, self.sems = states, a_v, w_v, sems
        self.count = 0
        self.slots = []

    def copy(self, src, dst):
        made = pltpu.make_async_copy(src, dst, self.sems.at[self.count])
        self.count += 1
        made.start()
        return made

    def copy_state(self, owner, dst):
        far = (owner - self.x) & 3
        place = jnp.where(far == 3, 1, jnp.where(far == 0, 0, far + 1))
        yh_bit = (owner >> 3) ^ (self.head >> 1)
        first = pl.multiple_of((place * 2 + yh_bit) * dst.shape[1], 128)
        other_core = ((owner >> 2) & 1) ^ (self.head & 1)
        sem = self.sems.at[self.count]
        self.count += 1
        made = [
            pltpu.make_async_copy(ref.at[:, pl.ds(first, dst.shape[1])], dst, sem)
            for ref in self.states
        ]
        pl.when(other_core == 0)(made[0].start)
        pl.when(other_core == 1)(made[1].start)
        return made[0]

    def load(self, offset, y_parts, own, crossed):
        slot, w_v = len(self.slots), self.w_v
        depth, z_cols = w_v.shape[2], w_v.shape[3] // 5
        y_cols = 3 * z_cols
        owner = (self.z + offset + 8) & 7
        made = [
            self.copy_state(2 * owner + side, self.a_v.at[slot, :, pl.ds(side * depth, depth)])
            for side in (0, 1)
        ]
        for side, (ref, row) in enumerate(y_parts):
            src = ref.at[pl.ds(row, depth), pl.ds(0, y_cols)]
            made.append(self.copy(src, w_v.at[slot, side, :, pl.ds(0, y_cols)]))
        for fold in (0, 1):
            cols = pl.ds(y_cols + fold * z_cols, z_cols)
            for (ref, row, col), side in ((own, self.yl), (crossed, 1 - self.yl)):
                src = ref.at[pl.ds(row + fold * depth, depth), pl.ds(col, z_cols)]
                made.append(self.copy(src, w_v.at[slot, side, :, cols]))
        self.slots.append(made)

    def term(self, slot):
        for made in self.slots[slot]:
            made.wait()
        a, w = self.a_v[slot], self.w_v[slot]
        return dot(a, w.reshape(w.shape[0] * w.shape[1], w.shape[2]))


def near_kernel(
    coord, mine, other, pair_y, z0, z1a, z1b, m1a, m1b, m2a, m2b, c1, c2, acc, a_v, w_v, sems
):
    depth, y_cols = w_v.shape[2], pair_y.shape[1]
    loader = Loader(coord, (mine, other), a_v, w_v, sems)
    pieces = (
        (pair_y, (z0, 0, 0), (c2, 4)),
        (m1a, (z1a, 0, 0), (c1, 0)),
        (m1b, (z1b, 0, 0), (c1, 2)),
        (m2a, (m1a, 0, y_cols), (c2, 0)),
        (m2b, (m1b, 0, y_cols), (c2, 2)),
    )
    for offset, (y_ref, own, (crossed, place)) in zip(OFFSETS, pieces):
        loader.load(
            offset, ((y_ref, 0), (y_ref, depth)), own, (crossed, place * depth, 0)
        )
    acc[...] = loader.term(0)
    for slot in range(1, 5):
        acc[...] += loader.term(slot)


def far_kernel(coord, before, mine, other, m2a, m2b, m3a, m3b, c3, acc, a_v, w_v, sems):
    depth, y_cols = w_v.shape[2], w_v.shape[3] // 5 * 3
    loader = Loader(coord, (mine, other), a_v, w_v, sems)
    loader.load(-3, ((m3a, 0), (m3a, depth)), (m2a, 0, y_cols), (c3, 0, 0))
    loader.load(3, ((m3b, 0), (m3b, depth)), (m2b, 0, y_cols), (c3, 2 * depth, 0))
    acc[...] = before[...] + loader.term(0)
    acc[...] += loader.term(1)


BLOCK = 384


HEADS = 12
NT = (((1,), (1,)), ((), ()))
TN = (((0,), (0,)), ((), ()))


def place_of(i, of_query, of_other):
    query = i < 4
    block = jnp.where(query, i + i // 3, 3)
    first = jnp.where(query, 0, (i - 4) * of_other)
    return block, first, jnp.where(query, 128, of_other), query


def only(cols, first, width):
    lane = lax.broadcasted_iota(jnp.int32, cols.shape, 1)
    mine = (lane >= first) & (lane < first + width)
    return jnp.where(mine, cols.astype(F32), 0.0).astype(BF)


def scale_of(query, widths):
    scales = [1.0 / (math.sqrt(w) * math.log(2.0)) for w in widths]
    return jnp.where(query, scales[0], scales[1])


def finish_kernel(
    widths, coord, before, student_ref, select_ref, mine_a, other_a, m3a, f0, f1, c4,
    grads_out, ordered_out, a_v, w_v, t_v, g_v, o_v, sg_v, turned_v, sems,
):
    depth, y_cols = f0.shape
    t_widths, s_widths = widths
    head, x, length = coord[2], coord[3], coord[4]
    rows = t_v.shape[0]
    loader = Loader(coord, (mine_a, other_a), a_v, w_v, sems)
    loader.load(4, ((f0, 0), (f1, 0)), (m3a, 0, y_cols), (c4, 0, 0))

    t_v[...] = (before[...] + loader.term(0)).astype(BF)
    valid_keys = lax.broadcasted_iota(jnp.int32, (1, rows), 1) < length
    o_v[...] = jnp.zeros_like(o_v)
    turned_v[...] = jnp.zeros_like(turned_v)

    def one_head(i, kl):
        block, t_first, t_width, query = place_of(i, *t_widths)
        _, s_first, s_width, _ = place_of(i, *s_widths)
        scale, s_scale = scale_of(query, t_widths), scale_of(query, s_widths)
        lanes = pl.ds(pl.multiple_of(block * 128, 128), 128)
        teacher = t_v[:, lanes]
        mine = only(teacher, t_first, t_width)
        student = student_ref[:, lanes]
        s_mine = only(student, s_first, s_width)
        for start in range(0, rows, BLOCK):
            part = slice(start, start + BLOCK)
            scores = lax.dot_general(mine[part], teacher, NT, preferred_element_type=F32)
            scores = jnp.where(valid_keys, scores * scale, MASK_VALUE)
            top = jnp.max(scores, axis=-1, keepdims=True)
            weight = jnp.exp2(scores - top)
            total = jnp.sum(weight, axis=-1, keepdims=True)
            other = lax.dot_general(s_mine[part], student, NT, preferred_element_type=F32)
            other = jnp.where(valid_keys, other * s_scale, MASK_VALUE)
            s_top = jnp.max(other, axis=-1, keepdims=True)
            s_weight = jnp.exp2(other - s_top)
            s_total = jnp.sum(s_weight, axis=-1, keepdims=True)
            cross = jnp.sum(weight * (scores - other), axis=-1, keepdims=True)
            row_kl = cross / total - (top + jnp.log2(total)) + (s_top + jnp.log2(s_total))
            valid = lax.broadcasted_iota(jnp.int32, (BLOCK, 1), 0) + start < length
            kl = kl + jnp.sum(jnp.where(valid, row_kl, 0.0), axis=0, keepdims=True)
            gain = jnp.where(valid, LOSS_SCALE / total, 0.0)
            s_gain = jnp.where(valid, LOSS_SCALE / s_total, 0.0)
            sg_v[part, :] = (s_weight * s_gain - weight * gain).astype(BF)
        sg = sg_v[...]
        o_v[:, lanes] += dot(sg, s_mine)
        turned_v[block] += lax.dot_general(s_mine, sg, TN, preferred_element_type=F32)
        return kl

    kl = lax.fori_loop(0, HEADS, one_head, jnp.zeros((1, 1), F32))
    over = [1.0 / math.sqrt(w) for w in s_widths]
    for block in range(5):
        lanes = slice(block * 128, block * 128 + 128)
        both = o_v[:, lanes] + turned_v[block].T
        g_v[:, lanes] = (both * over[block == 3]).astype(BF)
    loss = kl * math.log(2.0) / (3.0 * R * length.astype(F32))
    packed = dot(g_v[...], select_ref[...])
    lane = lax.broadcasted_iota(jnp.int32, packed.shape, 1)
    packed = jnp.where(lane == s_widths[0] * 4 + s_widths[1] * 8, loss, packed)
    o_v[:, pl.ds(0, packed.shape[1])] = packed
    grads_out[...] = packed.astype(BF)
    piece = rows // 16
    for place in range(8):
        core_bit, x_step = place // 4, place % 4
        halves = []
        for yh_bit in (0, 1):
            owner = (head ^ (2 * yh_bit + core_bit)) * 4 + ((x + x_step) & 3)
            own_rows = pl.ds(pl.multiple_of(owner * piece, 8), piece)
            halves.append(o_v[own_rows, pl.ds(0, packed.shape[1])])
        ordered_out[pl.ds(place * 2 * piece, 2 * piece), :] = jnp.concatenate(halves, 0).astype(BF)


ANY = pl.BlockSpec(memory_space=pl.ANY)
WHOLE = pl.BlockSpec(memory_space=pltpu.VMEM)
SCALARS = pl.BlockSpec(memory_space=pltpu.SMEM)


def call(kernel, name, args, specs, outs, slots, rows, depth, cols, scratch=(), more_flops=0):
    return pl.pallas_call(
        kernel,
        out_shape=outs,
        in_specs=specs,
        out_specs=jax.tree.map(lambda _: WHOLE, outs),
        scratch_shapes=[
            pltpu.VMEM((slots, rows, 2 * depth), BF),
            pltpu.VMEM((slots, 2, depth, cols), BF),
            *scratch,
            pltpu.SemaphoreType.DMA((8 * slots,)),
        ],
        compiler_params=pltpu.CompilerParams(vmem_limit_bytes=28 * 1024 * 1024),
        cost_estimate=pl.CostEstimate(
            flops=slots * 4 * rows * depth * cols + more_flops,
            bytes_accessed=slots * 4 * depth * (rows + cols),
            transcendentals=0,
        ),
        name=name,
    )(*args)


def per_device(
    teacher_states,
    teacher_wq,
    teacher_wk,
    teacher_wv,
    student_states,
    student_wq,
    student_wk,
    student_wv,
    lengths,
):
    d = lax.axis_index("dp")
    head = lax.axis_index("head")
    x = lax.axis_index("mp")
    z, yl = d // 2, d % 2
    rows = student_states.shape[0]
    depth = teacher_wq.shape[0]
    q_width = teacher_wq.shape[1] // 4

    depth = teacher_wq.shape[0]
    part_y = teacher_wq[:, q_width:]
    z0 = jnp.concatenate(
        [jnp.concatenate([teacher_wk, teacher_wv], axis=1), teacher_wq[:, :q_width]], axis=0
    )
    y_cols = part_y.shape[1]
    cat, fence = jnp.concatenate, lax.optimization_barrier

    sq, sk = student_wq.shape[1], student_wk.shape[1]
    q_head, width = sq // 4, student_states.shape[1]
    length = lengths[0]

    other_y = swap_dp(part_y, 1)
    z1a, z1b = shift_z(z0, 1), shift_z(z0, -1)
    pair = cat([teacher_states, swap_head(teacher_states, 2)], 1)
    other_y, z1a, z1b, student_wq, student_wk, student_wv = fence(
        (other_y, z1a, z1b, student_wq, student_wk, student_wv)
    )
    pair_y = jnp.where(yl == 0, cat([part_y, other_y], 0), cat([other_y, part_y], 0))
    m1a = shift_z(cat([pair_y, z1a], 1), 1)
    m1b = shift_z(cat([pair_y, z1b], 1), -1)
    c1 = swap_dp(cat([z1a, z1b], 0), 1)
    left, right = shift_x(pair, 1), shift_x(pair, -1)
    student_w = cat([student_wq, student_wk, student_wv], 1)
    wide_w = jnp.pad(student_w, ((0, 128), (0, 96)))
    wide_w = wide_w.at[width, sq + 2 * sk].set(1.0)
    padded = [student_wq[:, i * q_head : (i + 1) * q_head] for i in (1, 2, 3, 0)]
    padded.insert(3, cat([student_wk, student_wv], 1))
    padded = cat([jnp.pad(part, ((0, 0), (0, 128 - part.shape[1]))) for part in padded], 1)
    m1a, m1b, c1, wide_w, padded, student_states = fence(
        (m1a, m1b, c1, wide_w, padded, student_states)
    )
    m2a, m2b = shift_z(m1a, 1), shift_z(m1b, -1)
    c2 = swap_dp(cat([m1a[:, y_cols:], m1b[:, y_cols:], z0], 0), 1)
    part = rows // 2
    far = cat([shift_x(left[:part], 1), shift_x(right[part:], -1)], 0)
    unit = width // 16
    columns = []
    for e in range(4):
        blocks = []
        for r in range(4):
            owner = ((d ^ e) + 4 * r) % 16
            blocks.append(lax.dynamic_slice(student_states, (0, owner * unit), (rows, unit)))
        columns.append(cat(blocks, 1))
    student = dot(student_states, padded).astype(BF)
    mine = cat([pair, left, right, far], 1)
    other = swap_head(mine, 1)
    m2a, m2b, c2, other, student, *columns = fence((m2a, m2b, c2, other, student, *columns))
    m3a, m3b = shift_z(m2a, 1), shift_z(m2b, -1)
    c3 = swap_dp(cat([m2a[:, y_cols:], m2b[:, y_cols:]], 0), 1)
    coord = jnp.stack([z, yl, head, x, length]).astype(jnp.int32)
    cols = y_cols + 2 * q_width
    acc_shape = jax.ShapeDtypeStruct((rows, cols), F32)
    near = call(
        near_kernel, "near",
        (coord, mine, other, pair_y, z0, z1a, z1b, m1a, m1b, m2a, m2b, c1, c2),
        [SCALARS] + [ANY] * 12, acc_shape, 5, rows, depth, cols,
    )
    m3a, m3b, c3, near, student = fence((m3a, m3b, c3, near, student))
    f0 = shift_z(m3a[:depth, :y_cols], 1)
    f1 = shift_z(m3b[depth:, :y_cols], -1)
    c4 = swap_dp(m3a[:, y_cols:], 1)
    acc = call(
        far_kernel, "far", (coord, near, mine, other, m2a, m2b, m3a, m3b, c3),
        [SCALARS, WHOLE] + [ANY] * 7, acc_shape, 2, rows, depth, cols,
    )

    select = np.zeros((cols, 384), np.float32)
    for i, block in enumerate((4, 0, 1, 2)):
        for j in range(q_head):
            select[block * 128 + j, i * q_head + j] = 1.0
    for j in range(2 * sk):
        select[3 * 128 + j, sq + j] = 1.0
    widths = ((q_width, teacher_wk.shape[1] // 4), (q_head, sk // 4))
    out = jax.ShapeDtypeStruct((rows, 384), BF)
    with_loss, ordered = call(
        functools.partial(finish_kernel, widths), "finish",
        (coord, acc, student, jnp.asarray(select, BF), mine, other, m3a, f0, f1, c4),
        [SCALARS, WHOLE, WHOLE, WHOLE] + [ANY] * 6, (out, out), 1, rows, depth, cols,
        scratch=(
            pltpu.VMEM((rows, cols), BF),
            pltpu.VMEM((rows, cols), BF),
            pltpu.VMEM((rows, cols), F32),
            pltpu.VMEM((rows, rows), BF),
            pltpu.VMEM((5, 128, rows), F32),
        ),
        more_flops=12 * 8 * rows * rows * 128,
    )
    grads = with_loss[:, : sq + 2 * sk]
    half = rows // 2

    piece = rows // 16

    def state_term(part):
        return lax.dot_general(
            part, wide_w, (((1,), (1,)), ((), ())), preferred_element_type=F32
        ).astype(BF)

    def weight_term(e, grads):
        return lax.dot_general(
            grads, columns[e], (((0,), (0,)), ((), ())), preferred_element_type=F32
        )

    terms = [weight_term(e, grads).astype(BF) for e in (3, 2, 1)]
    *terms, ordered = fence((*terms, ordered))
    received = [swap_dp(term, e) for term, e in zip(terms, (3, 2, 1))]
    from_core = swap_head(state_term(ordered[half:]), 1)
    summed = (state_term(ordered[:half]).astype(F32) + from_core.astype(F32)).astype(BF)
    summed, grads = fence((summed, grads))
    slab = half // 4
    sent = [shift_x(summed[step * slab : (step + 1) * slab], step) for step in (2, 1, 3)]
    first_square = weight_term(0, grads)
    *received, first_square = fence((*received, *sent, first_square))
    received, sent = received[:3], received[3:]
    square = first_square
    for part in received:
        square = square + part.astype(F32)
    chunks = [square[:, r * unit : (r + 1) * unit] for r in range(4)]
    total = summed[:slab].astype(F32)
    for part in sent:
        total = total + part.astype(F32)
    last = swap_head(total[piece:].astype(BF), 2)
    weight_grad = chunks[0]
    for r in (2, 1, 3):
        moved = lax.ppermute(
            chunks[r].astype(BF), "dp", [(i, (i + 4 * r) % 16) for i in range(16)]
        )
        weight_grad = weight_grad + moved.astype(F32)
    weight_grad = weight_grad.T
    total = total[:piece] + last.astype(F32)
    grad_states = total[:, :width]
    seq_loss = total[0, width : width + 1]

    return (
        weight_grad[:, :sq],
        weight_grad[:, sq : sq + sk],
        weight_grad[:, sq + sk :],
        grad_states,
        seq_loss,
    )


def solution(mesh):
    in_specs = (
        P("dp", ("head", "mp")),
        P("dp", ("head", "mp")),
        P("dp", ("head", "mp")),
        P("dp", ("head", "mp")),
        P("dp", None),
        P(None, ("head", "mp")),
        P(None, ("head", "mp")),
        P(None, ("head", "mp")),
        P("dp"),
    )
    out_specs = (
        P("dp", ("head", "mp")),
        P("dp", ("head", "mp")),
        P("dp", ("head", "mp")),
        P(("dp", "head", "mp"), None),
        P("dp"),
    )
    return jax.shard_map(
        per_device, mesh=mesh, in_specs=in_specs, out_specs=out_specs, check_vma=False
    )
```
